32 devices in a mesh: gx: 8 (over z, x), af: 4 (over y, core).
Axes of the slice: x: 2, y: 2, z: 4, core: 2. Of those that a mesh axis runs over, the one named last changes fastest.
Arguments:
- scalar_field: float32 [16, 512, 512], P('gx', 'af'), may hold values from -256 to 256
- plane_sketch: float32 [16, 2, 256], P('gx'), may hold values from -1.5 to 1.5
- second_sketch: float32 [512, 256], P('af'), may hold values from -0.25 to 0.25
- third_sketch: float32 [512, 256], replicated, may hold values from -0.25 to 0.25
- mixing: float32 [2, 256, 128], replicated, may hold values from -0.375 to 0.375
- plane_targets: int32 [16, 2], replicated, may hold values from 0 to 7
- plane_signs: int32 [16, 2], replicated, may hold values from 0 to 1
Outputs:
- factor_second: float32 [512, 128], P(('af', 'gx'))
- factor_third: float32 [512, 128], P(('gx', 'af'))
- core_sketch: float32 [128, 128, 128], P('gx', 'af')
The draws below stay inside these ranges and needn't reach their ends.
Inputs may be any that keep to these rules, and one draw needn't show every extreme that they name: `plane_targets`: block id of each of a plane's two entries in the core sketch; the two may coincide. `plane_signs`: 1 stands for a plus sign, 0 for a minus sign.
All inputs are finite; a program needn't handle non-finite values.
Results may differ from the reference program's by a relative error of at most 0.0003.
Values sent between devices are 32-bit elements; how exact they have to be, the bound alone decides.
No kernel may reach another device: no remote copies, remote signals or barrier semaphores. Data moves between devices by JAX's collectives and lax.ppermute only.
A program may use at most 64 MiB of HBM per device.

```python
import jax
import jax.numpy as jnp
from jax import lax

NY = 512
NZ = 512
SKETCH = 256
RANK = 128
BLOCK = 16
BLOCKS = 8
NX = 16


def draw_scalar_field(key, part):
    keys = jax.random.split(jax.random.fold_in(key, 17), 4)
    pos_y = jnp.arange(NY, dtype=jnp.float32) / (NY - 1) - 0.5
    pos_z = jnp.arange(NZ, dtype=jnp.float32) / (NZ - 1) - 0.5
    scale_y = jnp.exp(jax.random.uniform(keys[0], (NY,), jnp.float32, -1.15, 1.15) + 1.0986 * pos_y)
    scale_z = jnp.exp(jax.random.uniform(keys[1], (NZ,), jnp.float32, -1.15, 1.15) - 1.0986 * pos_z)
    scale_x = jnp.exp(jax.random.uniform(keys[2], (NX,), jnp.float32, -0.69, 0.69))
    noise = jax.random.truncated_normal(keys[3], -4.0, 4.0, (NX, NY, NZ), jnp.float32)
    return noise * scale_x[:, None, None] * scale_y[None, :, None] * scale_z[None, None, :]


def with_ends(entries, key, smallest, largest):
    index_at = [jax.random.randint(jax.random.fold_in(key, axis), (), 0, length) for axis, length in enumerate(entries.shape)]
    main_axis = entries.shape.index(max(entries.shape))
    beside = index_at[:main_axis] + [(index_at[main_axis] + 1) % entries.shape[main_axis]] + index_at[main_axis + 1:]
    return entries.at[tuple(index_at)].set(smallest).at[tuple(beside)].set(largest)


def steps_of(stream_key, extent, cuts, low, high):
    level = 1.0
    for position, blocks in cuts:
        steps = jax.random.uniform(jax.random.fold_in(jax.random.fold_in(stream_key, 6), position), (blocks,), jnp.float32, low / len(cuts), high / len(cuts))
        level = level * jnp.repeat(jnp.exp(steps), extent[position] // blocks).reshape((-1,) + (1,) * (len(extent) - 1 - position))
    return level


def centred(key, extent, scale, most, pieces=(), kind=jnp.bfloat16):
    result = scale * jax.random.normal(key, extent, jnp.float32)
    if pieces:
        result = result * steps_of(key, extent, pieces, -0.22, 0.18)
    return jnp.clip(result, -most, most).astype(kind)


def setup_inputs(seed: int = 0) -> dict:
    streams_of = jax.random.split(jax.random.key(seed), 8)
    return {
        "scalar_field": draw_scalar_field(jax.random.fold_in(streams_of[7], 71), 0),
        "plane_sketch": centred(streams_of[1], (NX, 2, SKETCH), NX ** -0.5, 1.5, ((0, 8),), jnp.float32),
        "second_sketch": centred(streams_of[2], (NY, SKETCH), NY ** -0.5, 0.25, ((0, 4),), jnp.float32),
        "third_sketch": centred(streams_of[3], (NZ, SKETCH), NZ ** -0.5, 0.25, (), jnp.float32),
        "mixing": centred(streams_of[4], (2, SKETCH, RANK), SKETCH ** -0.5, 0.375, (), jnp.float32),
        "plane_targets": with_ends(jax.random.randint(streams_of[5], (NX, 2), 0, BLOCKS), jax.random.fold_in(streams_of[5], 1), 0, BLOCKS - 1).astype(jnp.int32),
        "plane_signs": with_ends(jax.random.randint(streams_of[6], (NX, 2), 0, 2), jax.random.fold_in(streams_of[6], 1), 0, 1).astype(jnp.int32),
    }


precise = lax.Precision.HIGHEST

def orthonormal(ranged):
    gram_matrix = jnp.dot(ranged.T, ranged, precision=precise)
    lower_factor = jnp.linalg.cholesky(gram_matrix)
    return jax.scipy.linalg.solve_triangular(lower_factor, ranged.T, lower=True).T

def reference(scalar_field, plane_sketch, second_sketch, third_sketch, mixing, plane_targets, plane_signs):

    def accumulate(totals, element):
        one_plane, plane_weights = element
        along_rows = jnp.dot(one_plane, third_sketch, precision=precise) * plane_weights[0][None, :]
        across = jnp.dot(one_plane.T, second_sketch, precision=precise) * plane_weights[1][None, :]
        return ((totals[0] + along_rows, totals[1] + across), None)
    initial = (jnp.zeros((NY, SKETCH), jnp.float32), jnp.zeros((NZ, SKETCH), jnp.float32))
    (second_mode, third_mode), unused = lax.scan(accumulate, initial, (scalar_field, plane_sketch))
    second_range = jnp.dot(second_mode, mixing[0], precision=precise)
    third_range = jnp.dot(third_mode, mixing[1], precision=precise)
    factor_second = orthonormal(second_range)
    factor_third = orthonormal(third_range)

    def project(one_plane):
        left_side = jnp.dot(factor_second.T, one_plane, precision=precise)
        return jnp.dot(left_side, factor_third, precision=precise)
    projected = lax.map(project, scalar_field)
    plane_ids = jnp.arange(NX, dtype=jnp.int32)
    targets = plane_targets * BLOCK + (plane_ids % BLOCK)[:, None]
    sign_values = (2 * plane_signs - 1).astype(jnp.float32)
    row_ids = jnp.arange(BLOCKS * BLOCK, dtype=jnp.int32)
    select = jnp.sum(jnp.where(targets[None, :, :] == row_ids[:, None, None], sign_values[None, :, :], 0.0), axis=2)
    core_sketch = jnp.dot(select, projected.reshape(NX, RANK * RANK), precision=precise)
    return (factor_second, factor_third, core_sketch.reshape(BLOCKS * BLOCK, RANK, RANK))
```

```python
import jax
import jax.numpy as jnp
from jax import lax
from jax.sharding import PartitionSpec as P

BLOCK = 16
BLOCKS = 8


precise = lax.Precision.HIGHEST


def gram_of(ranged):
    return jnp.dot(ranged.T, ranged, precision=precise)


def inverse_lower(gram_matrix):
    lower_factor = jnp.linalg.cholesky(gram_matrix)
    eye = jnp.eye(gram_matrix.shape[0], dtype=jnp.float32)
    return jax.scipy.linalg.solve_triangular(lower_factor, eye, lower=True)


def scatter_sum(blocks, axes):
    return jnp.sum(lax.all_to_all(blocks, axes, 0, 0, tiled=True), axis=0)


def gather(block, axes, count):
    return lax.all_to_all(
        jnp.broadcast_to(block[None], (count,) + block.shape), axes, 0, 0, tiled=True
    )


def body(
    scalar_field, plane_sketch, second_sketch, third_sketch, mixing, plane_targets, plane_signs
):
    gx, af = lax.axis_size("gx"), lax.axis_size("af")
    planes, rows, cells = scalar_field.shape
    rank = mixing.shape[2]
    along_second = jnp.einsum("pjl,lk->pjk", scalar_field, third_sketch, precision=precise)
    partial_second = jnp.dot(
        jnp.sum(along_second * plane_sketch[:, 0, None, :], axis=0), mixing[0], precision=precise
    )
    weights = second_sketch[None] * plane_sketch[:, 1, None, :]
    weights = jnp.einsum("pjk,kr->pjr", weights, mixing[1], precision=precise)
    partial_third = jnp.einsum("pjl,pjr->lr", scalar_field, weights, precision=precise)

    own = cells // (gx * af)
    own_third = scatter_sum(partial_third.reshape(gx * af, own, rank), ("gx", "af"))
    own_second = scatter_sum(partial_second.reshape(gx, rows // gx, rank), "gx")
    both = jnp.concatenate([own_second, own_third], axis=0)
    everyone = gather(both, ("gx", "af"), gx * af).reshape(gx, af, 2, own, rank)
    range_second = everyone[:, :, 0].transpose(1, 0, 2, 3).reshape(af * rows, rank)
    range_third = everyone[:, :, 1].reshape(cells, rank)
    inverse_second = inverse_lower(gram_of(range_second))
    inverse_third = inverse_lower(gram_of(range_third))
    factor_second = jnp.dot(own_second, inverse_second.T, precision=precise)
    factor_third = jnp.dot(own_third, inverse_third.T, precision=precise)
    my_second = lax.dynamic_slice_in_dim(range_second, lax.axis_index("af") * rows, rows, 0)
    right = jnp.einsum("pjl,lr->pjr", scalar_field, range_third, precision=precise)
    raw = jnp.einsum("jr,pjs->prs", my_second, right, precision=precise)
    half = jnp.einsum("qr,prs->pqs", inverse_second, raw, precision=precise)
    half = half.reshape(planes, af, rank // af, rank).transpose(1, 0, 2, 3)
    own_planes = scatter_sum(half, "af")
    projected = jnp.einsum("pqs,ts->pqt", own_planes, inverse_third, precision=precise)
    all_planes = gather(projected, "gx", gx).reshape(gx * planes, rank // af, rank)

    out_rows = BLOCKS * BLOCK // gx
    plane_ids = jnp.arange(gx * planes, dtype=jnp.int32)
    all_targets = plane_targets * BLOCK + (plane_ids % BLOCK)[:, None]
    all_signs = (2 * plane_signs - 1).astype(jnp.float32)
    row_ids = lax.axis_index("gx") * out_rows + jnp.arange(out_rows, dtype=jnp.int32)
    select = jnp.sum(
        jnp.where(all_targets[None] == row_ids[:, None, None], all_signs[None], 0.0), axis=2
    )
    core_sketch = jnp.dot(
        select, all_planes.reshape(gx * planes, -1), precision=precise
    ).reshape(out_rows, rank // af, rank)
    return (factor_second, factor_third, core_sketch)


def solution(mesh):
    in_specs = (P("gx", "af", None), P("gx", None, None), P("af", None), P(), P(), P(), P())
    out_specs = (P(("af", "gx"), None), P(("gx", "af"), None), P("gx", "af", None))
    return jax.shard_map(body, mesh=mesh, in_specs=in_specs, out_specs=out_specs, check_vma=False)
```

```python
import functools

import jax
import jax.numpy as jnp
from jax import lax
from jax.experimental import pallas as pl
from jax.experimental.pallas import tpu as pltpu
from jax.sharding import PartitionSpec as P

BLOCK = 16
BLOCKS = 8
SUB = 8

precise = lax.Precision.HIGHEST
VMEM = pl.BlockSpec(memory_space=pltpu.VMEM)
SMEM = pl.BlockSpec(memory_space=pltpu.SMEM)


def dot(left, right, dims):
    return lax.dot_general(
        left, right, (dims, ((), ())), precision=precise, preferred_element_type=jnp.float32
    )


def mm(left, right):
    return dot(left, right, ((1,), (0,)))


def mm_tn(left, right):
    return dot(left, right, ((0,), (0,)))


def mm_nt(left, right):
    return dot(left, right, ((1,), (1,)))


def inverse_lower(gram):
    size = gram.shape[0]
    count = size // SUB
    sub_ids = lax.broadcasted_iota(jnp.int32, (SUB, size), 0)
    lane_ids = lax.broadcasted_iota(jnp.int32, (SUB, size), 1)
    rows = [gram[SUB * i : SUB * i + SUB, :] for i in range(count)]
    ext = [jnp.where(lane_ids == sub_ids + SUB * i, 1.0, 0.0) for i in range(count)]
    done = []

    def along_sub(tile, j):
        return jnp.broadcast_to(tile[j : j + 1, :], (SUB, size))

    for k in range(count):
        cols = {
            i: [
                jnp.broadcast_to(rows[i][:, SUB * k + c : SUB * k + c + 1], (SUB, size))
                for c in range(SUB)
            ]
            for i in range(k, count)
        }
        pivots = jnp.ones((SUB, size), jnp.float32)
        for j in range(SUB):
            pivot = along_sub(cols[k][j], j)
            pivots = jnp.where(sub_ids == j, pivot, pivots)
            scale = 1.0 / pivot
            heads = [along_sub(cols[k][c], j) for c in range(j + 1, SUB)]
            row_head, ext_head = along_sub(rows[k], j), along_sub(ext[k], j)
            for i in range(k, count):
                factor = cols[i][j] * scale
                if i == k:
                    if j == SUB - 1:
                        continue
                    factor = jnp.where(sub_ids > j, factor, 0.0)
                for c in range(j + 1, SUB):
                    cols[i][c] = cols[i][c] - factor * heads[c - j - 1]
                rows[i] = rows[i] - factor * row_head
                ext[i] = ext[i] - factor * ext_head
        root = lax.rsqrt(pivots)
        root = root * (1.5 - 0.5 * (pivots * root) * root)
        done.append(ext[k] * root)
    return jnp.concatenate(done, axis=0)


def sketch_kernel(
    gx, af, place, field, plane_sketch, second_sketch, third_sketch, mixing, out
):
    planes, rows, cells = field.shape
    across, wide = None, None
    for p in range(planes):
        weights = third_sketch[...] * plane_sketch[p, 0:1, :]
        term = mm(field[p], weights)
        across = term if across is None else across + term
        weights = mm(second_sketch[...] * plane_sketch[p, 1:2, :], mixing[1])
        term = mm_tn(field[p], weights)
        wide = term if wide is None else wide + term
    second = mm(across, mixing[0])
    own = rows // gx
    for g in range(gx):
        piece = second[g * own : g * own + own, :]
        for a in range(af):
            d = g * af + a
            out[d, 0:own, :] = jnp.where(place[1] == a, piece, 0.0)
            out[d, own:, :] = wide[d * own : d * own + own, :]


def second_kernel(gx, af, place, ranges, mine, *refs):
    fields, (factor, partial) = refs[:af], refs[af:]
    planes, rows, cells = fields[0].shape
    own = rows // gx
    rank = ranges.shape[2]
    all_second = jnp.concatenate([ranges[d, 0:own, :] for d in range(gx * af)], axis=0)
    all_third = jnp.concatenate([ranges[d, own:, :] for d in range(gx * af)], axis=0)
    raw = [None] * planes
    for mask in range(af):
        group = place[1] ^ mask
        quarter = jnp.concatenate(
            [ranges[g * af + group, 0:own, :] for g in range(gx)], axis=0
        )
        for p in range(planes):
            term = mm_tn(quarter, mm(fields[mask][p], all_third))
            raw[p] = term if raw[p] is None else raw[p] + term
    inverse = inverse_lower(mm_tn(all_second, all_second))
    factor[...] = mm_nt(mine[0:own, :], inverse)
    share = rank // af
    own_rows = inverse[0:share, :]
    for a in range(1, af):
        own_rows = jnp.where(place[1] == a, inverse[a * share : a * share + share, :], own_rows)
    for p in range(planes):
        partial[p] = mm(own_rows, raw[p])


def third_kernel(own, ranges, mine, factor, inverse_out):
    all_third = jnp.concatenate([ranges[d, own:, :] for d in range(ranges.shape[0])], axis=0)
    inverse = inverse_lower(mm_tn(all_third, all_third))
    inverse_out[...] = inverse
    factor[...] = mm_nt(mine[own:, :], inverse)


def core_kernel(place, targets, signs, planes, inverse, out):
    total, share, rank = planes.shape
    out_rows = out.shape[0]
    for r in range(out_rows):
        row = place[0] * out_rows + r
        slot = lax.rem(row, BLOCK)
        block = lax.div(row, BLOCK)
        value = jnp.zeros((share, rank), jnp.float32)
        for m in range(total // BLOCK):
            plane = m * BLOCK + slot
            weight = jnp.float32(0)
            for t in range(targets.shape[1]):
                sign = (2 * signs[plane, t] - 1).astype(jnp.float32)
                weight = weight + jnp.where(targets[plane, t] == block, sign, 0.0)
            value = value + weight * planes[plane]
        out[r] = mm_nt(value, inverse[...])


def call(kernel, out_shapes, in_specs, flops):
    return pl.pallas_call(
        kernel,
        out_shape=out_shapes,
        in_specs=in_specs,
        out_specs=jax.tree.map(lambda _: VMEM, out_shapes),
        compiler_params=pltpu.CompilerParams(vmem_limit_bytes=48 * 1024 * 1024),
        cost_estimate=pl.CostEstimate(flops=flops, bytes_accessed=2**20, transcendentals=0),
    )


def gather_field(field, af):
    held = {0: field}
    bit = af // 2
    while bit:
        perm = [(a, a ^ bit) for a in range(af)]
        for mask in list(held):
            held[mask ^ bit] = lax.ppermute(held[mask], "af", perm)
        bit //= 2
    return [held[mask] for mask in range(af)]


def body(
    scalar_field, plane_sketch, second_sketch, third_sketch, mixing, plane_targets, plane_signs
):
    gx, af = lax.axis_size("gx"), lax.axis_size("af")
    planes, rows, cells = scalar_field.shape
    rank = mixing.shape[2]
    own = rows // gx
    share = rank // af
    place = jnp.stack([lax.axis_index("gx"), lax.axis_index("af")]).astype(jnp.int32)
    f32 = functools.partial(jax.ShapeDtypeStruct, dtype=jnp.float32)

    fields = gather_field(scalar_field, af)
    slots = call(
        functools.partial(sketch_kernel, gx, af),
        f32((gx * af, 2 * own, rank)),
        [SMEM] + [VMEM] * 5,
        2 * 10**9,
    )(place, scalar_field, plane_sketch, second_sketch, third_sketch, mixing)
    mine = jnp.sum(lax.all_to_all(slots, ("gx", "af"), 0, 0, tiled=True), axis=0)
    ranges = lax.all_to_all(
        jnp.broadcast_to(mine[None], slots.shape), ("gx", "af"), 0, 0, tiled=True
    )
    factor_second, partial = call(
        functools.partial(second_kernel, gx, af),
        (f32((own, rank)), f32((planes, share, rank))),
        [SMEM] + [VMEM] * (2 + af),
        2 * 10**9,
    )(place, ranges, mine, *fields)
    every = lax.all_to_all(
        jnp.broadcast_to(partial[None], (gx,) + partial.shape), "gx", 0, 0, tiled=True
    ).reshape(gx * planes, share, rank)
    factor_third, inverse_third = call(
        functools.partial(third_kernel, own),
        (f32((own, rank)), f32((rank, rank))),
        [VMEM] * 2,
        10**9,
    )(ranges, mine)
    core_sketch = call(
        core_kernel,
        f32((BLOCKS * BLOCK // gx, share, rank)),
        [SMEM] * 3 + [VMEM] * 2,
        10**8,
    )(place, plane_targets, plane_signs, every, inverse_third)
    return (factor_second, factor_third, core_sketch)


def solution(mesh):
    in_specs = (P("gx", "af", None), P("gx", None, None), P("af", None), P(), P(), P(), P())
    out_specs = (P(("af", "gx"), None), P(("gx", "af"), None), P("gx", "af", None))
    return jax.shard_map(body, mesh=mesh, in_specs=in_specs, out_specs=out_specs, check_vma=False)
```

```python
import functools

import jax
import jax.numpy as jnp
from jax import lax
from jax.experimental import pallas as pl
from jax.experimental.pallas import tpu as pltpu
from jax.sharding import PartitionSpec as P

BLOCK = 16
BLOCKS = 8
SUB = 8

precise = lax.Precision.HIGHEST
VMEM = pl.BlockSpec(memory_space=pltpu.VMEM)
SMEM = pl.BlockSpec(memory_space=pltpu.SMEM)


def dot(left, right, dims):
    return lax.dot_general(
        left, right, (dims, ((), ())), precision=precise, preferred_element_type=jnp.float32
    )


def mm(left, right):
    return dot(left, right, ((1,), (0,)))


def mm_tn(left, right):
    return dot(left, right, ((0,), (0,)))


def mm_nt(left, right):
    return dot(left, right, ((1,), (1,)))


def inverse_lower(gram):
    size = gram.shape[0]
    count = size // SUB
    sub_ids = lax.broadcasted_iota(jnp.int32, (SUB, size), 0)
    lane_ids = lax.broadcasted_iota(jnp.int32, (SUB, size), 1)
    rows = [gram[SUB * i : SUB * i + SUB, :] for i in range(count)]
    ext = [jnp.where(lane_ids == sub_ids + SUB * i, 1.0, 0.0) for i in range(count)]
    done = []

    def along_sub(tile, j):
        return jnp.broadcast_to(tile[j : j + 1, :], (SUB, size))

    for k in range(count):
        cols = {
            i: [
                jnp.broadcast_to(rows[i][:, SUB * k + c : SUB * k + c + 1], (SUB, size))
                for c in range(SUB)
            ]
            for i in range(k, count)
        }
        pivots = jnp.ones((SUB, size), jnp.float32)
        for j in range(SUB):
            pivot = along_sub(cols[k][j], j)
            pivots = jnp.where(sub_ids == j, pivot, pivots)
            scale = 1.0 / pivot
            heads = [along_sub(cols[k][c], j) for c in range(j + 1, SUB)]
            row_head, ext_head = along_sub(rows[k], j), along_sub(ext[k], j)
            for i in range(k, count):
                factor = cols[i][j] * scale
                if i == k:
                    if j == SUB - 1:
                        continue
                    factor = jnp.where(sub_ids > j, factor, 0.0)
                for c in range(j + 1, SUB):
                    cols[i][c] = cols[i][c] - factor * heads[c - j - 1]
                rows[i] = rows[i] - factor * row_head
                ext[i] = ext[i] - factor * ext_head
        root = lax.rsqrt(pivots)
        root = root * (1.5 - 0.5 * (pivots * root) * root)
        done.append(ext[k] * root)
    return jnp.concatenate(done, axis=0)


def sketch_kernel(
    gx, af, place, field, plane_sketch, second_sketch, third_sketch, mixing, *refs
):
    second_out, third_outs = refs[0], refs[1 : 1 + af]
    held, wide_blocks, arrived = refs[1 + af : 6 + af], refs[6 + af], refs[7 + af]
    sources = (third_sketch, plane_sketch, field, second_sketch, mixing)
    copies = [
        pltpu.make_async_copy(source, target, arrived.at[n])
        for n, (source, target) in enumerate(zip(sources, held))
    ]
    for copy in copies:
        copy.start()
    for copy in copies:
        copy.wait()
    third_sketch, plane_sketch, field, second_sketch, mixing = held
    planes, rows, cells = field.shape
    across, wide = None, None
    for p in range(planes):
        weights = third_sketch[...] * plane_sketch[p, 0:1, :]
        term = mm(field[p], weights)
        across = term if across is None else across + term
        weights = mm(second_sketch[...] * plane_sketch[p, 1:2, :], mixing[1])
        term = mm_tn(field[p], weights)
        wide = term if wide is None else wide + term
    second = mm(across, mixing[0])
    own = rows // gx
    for g in range(gx):
        second_out[g] = second[g * own : g * own + own, :]
        for a in range(af):
            d = g * af + a
            wide_blocks[a, g] = wide[d * own : d * own + own, :]
    for mask in range(af):
        third_outs[mask][...] = wide_blocks[place[1] ^ mask]


def share_kernel(gx, af, place, second, *refs):
    thirds, outs, total = refs[:af], refs[af : af + gx], refs[af + gx]
    value = thirds[0][...]
    for third in thirds[1:]:
        value = value + third[...]
    total[...] = value
    for mask in range(gx):
        outs[mask][0] = second[place[0] ^ mask]
        outs[mask][1] = total[place[0] ^ mask]


def second_kernel(gx, af, place, *refs):
    ranges, fields = refs[:af], refs[af : 2 * af]
    factor, partial, natural = refs[2 * af :]
    planes, rows, cells = fields[0].shape
    own, rank = ranges[0].shape[2:]
    for mask in range(af):
        for g in range(gx):
            natural[0, place[1] ^ mask, place[0] ^ g] = ranges[mask][g, 0]
            natural[1, place[1] ^ mask, place[0] ^ g] = ranges[mask][g, 1]
    quarters = [
        jnp.concatenate([natural[0, place[1] ^ mask, g] for g in range(gx)], axis=0)
        for mask in range(af)
    ]
    all_third = jnp.concatenate(
        [natural[1, a, g] for g in range(gx) for a in range(af)], axis=0
    )
    all_second = jnp.concatenate(
        [natural[0, a, g] for a in range(af) for g in range(gx)], axis=0
    )
    raw = [None] * planes
    for mask in range(af):
        for p in range(planes):
            term = mm_tn(quarters[mask], mm(fields[mask][p], all_third))
            raw[p] = term if raw[p] is None else raw[p] + term
    inverse = inverse_lower(mm_tn(all_second, all_second))
    factor[...] = mm_nt(ranges[0][0, 0], inverse)
    share = rank // af
    own_rows = inverse[0:share, :]
    for a in range(1, af):
        own_rows = jnp.where(place[1] == a, inverse[a * share : a * share + share, :], own_rows)
    for p in range(planes):
        partial[p] = mm(own_rows, raw[p])


def third_kernel(gx, af, place, *refs):
    ranges, (factor, inverse_out, natural) = refs[:af], refs[af:]
    for mask in range(af):
        for g in range(gx):
            natural[place[1] ^ mask, place[0] ^ g] = ranges[mask][g, 1]
    all_third = jnp.concatenate(
        [natural[a, g] for g in range(gx) for a in range(af)], axis=0
    )
    inverse = inverse_lower(mm_tn(all_third, all_third))
    inverse_out[...] = inverse
    factor[...] = mm_nt(ranges[0][0, 1], inverse)


def core_kernel(gx, place, targets, signs, inverse, *refs):
    parts, (out, planes) = refs[:gx], refs[gx:]
    count, share, rank = parts[0].shape
    for mask in range(gx):
        for p in range(count):
            planes[(place[0] ^ mask) * count + p] = parts[mask][p]
    out_rows = out.shape[0]
    values = []
    for r in range(out_rows):
        row = place[0] * out_rows + r
        slot = lax.rem(row, BLOCK)
        block = lax.div(row, BLOCK)
        value = jnp.zeros((share, rank), jnp.float32)
        for m in range(gx * count // BLOCK):
            plane = m * BLOCK + slot
            weight = jnp.float32(0)
            for t in range(targets.shape[1]):
                sign = (2 * signs[plane, t] - 1).astype(jnp.float32)
                weight = weight + jnp.where(targets[plane, t] == block, sign, 0.0)
            value = value + weight * planes[plane]
        values.append(value)
    whole = mm_nt(jnp.concatenate(values, axis=0), inverse[...])
    for r in range(out_rows):
        out[r] = whole[r * share : r * share + share, :]


def call(kernel, out_shapes, in_specs, flops, scratch=()):
    return pl.pallas_call(
        kernel,
        out_shape=out_shapes,
        in_specs=in_specs,
        out_specs=jax.tree.map(lambda _: VMEM, out_shapes),
        scratch_shapes=scratch,
        compiler_params=pltpu.CompilerParams(vmem_limit_bytes=48 * 1024 * 1024),
        cost_estimate=pl.CostEstimate(flops=flops, bytes_accessed=2**20, transcendentals=0),
    )


def swap(block, axis, mask):
    perm = [(n, n ^ mask) for n in range(lax.axis_size(axis))]
    return lax.ppermute(block, axis, perm)


def gather_field(field, af):
    held = {0: field}
    bit = af // 2
    while bit:
        for mask in list(held):
            held[mask ^ bit] = swap(held[mask], "af", bit)
        bit //= 2
    return [held[mask] for mask in range(af)]


def exchange(blocks, axis):
    return list(blocks[:1]) + [swap(block, axis, m + 1) for m, block in enumerate(blocks[1:])]


def body(
    scalar_field, plane_sketch, second_sketch, third_sketch, mixing, plane_targets, plane_signs
):
    gx, af = lax.axis_size("gx"), lax.axis_size("af")
    planes, rows, cells = scalar_field.shape
    rank = mixing.shape[2]
    own = rows // gx
    share = rank // af
    place = jnp.stack([lax.axis_index("gx"), lax.axis_index("af")]).astype(jnp.int32)
    f32 = functools.partial(jax.ShapeDtypeStruct, dtype=jnp.float32)
    quarter = (gx, own, rank)

    sources = (third_sketch, plane_sketch, scalar_field, second_sketch, mixing)
    sketched = call(
        functools.partial(sketch_kernel, gx, af),
        [f32(quarter)] * (1 + af),
        [SMEM] + [pl.BlockSpec(memory_space=pltpu.HBM)] * 5,
        10**9,
        [pltpu.VMEM(source.shape, jnp.float32) for source in sources]
        + [pltpu.VMEM((af,) + quarter, jnp.float32), pltpu.SemaphoreType.DMA((5,))],
    )(place, scalar_field, plane_sketch, second_sketch, third_sketch, mixing)
    fields = gather_field(scalar_field, af)
    shares = call(
        functools.partial(share_kernel, gx, af),
        [f32((2, own, rank))] * gx,
        [SMEM] + [VMEM] * (1 + af),
        10**6,
        [pltpu.VMEM(quarter, jnp.float32)],
    )(place, sketched[0], *exchange(sketched[1:], "af"))
    mine = sum(exchange(shares, "gx"))
    mine_quarter = jnp.stack(exchange([mine] * gx, "gx"))
    ranges = exchange([mine_quarter] * af, "af")
    factor_second, partial = call(
        functools.partial(second_kernel, gx, af),
        [f32((own, rank)), f32((planes, share, rank))],
        [SMEM] + [VMEM] * (2 * af),
        2 * 10**9,
        [pltpu.VMEM((2, af) + quarter, jnp.float32)],
    )(place, *ranges, *fields)
    every = exchange([partial] * gx, "gx")
    factor_third, inverse_third = call(
        functools.partial(third_kernel, gx, af),
        [f32((own, rank)), f32((rank, rank))],
        [SMEM] + [VMEM] * af,
        10**9,
        [pltpu.VMEM((af,) + quarter, jnp.float32)],
    )(place, *ranges)
    core_sketch = call(
        functools.partial(core_kernel, gx),
        f32((BLOCKS * BLOCK // gx, share, rank)),
        [SMEM] * 3 + [VMEM] * (1 + gx),
        10**8,
        [pltpu.VMEM((gx * planes, share, rank), jnp.float32)],
    )(place, plane_targets, plane_signs, inverse_third, *every)
    return (factor_second, factor_third, core_sketch)


def solution(mesh):
    in_specs = (P("gx", "af", None), P("gx", None, None), P("af", None), P(), P(), P(), P())
    out_specs = (P(("af", "gx"), None), P(("gx", "af"), None), P("gx", "af", None))
    return jax.shard_map(body, mesh=mesh, in_specs=in_specs, out_specs=out_specs, check_vma=False)
```

```python
import functools

import jax
import jax.numpy as jnp
from jax import lax
from jax.experimental import pallas as pl
from jax.experimental.pallas import tpu as pltpu
from jax.sharding import PartitionSpec as P

BLOCK = 16
BLOCKS = 8
SUB = 8

precise = lax.Precision.HIGHEST
VMEM = pl.BlockSpec(memory_space=pltpu.VMEM)
SMEM = pl.BlockSpec(memory_space=pltpu.SMEM)


def dot(left, right, dims):
    return lax.dot_general(
        left, right, (dims, ((), ())), precision=precise, preferred_element_type=jnp.float32
    )


def mm(left, right):
    return dot(left, right, ((1,), (0,)))


def mm_tn(left, right):
    return dot(left, right, ((0,), (0,)))


def mm_nt(left, right):
    return dot(left, right, ((1,), (1,)))


def inverse_lower(gram):
    size = gram.shape[0]
    count = size // SUB
    sub_ids = lax.broadcasted_iota(jnp.int32, (SUB, size), 0)
    lane_ids = lax.broadcasted_iota(jnp.int32, (SUB, size), 1)
    rows = [gram[SUB * i : SUB * i + SUB, :] for i in range(count)]
    ext = [jnp.where(lane_ids == sub_ids + SUB * i, 1.0, 0.0) for i in range(count)]
    done = []

    def along_sub(tile, j):
        return jnp.broadcast_to(tile[j : j + 1, :], (SUB, size))

    for k in range(count):
        cols = {
            i: [
                jnp.broadcast_to(rows[i][:, SUB * k + c : SUB * k + c + 1], (SUB, size))
                for c in range(SUB)
            ]
            for i in range(k, count)
        }
        pivots = jnp.ones((SUB, size), jnp.float32)
        for j in range(SUB):
            pivot = along_sub(cols[k][j], j)
            pivots = jnp.where(sub_ids == j, pivot, pivots)
            scale = 1.0 / pivot
            heads = [along_sub(cols[k][c], j) for c in range(j + 1, SUB)]
            row_head, ext_head = along_sub(rows[k], j), along_sub(ext[k], j)
            for i in range(k, count):
                factor = cols[i][j] * scale
                if i == k:
                    if j == SUB - 1:
                        continue
                    factor = jnp.where(sub_ids > j, factor, 0.0)
                for c in range(j + 1, SUB):
                    cols[i][c] = cols[i][c] - factor * heads[c - j - 1]
                rows[i] = rows[i] - factor * row_head
                ext[i] = ext[i] - factor * ext_head
        root = lax.rsqrt(pivots)
        root = root * (1.5 - 0.5 * (pivots * root) * root)
        done.append(ext[k] * root)
    return jnp.concatenate(done, axis=0)


def sketch_kernel(
    gx, ay, ac, place, field, plane_sketch, second_sketch, third_sketch, mixing, *refs
):
    kept, given = refs[:2]
    held, wide_blocks, arrived = refs[2:7], refs[7], refs[8]
    sources = (third_sketch, plane_sketch, field, second_sketch, mixing)
    copies = [
        pltpu.make_async_copy(source, target, arrived.at[n])
        for n, (source, target) in enumerate(zip(sources, held))
    ]
    for copy in copies:
        copy.start()
    for copy in copies:
        copy.wait()
    third_sketch, plane_sketch, field, second_sketch, mixing = held
    planes, rows, cells = field.shape
    across, wide = None, None
    for p in range(planes):
        weights = third_sketch[...] * plane_sketch[p, 0:1, :]
        term = mm(field[p], weights)
        across = term if across is None else across + term
        weights = mm(second_sketch[...] * plane_sketch[p, 1:2, :], mixing[1])
        term = mm_tn(field[p], weights)
        wide = term if wide is None else wide + term
    second = mm(across, mixing[0])
    strip = rows // (gx * ay)
    own = cells // (gx * ay * ac)
    for n in range(gx * ay):
        kept[n, own:, :] = second[n * strip : n * strip + strip, :]
        for c in range(ac):
            d = n * ac + c
            wide_blocks[c, n] = wide[d * own : d * own + own, :]
    kept[:, 0:own, :] = wide_blocks[place[2]]
    given[...] = wide_blocks[1 - place[2]]


def slots_kernel(kept, taken, out):
    own = taken.shape[1]
    out[:, 0:own, :] = kept[:, 0:own, :] + taken[...]
    out[:, own:, :] = kept[:, own:, :]


def total_kernel(gx, ay, own, received, out):
    strip = received.shape[1] - own
    third = received[0, 0:own, :]
    for n in range(1, gx * ay):
        third = third + received[n, 0:own, :]
    seconds = []
    for y in range(ay):
        second = received[y, own:, :]
        for g in range(1, gx):
            second = second + received[g * ay + y, own:, :]
        seconds.append(second)
    for n in range(gx * ay):
        out[n, 0:own, :] = third
        for y in range(ay):
            out[n, own + y * strip : own + (y + 1) * strip, :] = seconds[y]


def second_kernel(gx, ay, ac, place, same, other, *refs):
    fields, (factor, partial, second, third) = refs[: ay * ac], refs[ay * ac :]
    planes, rows, cells = fields[0].shape
    own = cells // (gx * ay * ac)
    strip = rows // (gx * ay)
    rank = same.shape[2]
    for swapped, ranges in enumerate((same, other)):
        core = place[2] ^ swapped
        for n in range(gx * ay):
            third[n, core] = ranges[n, 0:own, :]
            for y in range(ay):
                second[y, core, n] = ranges[n, own + y * strip : own + (y + 1) * strip, :]

    def quarter(y, c):
        return jnp.concatenate([second[y, c, n] for n in range(gx * ay)], axis=0)

    all_third = jnp.concatenate([third[n, c] for n in range(gx * ay) for c in range(ac)], axis=0)
    all_second = jnp.concatenate([quarter(y, c) for y in range(ay) for c in range(ac)], axis=0)
    raw = [None] * planes
    for mask in range(ay * ac):
        left = quarter(place[1] ^ (mask // ac), place[2] ^ (mask % ac))
        for p in range(planes):
            term = mm_tn(left, mm(fields[mask][p], all_third))
            raw[p] = term if raw[p] is None else raw[p] + term
    inverse = inverse_lower(mm_tn(all_second, all_second))
    mine = [second[place[1], place[2], place[0] * ay + y] for y in range(ay)]
    factor[...] = mm_nt(jnp.concatenate(mine, axis=0), inverse)
    share = rank // (ay * ac)
    own_rows = inverse[0:share, :]
    for a in range(1, ay * ac):
        piece = inverse[a * share : a * share + share, :]
        own_rows = jnp.where(place[1] * ac + place[2] == a, piece, own_rows)
    for p in range(planes):
        value = mm(own_rows, raw[p])
        for g in range(gx):
            partial[g, p] = value


def third_kernel(gx, ay, ac, own, place, same, other, factor, inverse_out, third):
    for swapped, ranges in enumerate((same, other)):
        for n in range(gx * ay):
            third[n, place[2] ^ swapped] = ranges[n, 0:own, :]
    all_third = jnp.concatenate([third[n, c] for n in range(gx * ay) for c in range(ac)], axis=0)
    inverse = inverse_lower(mm_tn(all_third, all_third))
    inverse_out[...] = inverse
    factor[...] = mm_nt(third[place[0] * ay + place[1], place[2]], inverse)


def core_kernel(place, targets, signs, inverse, planes, out):
    total, share, rank = planes.shape
    out_rows = out.shape[0]
    values = []
    for r in range(out_rows):
        row = place[0] * out_rows + r
        slot = lax.rem(row, BLOCK)
        block = lax.div(row, BLOCK)
        value = jnp.zeros((share, rank), jnp.float32)
        for m in range(total // BLOCK):
            plane = m * BLOCK + slot
            weight = jnp.float32(0)
            for t in range(targets.shape[1]):
                sign = (2 * signs[plane, t] - 1).astype(jnp.float32)
                weight = weight + jnp.where(targets[plane, t] == block, sign, 0.0)
            value = value + weight * planes[plane]
        values.append(value)
    whole = mm_nt(jnp.concatenate(values, axis=0), inverse[...])
    for r in range(out_rows):
        out[r] = whole[r * share : r * share + share, :]


def call(kernel, out_shapes, in_specs, flops, scratch=(), mib=48):
    return pl.pallas_call(
        kernel,
        out_shape=out_shapes,
        in_specs=in_specs,
        out_specs=jax.tree.map(lambda _: VMEM, out_shapes),
        scratch_shapes=scratch,
        compiler_params=pltpu.CompilerParams(vmem_limit_bytes=int(mib * 2**20)),
        cost_estimate=pl.CostEstimate(flops=flops, bytes_accessed=2**20, transcendentals=0),
    )


def swap(block, axis):
    perm = [(n, n ^ 1) for n in range(lax.axis_size(axis))]
    return lax.ppermute(block, axis, perm)


def body(
    scalar_field, plane_sketch, second_sketch, third_sketch, mixing, plane_targets, plane_signs
):
    gx, ay, ac = lax.axis_size("gx"), lax.axis_size("ay"), lax.axis_size("ac")
    planes, rows, cells = scalar_field.shape
    rank = mixing.shape[2]
    own = cells // (gx * ay * ac)
    strip = rows // (gx * ay)
    share = rank // (ay * ac)
    place = jnp.stack([lax.axis_index(axis) for axis in ("gx", "ay", "ac")]).astype(jnp.int32)
    f32 = functools.partial(jax.ShapeDtypeStruct, dtype=jnp.float32)
    third_blocks = (gx * ay, own, rank)
    second_blocks = (gx * ay, strip, rank)

    sources = (third_sketch, plane_sketch, scalar_field, second_sketch, mixing)
    kept, given = call(
        functools.partial(sketch_kernel, gx, ay, ac),
        [f32((gx * ay, own + strip, rank)), f32(third_blocks)],
        [SMEM] + [pl.BlockSpec(memory_space=pltpu.HBM)] * 5,
        10**9,
        [pltpu.VMEM(source.shape, jnp.float32) for source in sources]
        + [pltpu.VMEM((ac,) + third_blocks, jnp.float32), pltpu.SemaphoreType.DMA((5,))],
        62,
    )(place, scalar_field, plane_sketch, second_sketch, third_sketch, mixing)
    slots = call(slots_kernel, f32((gx * ay, own + strip, rank)), [VMEM] * 2, 10**6)(
        kept, swap(given, "ac")
    )
    received = lax.all_to_all(slots, ("gx", "ay"), 0, 0, tiled=True)
    copies = call(
        functools.partial(total_kernel, gx, ay, own),
        f32((gx * ay, own + ay * strip, rank)),
        [VMEM],
        10**6,
    )(received)
    same = lax.all_to_all(copies, ("gx", "ay"), 0, 0, tiled=True)
    other = swap(same, "ac")
    across = swap(scalar_field, "ay")
    fields = (scalar_field, swap(scalar_field, "ac"), across, swap(across, "ac"))
    factor_second, partial = call(
        functools.partial(second_kernel, gx, ay, ac),
        [f32((own, rank)), f32((gx, planes, share, rank))],
        [SMEM] + [VMEM] * (2 + ay * ac),
        2 * 10**9,
        [
            pltpu.VMEM((ay, ac) + second_blocks, jnp.float32),
            pltpu.VMEM((gx * ay, ac, own, rank), jnp.float32),
        ],
    )(place, same, other, *fields)
    every = lax.all_to_all(partial, "gx", 0, 0, tiled=True)
    factor_third, inverse_third = call(
        functools.partial(third_kernel, gx, ay, ac, own),
        [f32((own, rank)), f32((rank, rank))],
        [SMEM] + [VMEM] * 2,
        10**9,
        [pltpu.VMEM((gx * ay, ac, own, rank), jnp.float32)],
    )(place, same, other)
    core_sketch = call(
        core_kernel,
        f32((BLOCKS * BLOCK // gx, share, rank)),
        [SMEM] * 3 + [VMEM] * 2,
        10**8,
    )(place, plane_targets, plane_signs, inverse_third, every.reshape(gx * planes, share, rank))
    return (factor_second, factor_third, core_sketch)


def solution(mesh):
    gx, af = mesh.devices.shape
    mesh = jax.sharding.Mesh(mesh.devices.reshape(gx, af // 2, 2), ("gx", "ay", "ac"))
    af = ("ay", "ac")
    in_specs = (P("gx", af, None), P("gx", None, None), P(af, None), P(), P(), P(), P())
    out_specs = (P(af + ("gx",), None), P(("gx",) + af, None), P("gx", af, None))
    return jax.shard_map(body, mesh=mesh, in_specs=in_specs, out_specs=out_specs, check_vma=False)
```

```python
import functools

import jax
import jax.numpy as jnp
from jax import lax
from jax.experimental import pallas as pl
from jax.experimental.pallas import tpu as pltpu
from jax.sharding import PartitionSpec as P

BLOCK = 16
BLOCKS = 8
SUB = 8

precise = lax.Precision.HIGHEST
VMEM = pl.BlockSpec(memory_space=pltpu.VMEM)
SMEM = pl.BlockSpec(memory_space=pltpu.SMEM)
HBM = pl.BlockSpec(memory_space=pltpu.HBM)


def dot(left, right, dims):
    return lax.dot_general(
        left, right, (dims, ((), ())), precision=precise, preferred_element_type=jnp.float32
    )


def mm(left, right):
    return dot(left, right, ((1,), (0,)))


def mm_tn(left, right):
    return dot(left, right, ((0,), (0,)))


def mm_nt(left, right):
    return dot(left, right, ((1,), (1,)))


def split(value):
    high = value.astype(jnp.bfloat16)
    return high, (value - high.astype(jnp.float32)).astype(jnp.bfloat16)


def dot_split(left, right, dims):
    def one(x, y):
        return lax.dot_general(x, y, (dims, ((), ())), preferred_element_type=jnp.float32)

    return one(left[0], right[0]) + (one(left[0], right[1]) + one(left[1], right[0]))


def inverse_lower(gram, tasks=()):
    size = gram.shape[0]
    count = size // SUB
    tasks = list(tasks)
    sub_ids = lax.broadcasted_iota(jnp.int32, (SUB, size), 0)
    lane_ids = lax.broadcasted_iota(jnp.int32, (SUB, size), 1)
    rows = [gram[SUB * i : SUB * i + SUB, :] for i in range(count)]
    done = []

    def along_sub(tile, j):
        return jnp.broadcast_to(tile[j : j + 1, :], (SUB, size))

    def along_lanes(tile, block):
        return [
            jnp.broadcast_to(tile[:, SUB * block + c : SUB * block + c + 1], (SUB, size))
            for c in range(SUB)
        ]

    diag = along_lanes(rows[0], 0)
    for k in range(count):
        inside = (lane_ids >= SUB * k) & (lane_ids < SUB * k + SUB)
        cols = {i: along_lanes(rows[i], k) for i in range(k + 1, count)}
        ahead = along_lanes(rows[k + 1], k + 1) if k + 1 < count else None
        identity = jnp.where(lane_ids == sub_ids + SUB * k, 1.0, 0.0)
        rows[k] = jnp.where(inside, identity, rows[k])
        for i in range(k + 1, count):
            rows[i] = jnp.where(inside, 0.0, rows[i])
        pivots = None
        for j in range(SUB):
            pivot = along_sub(diag[j], j)
            pivots = pivot if j == 0 else jnp.where(sub_ids == j, pivot, pivots)
            scale = 1.0 / pivot
            heads = {c: along_sub(diag[c], j) for c in range(j + 1, SUB)}
            row_head = along_sub(rows[k], j)
            if j < SUB - 1:
                below = jnp.where(sub_ids > j, diag[j], 0.0)
                diag[j + 1] = diag[j + 1] - (below * heads[j + 1]) * scale
                factor = below * scale
                for c in range(j + 2, SUB):
                    diag[c] = diag[c] - factor * heads[c]
                rows[k] = rows[k] - factor * row_head
            for i in range(k + 1, count):
                factor = cols[i][j] * scale
                if i == k + 1:
                    for c in range(SUB):
                        ahead[c] = ahead[c] - factor * along_sub(cols[i][j], c)
                for c in range(j + 1, SUB):
                    cols[i][c] = cols[i][c] - factor * heads[c]
                rows[i] = rows[i] - factor * row_head
        kept = jnp.where(lane_ids < SUB * k + SUB, rows[k], 0.0)
        done.append(kept * lax.rsqrt(pivots))
        diag = ahead
        for task in tasks[: -(-len(tasks) // (count - k))]:
            task()
        tasks = tasks[-(-len(tasks) // (count - k)) :]
    return jnp.concatenate(done, axis=0)


def place():
    return [lax.axis_index(axis) for axis in ("gx", "ay", "ac")]


def fetch(sources, held, arrived):
    copies = [
        pltpu.make_async_copy(source, target, arrived.at[n])
        for n, (source, target) in enumerate(zip(sources, held))
    ]
    for copy in copies:
        copy.start()
    for copy in copies:
        copy.wait()


def third_sketch_kernel(
    gx, ay, ac, field_in, plane_in, second_in, mixing_in, kept, given, *scratch
):
    field, plane_sketch, second_sketch, mixing, blocks, arrived = scratch
    fetch(
        (field_in, plane_in, second_in, mixing_in.at[1]),
        (field, plane_sketch, second_sketch, mixing),
        arrived,
    )
    core = place()[2]
    wide = None
    for p in range(field.shape[0]):
        weights = mm(second_sketch[...] * plane_sketch[p, 1:2, :], mixing[...])
        term = mm_tn(field[p], weights)
        wide = term if wide is None else wide + term
    own = blocks.shape[2]
    for c in range(ac):
        for n in range(gx * ay):
            first = (c * gx * ay + n) * own
            blocks[c, n] = wide[first : first + own, :]
    kept[...] = blocks[core]
    given[...] = blocks[1 - core]


def second_sketch_kernel(gx, ay, field, plane_sketch, third_sketch, mixing, kept, out):
    planes, rows, cells = field.shape
    across = None
    for p in range(planes):
        term = mm(field[p], third_sketch[...] * plane_sketch[p, 0:1, :])
        across = term if across is None else across + term
    second = mm(across, mixing[0])
    strip = rows // (gx * ay)
    own = kept.shape[1]
    out[:, 0:own, :] = kept[...]
    for n in range(gx * ay):
        out[n, own:, :] = second[n * strip : n * strip + strip, :]


def slots_kernel(kept, taken, out):
    own = taken.shape[1]
    out[:, 0:own, :] = kept[:, 0:own, :] + taken[...]
    out[:, own:, :] = kept[:, own:, :]


def total_kernel(gx, ay, own, received, out):
    strip = received.shape[1] - own
    third = received[0, 0:own, :]
    for n in range(1, gx * ay):
        third = third + received[n, 0:own, :]
    seconds = []
    for y in range(ay):
        second = received[y, own:, :]
        for g in range(1, gx):
            second = second + received[g * ay + y, own:, :]
        seconds.append(second)
    for n in range(gx * ay):
        out[n, 0:own, :] = third
        for y in range(ay):
            out[n, own + y * strip : own + (y + 1) * strip, :] = seconds[y]


def second_kernel(gx, ay, ac, same, other, *refs):
    fields, (factor, partial, second, third) = refs[: ay * ac], refs[ay * ac :]
    at = place()
    planes, rows, cells = fields[0].shape
    own = cells // (gx * ay * ac)
    strip = rows // (gx * ay)
    rank = same.shape[2]
    for swapped, ranges in enumerate((same, other)):
        core = at[2] ^ swapped
        for n in range(gx * ay):
            third[core * (gx * ay) + n] = ranges[n, 0:own, :]
            for y in range(ay):
                second[y, core, n] = ranges[n, own + y * strip : own + (y + 1) * strip, :]

    def quarter(y, c):
        return jnp.concatenate([second[y, c, n] for n in range(gx * ay)], axis=0)

    all_second = jnp.concatenate([quarter(y, c) for y in range(ay) for c in range(ac)], axis=0)
    gram = mm_tn(all_second, all_second)
    all_third = split(jnp.concatenate([third[n] for n in range(gx * ay * ac)], axis=0))
    raw = [None] * planes

    def project(mask, p):
        left = split(quarter(at[1] ^ (mask // ac), at[2] ^ (mask % ac)))
        right = split(dot_split(split(fields[mask][p]), all_third, ((1,), (0,))))
        term = dot_split(left, right, ((0,), (0,)))
        raw[p] = term if raw[p] is None else raw[p] + term

    inverse = inverse_lower(
        gram,
        [functools.partial(project, mask, p) for mask in range(ay * ac) for p in range(planes)],
    )
    mine = [second[at[1], at[2], at[0] * ay + y] for y in range(ay)]
    factor[...] = mm_nt(jnp.concatenate(mine, axis=0), inverse)
    share = rank // (ay * ac)
    own_rows = inverse[0:share, :]
    for a in range(1, ay * ac):
        piece = inverse[a * share : a * share + share, :]
        own_rows = jnp.where(at[1] * ac + at[2] == a, piece, own_rows)
    for p in range(planes):
        value = mm(own_rows, raw[p])
        for g in range(gx):
            partial[g, p] = value


def third_kernel(gx, ay, ac, own, same, other, factor, inverse_out, third):
    at = place()
    for swapped, ranges in enumerate((same, other)):
        for n in range(gx * ay):
            third[(at[2] ^ swapped) * (gx * ay) + n] = ranges[n, 0:own, :]
    all_third = jnp.concatenate([third[n] for n in range(gx * ay * ac)], axis=0)
    inverse = inverse_lower(mm_tn(all_third, all_third))
    inverse_out[...] = inverse
    factor[...] = mm_nt(third[(at[0] * ay + at[1]) * ac + at[2]], inverse)


def core_kernel(targets, signs, inverse, planes, out):
    total, share, rank = planes.shape
    out_rows = out.shape[0]
    first = place()[0] * out_rows
    values = []
    for r in range(out_rows):
        slot = lax.rem(first + r, BLOCK)
        block = lax.div(first + r, BLOCK)
        value = jnp.zeros((share, rank), jnp.float32)
        for m in range(total // BLOCK):
            plane = m * BLOCK + slot
            weight = jnp.float32(0)
            for t in range(targets.shape[1]):
                sign = (2 * signs[plane, t] - 1).astype(jnp.float32)
                weight = weight + jnp.where(targets[plane, t] == block, sign, 0.0)
            value = value + weight * planes[plane]
        values.append(value)
    whole = mm_nt(jnp.concatenate(values, axis=0), inverse[...])
    for r in range(out_rows):
        out[r] = whole[r * share : r * share + share, :]


def call(kernel, out_shapes, in_specs, flops, scratch=(), mib=48):
    return pl.pallas_call(
        kernel,
        out_shape=out_shapes,
        in_specs=in_specs,
        out_specs=jax.tree.map(lambda _: VMEM, out_shapes),
        scratch_shapes=scratch,
        compiler_params=pltpu.CompilerParams(vmem_limit_bytes=int(mib * 2**20)),
        cost_estimate=pl.CostEstimate(flops=flops, bytes_accessed=2**20, transcendentals=0),
    )


def swap(block, axis):
    perm = [(n, n ^ 1) for n in range(lax.axis_size(axis))]
    return lax.ppermute(block, axis, perm)


def body(
    scalar_field, plane_sketch, second_sketch, third_sketch, mixing, plane_targets, plane_signs
):
    gx, ay, ac = lax.axis_size("gx"), lax.axis_size("ay"), lax.axis_size("ac")
    planes, rows, cells = scalar_field.shape
    rank = mixing.shape[2]
    own = cells // (gx * ay * ac)
    strip = rows // (gx * ay)
    share = rank // (ay * ac)
    f32 = functools.partial(jax.ShapeDtypeStruct, dtype=jnp.float32)
    third_blocks = (gx * ay, own, rank)
    second_blocks = (gx * ay, strip, rank)

    kept, given = call(
        functools.partial(third_sketch_kernel, gx, ay, ac),
        [f32(third_blocks), f32(third_blocks)],
        [HBM] * 4,
        10**9,
        [
            pltpu.VMEM(scalar_field.shape, jnp.float32),
            pltpu.VMEM(plane_sketch.shape, jnp.float32),
            pltpu.VMEM(second_sketch.shape, jnp.float32),
            pltpu.VMEM(mixing.shape[1:], jnp.float32),
            pltpu.VMEM((ac,) + third_blocks, jnp.float32),
            pltpu.SemaphoreType.DMA((4,)),
        ],
        62,
    )(scalar_field, plane_sketch, second_sketch, mixing)
    taken = swap(given, "ac")
    slots = call(
        functools.partial(second_sketch_kernel, gx, ay),
        f32((gx * ay, own + strip, rank)),
        [VMEM] * 5,
        10**9,
    )(scalar_field, plane_sketch, third_sketch, mixing, kept)
    slots = call(slots_kernel, f32(slots.shape), [VMEM] * 2, 10**6)(slots, taken)
    received = lax.all_to_all(slots, ("gx", "ay"), 0, 0, tiled=True)
    copies = call(
        functools.partial(total_kernel, gx, ay, own),
        f32((gx * ay, own + ay * strip, rank)),
        [VMEM],
        10**6,
    )(received)
    same = lax.all_to_all(copies, ("gx", "ay"), 0, 0, tiled=True)
    other = swap(same, "ac")
    across = swap(scalar_field, "ay")
    fields = (scalar_field, swap(scalar_field, "ac"), across, swap(across, "ac"))
    factor_second, partial = call(
        functools.partial(second_kernel, gx, ay, ac),
        [f32((own, rank)), f32((gx, planes, share, rank))],
        [VMEM] * (2 + ay * ac),
        2 * 10**9,
        [
            pltpu.VMEM((ay, ac) + second_blocks, jnp.float32),
            pltpu.VMEM((gx * ay * ac, own, rank), jnp.float32),
        ],
    )(same, other, *fields)
    every = lax.all_to_all(partial, "gx", 0, 0, tiled=True)
    factor_third, inverse_third = call(
        functools.partial(third_kernel, gx, ay, ac, own),
        [f32((own, rank)), f32((rank, rank))],
        [VMEM] * 2,
        10**9,
        [pltpu.VMEM((gx * ay * ac, own, rank), jnp.float32)],
    )(same, other)
    core_sketch = call(
        core_kernel,
        f32((BLOCKS * BLOCK // gx, share, rank)),
        [SMEM] * 2 + [VMEM] * 2,
        10**8,
    )(plane_targets, plane_signs, inverse_third, every.reshape(gx * planes, share, rank))
    return (factor_second, factor_third, core_sketch)


def solution(mesh):
    gx, af = mesh.devices.shape
    mesh = jax.sharding.Mesh(mesh.devices.reshape(gx, af // 2, 2), ("gx", "ay", "ac"))
    af = ("ay", "ac")
    in_specs = (P("gx", af, None), P("gx", None, None), P(af, None), P(), P(), P(), P())
    out_specs = (P(af + ("gx",), None), P(("gx",) + af, None), P("gx", af, None))
    return jax.shard_map(body, mesh=mesh, in_specs=in_specs, out_specs=out_specs, check_vma=False)
```

```python
import functools

import jax
import jax.numpy as jnp
from jax import lax
from jax.experimental import pallas as pl
from jax.experimental.pallas import tpu as pltpu
from jax.sharding import PartitionSpec as P

BLOCK = 16
BLOCKS = 8
SUB = 8

precise = lax.Precision.HIGHEST
VMEM = pl.BlockSpec(memory_space=pltpu.VMEM)
SMEM = pl.BlockSpec(memory_space=pltpu.SMEM)
HBM = pl.BlockSpec(memory_space=pltpu.HBM)


def dot(left, right, dims):
    return lax.dot_general(
        left, right, (dims, ((), ())), precision=precise, preferred_element_type=jnp.float32
    )


def mm(left, right):
    return dot(left, right, ((1,), (0,)))


def mm_tn(left, right):
    return dot(left, right, ((0,), (0,)))


def mm_nt(left, right):
    return dot(left, right, ((1,), (1,)))


def inverse_lower(gram, tasks=()):
    size = gram.shape[0]
    count = size // SUB
    tasks = list(tasks)
    sub_ids = lax.broadcasted_iota(jnp.int32, (SUB, size), 0)
    lane_ids = lax.broadcasted_iota(jnp.int32, (SUB, size), 1)
    rows = [gram[SUB * i : SUB * i + SUB, :] for i in range(count)]
    done = []

    def along_sub(tile, j):
        return jnp.broadcast_to(tile[j : j + 1, :], (SUB, size))

    def along_lanes(tile, block):
        return [
            jnp.broadcast_to(tile[:, SUB * block + c : SUB * block + c + 1], (SUB, size))
            for c in range(SUB)
        ]

    diag = along_lanes(rows[0], 0)
    pivot = along_sub(diag[0], 0)
    for k in range(count):
        inside = (lane_ids >= SUB * k) & (lane_ids < SUB * k + SUB)
        cols = {i: along_lanes(rows[i], k) for i in range(k + 1, count)}
        ahead = along_lanes(rows[k + 1], k + 1) if k + 1 < count else None
        identity = jnp.where(lane_ids == sub_ids + SUB * k, 1.0, 0.0)
        rows[k] = jnp.where(inside, identity, rows[k])
        for i in range(k + 1, count):
            rows[i] = jnp.where(inside, 0.0, rows[i])
        pivots = None
        for j in range(SUB):
            pivots = pivot if j == 0 else jnp.where(sub_ids == j, pivot, pivots)
            scale = 1.0 / pivot
            heads = {c: along_sub(diag[c], j) for c in range(j + 1, SUB)}
            row_head = along_sub(rows[k], j)
            if j < SUB - 1:
                pivot = along_sub(diag[j + 1], j + 1) - (heads[j + 1] * heads[j + 1]) * scale
            elif k + 1 < count:
                head = along_sub(cols[k + 1][j], 0)
                pivot = along_sub(ahead[0], 0) - (head * head) * scale
            if j < SUB - 1:
                below = jnp.where(sub_ids > j, diag[j], 0.0)
                diag[j + 1] = diag[j + 1] - (below * heads[j + 1]) * scale
                factor = below * scale
                for c in range(j + 2, SUB):
                    diag[c] = diag[c] - factor * heads[c]
                rows[k] = rows[k] - factor * row_head
            for i in range(k + 1, count):
                factor = cols[i][j] * scale
                if i == k + 1:
                    for c in range(SUB):
                        ahead[c] = ahead[c] - factor * along_sub(cols[i][j], c)
                for c in range(j + 1, SUB):
                    cols[i][c] = cols[i][c] - factor * heads[c]
                rows[i] = rows[i] - factor * row_head
        kept = jnp.where(lane_ids < SUB * k + SUB, rows[k], 0.0)
        done.append(kept * lax.rsqrt(pivots))
        diag = ahead
        for task in tasks[: -(-len(tasks) // (count - k))]:
            task()
        tasks = tasks[-(-len(tasks) // (count - k)) :]
    return jnp.concatenate(done, axis=0)


def place():
    return [lax.axis_index(axis) for axis in ("gx", "ay", "ac")]


def half_of(field, weights, half):
    planes, rows, cells = field.shape
    width = cells // 2
    lanes = pl.ds(pl.multiple_of(half * width, width), width)
    return mm_tn(field[:, :, lanes].reshape(planes * rows, width), weights)


def weights_of(second_sketch, plane_sketch, mixing):
    planes = plane_sketch.shape[0]
    scaled = [second_sketch[...] * plane_sketch[p, 1:2, :] for p in range(planes)]
    return mm(jnp.concatenate(scaled, axis=0), mixing)


def third_sketch_kernel(field_in, plane_in, second_in, mixing_in, given, *scratch):
    field, plane_sketch, second_sketch, mixing, arrived = scratch
    copies = [
        pltpu.make_async_copy(source, target, arrived.at[n])
        for n, (source, target) in enumerate(
            (
                (plane_in, plane_sketch),
                (second_in, second_sketch),
                (mixing_in.at[1], mixing),
                (field_in, field),
            )
        )
    ]
    for copy in copies:
        copy.start()
    for copy in copies[:3]:
        copy.wait()
    weights = weights_of(second_sketch, plane_sketch, mixing[...])
    copies[3].wait()
    wide = half_of(field, weights, 1 - place()[2])
    own = wide.shape[0] // given.shape[0]
    for n in range(given.shape[0]):
        given[n, 0:own, :] = wide[n * own : n * own + own, :]
        given[n, own:, :] = jnp.zeros((given.shape[1] - own, given.shape[2]), jnp.float32)


def second_sketch_kernel(
    own, field, plane_sketch, second_sketch, third_sketch, mixing, out
):
    planes, rows, cells = field.shape
    across = None
    for p in range(planes):
        term = mm(field[p], third_sketch[...] * plane_sketch[p, 0:1, :])
        across = term if across is None else across + term
    second = mm(across, mixing[0])
    wide = half_of(field, weights_of(second_sketch, plane_sketch, mixing[1]), place()[2])
    strip = out.shape[1] - own
    for n in range(out.shape[0]):
        out[n, 0:own, :] = wide[n * own : n * own + own, :]
        out[n, own:, :] = second[n * strip : n * strip + strip, :]


def total_kernel(gx, ay, own, received, out):
    strip = received.shape[1] - own
    third = received[0, 0:own, :]
    for n in range(1, gx * ay):
        third = third + received[n, 0:own, :]
    seconds = []
    for y in range(ay):
        second = received[y, own:, :]
        for g in range(1, gx):
            second = second + received[g * ay + y, own:, :]
        seconds.append(second)
    for n in range(gx * ay):
        out[n, 0:own, :] = third
        for y in range(ay):
            out[n, own + y * strip : own + (y + 1) * strip, :] = seconds[y]


def second_kernel(gx, ay, ac, same, other, *refs):
    fields, (factor, partial, second, third) = refs[: ay * ac], refs[ay * ac :]
    at = place()
    planes, rows, cells = fields[0].shape
    own = cells // (gx * ay * ac)
    strip = rows // (gx * ay)
    rank = same.shape[2]
    for swapped, ranges in enumerate((same, other)):
        core = at[2] ^ swapped
        for n in range(gx * ay):
            third[core * (gx * ay) + n] = ranges[n, 0:own, :]
            for y in range(ay):
                second[y, core, n] = ranges[n, own + y * strip : own + (y + 1) * strip, :]

    def quarter(y, c):
        return jnp.concatenate([second[y, c, n] for n in range(gx * ay)], axis=0)

    all_second = jnp.concatenate([quarter(y, c) for y in range(ay) for c in range(ac)], axis=0)
    gram = mm_tn(all_second, all_second)
    all_third = jnp.concatenate([third[n] for n in range(gx * ay * ac)], axis=0)
    group = [(at[1] ^ (mask // ac), at[2] ^ (mask % ac)) for mask in range(ay * ac)]
    along = [[None] * planes for _ in group]
    raw = [None]

    def field_product(mask, p):
        along[mask][p] = mm(fields[mask][p], all_third)

    def range_product():
        right = [jnp.concatenate(terms, axis=1) for terms in along]
        left = [quarter(y, c) for y, c in group]
        raw[0] = mm_tn(jnp.concatenate(left, axis=0), jnp.concatenate(right, axis=0))

    tasks = [
        functools.partial(field_product, mask, p) for mask in range(len(group)) for p in range(planes)
    ]
    inverse = inverse_lower(gram, tasks + [range_product])
    mine = [second[at[1], at[2], at[0] * ay + y] for y in range(ay)]
    factor[...] = mm_nt(jnp.concatenate(mine, axis=0), inverse)
    share = rank // (ay * ac)
    own_rows = inverse[0:share, :]
    for a in range(1, ay * ac):
        piece = inverse[a * share : a * share + share, :]
        own_rows = jnp.where(at[1] * ac + at[2] == a, piece, own_rows)
    value = mm(own_rows, raw[0])
    for p in range(planes):
        for g in range(gx):
            partial[g, p] = value[:, p * rank : p * rank + rank]


def third_kernel(gx, ay, ac, own, same, other, factor, inverse_out, third):
    at = place()
    for swapped, ranges in enumerate((same, other)):
        for n in range(gx * ay):
            third[(at[2] ^ swapped) * (gx * ay) + n] = ranges[n, 0:own, :]
    all_third = jnp.concatenate([third[n] for n in range(gx * ay * ac)], axis=0)
    inverse = inverse_lower(mm_tn(all_third, all_third))
    inverse_out[...] = inverse
    factor[...] = mm_nt(third[(at[0] * ay + at[1]) * ac + at[2]], inverse)


def core_kernel(targets, signs, inverse, planes, out, held, sent):
    total, share, rank = planes.shape
    out_rows = out.shape[0]
    first = place()[0] * out_rows

    def one_row(r):
        slot = lax.rem(first + r, BLOCK)
        block = lax.div(first + r, BLOCK)
        value = jnp.zeros((share, rank), jnp.float32)
        for m in range(total // BLOCK):
            plane = m * BLOCK + slot
            weight = jnp.float32(0)
            for t in range(targets.shape[1]):
                sign = (2 * signs[plane, t] - 1).astype(jnp.float32)
                weight = weight + jnp.where(targets[plane, t] == block, sign, 0.0)
            value = value + weight * planes[plane]
        return value

    parts = min(4, out_rows)
    size = out_rows // parts
    copies = []
    for part in range(parts):
        rows = range(part * size, part * size + size)
        whole = mm_nt(jnp.concatenate([one_row(r) for r in rows], axis=0), inverse[...])
        for n, r in enumerate(rows):
            held[r] = whole[n * share : n * share + share, :]
        span = pl.ds(part * size, size)
        copies.append(pltpu.make_async_copy(held.at[span], out.at[span], sent.at[part]))
        copies[-1].start()
    for copy in copies:
        copy.wait()


def call(kernel, out_shapes, in_specs, flops, scratch=(), mib=48, out_spec=VMEM):
    return pl.pallas_call(
        kernel,
        out_shape=out_shapes,
        in_specs=in_specs,
        out_specs=jax.tree.map(lambda _: out_spec, out_shapes),
        scratch_shapes=scratch,
        compiler_params=pltpu.CompilerParams(vmem_limit_bytes=int(mib * 2**20)),
        cost_estimate=pl.CostEstimate(flops=flops, bytes_accessed=2**20, transcendentals=0),
    )


def swap(block, axis):
    perm = [(n, n ^ 1) for n in range(lax.axis_size(axis))]
    return lax.ppermute(block, axis, perm)


def body(
    scalar_field, plane_sketch, second_sketch, third_sketch, mixing, plane_targets, plane_signs
):
    gx, ay, ac = lax.axis_size("gx"), lax.axis_size("ay"), lax.axis_size("ac")
    planes, rows, cells = scalar_field.shape
    rank = mixing.shape[2]
    own = cells // (gx * ay * ac)
    strip = rows // (gx * ay)
    share = rank // (ay * ac)
    f32 = functools.partial(jax.ShapeDtypeStruct, dtype=jnp.float32)
    second_blocks = (gx * ay, strip, rank)

    slot = f32((gx * ay, own + strip, rank))
    given = call(
        third_sketch_kernel,
        slot,
        [HBM] * 4,
        10**9,
        [
            pltpu.VMEM(scalar_field.shape, jnp.float32),
            pltpu.VMEM(plane_sketch.shape, jnp.float32),
            pltpu.VMEM(second_sketch.shape, jnp.float32),
            pltpu.VMEM(mixing.shape[1:], jnp.float32),
            pltpu.SemaphoreType.DMA((4,)),
        ],
        62,
    )(scalar_field, plane_sketch, second_sketch, mixing)
    taken = swap(given, "ac")
    kept = call(functools.partial(second_sketch_kernel, own), slot, [VMEM] * 5, 10**9)(
        scalar_field, plane_sketch, second_sketch, third_sketch, mixing
    )
    slots = kept + taken
    received = lax.all_to_all(slots, ("gx", "ay"), 0, 0, tiled=True)
    copies = call(
        functools.partial(total_kernel, gx, ay, own),
        f32((gx * ay, own + ay * strip, rank)),
        [VMEM],
        10**6,
    )(received)
    same = lax.all_to_all(copies, ("gx", "ay"), 0, 0, tiled=True)
    other = swap(same, "ac")
    across = swap(scalar_field, "ay")
    fields = (scalar_field, swap(scalar_field, "ac"), across, swap(across, "ac"))
    factor_second, partial = call(
        functools.partial(second_kernel, gx, ay, ac),
        [f32((own, rank)), f32((gx, planes, share, rank))],
        [VMEM] * (2 + ay * ac),
        2 * 10**9,
        [
            pltpu.VMEM((ay, ac) + second_blocks, jnp.float32),
            pltpu.VMEM((gx * ay * ac, own, rank), jnp.float32),
        ],
    )(same, other, *fields)
    every = lax.all_to_all(partial, "gx", 0, 0, tiled=True)
    factor_third, inverse_third = call(
        functools.partial(third_kernel, gx, ay, ac, own),
        [f32((own, rank)), f32((rank, rank))],
        [VMEM] * 2,
        10**9,
        [pltpu.VMEM((gx * ay * ac, own, rank), jnp.float32)],
    )(same, other)
    out_rows = BLOCKS * BLOCK // gx
    core_sketch = call(
        core_kernel,
        f32((out_rows, share, rank)),
        [SMEM] * 2 + [VMEM] * 2,
        10**8,
        [pltpu.VMEM((out_rows, share, rank), jnp.float32), pltpu.SemaphoreType.DMA((4,))],
        out_spec=HBM,
    )(plane_targets, plane_signs, inverse_third, every.reshape(gx * planes, share, rank))
    return (factor_second, factor_third, core_sketch)


def solution(mesh):
    gx, af = mesh.devices.shape
    mesh = jax.sharding.Mesh(mesh.devices.reshape(gx, af // 2, 2), ("gx", "ay", "ac"))
    af = ("ay", "ac")
    in_specs = (P("gx", af, None), P("gx", None, None), P(af, None), P(), P(), P(), P())
    out_specs = (P(af + ("gx",), None), P(("gx",) + af, None), P("gx", af, None))
    return jax.shard_map(body, mesh=mesh, in_specs=in_specs, out_specs=out_specs, check_vma=False)
```

```python
import functools

import jax
import jax.numpy as jnp
from jax import lax
from jax.experimental import pallas as pl
from jax.experimental.pallas import tpu as pltpu
from jax.sharding import PartitionSpec as P

BLOCK = 16
BLOCKS = 8
SUB = 8
NEAR = 2

precise = lax.Precision.HIGHEST
VMEM = pl.BlockSpec(memory_space=pltpu.VMEM)
SMEM = pl.BlockSpec(memory_space=pltpu.SMEM)
HBM = pl.BlockSpec(memory_space=pltpu.HBM)


def dot(left, right, dims):
    return lax.dot_general(
        left, right, (dims, ((), ())), precision=precise, preferred_element_type=jnp.float32
    )


def mm(left, right):
    return dot(left, right, ((1,), (0,)))


def mm_tn(left, right):
    return dot(left, right, ((0,), (0,)))


def mm_nt(left, right):
    return dot(left, right, ((1,), (1,)))


def inverse_lower(gram, tasks=()):
    size = gram.shape[0]
    count = size // SUB
    tasks = list(tasks)
    sub_ids = lax.broadcasted_iota(jnp.int32, (SUB, size), 0)
    lane_ids = lax.broadcasted_iota(jnp.int32, (SUB, size), 1)
    rows = [gram[SUB * i : SUB * i + SUB, :] for i in range(count)]
    done = []

    def along_sub(tile, j):
        return jnp.broadcast_to(tile[j : j + 1, :], (SUB, size))

    def along_lanes(tile, block):
        return [
            jnp.broadcast_to(tile[:, SUB * block + c : SUB * block + c + 1], (SUB, size))
            for c in range(SUB)
        ]

    diag = along_lanes(rows[0], 0)
    pivot = along_sub(diag[0], 0)
    for k in range(count):
        inside = (lane_ids >= SUB * k) & (lane_ids < SUB * k + SUB)
        near = range(k + 1, min(k + 1 + NEAR, count))
        cols = {i: along_lanes(rows[i], k) for i in near}
        ahead = along_lanes(rows[k + 1], k + 1) if k + 1 < count else None
        identity = jnp.where(lane_ids == sub_ids + SUB * k, 1.0, 0.0)
        rows[k] = jnp.where(inside, identity, rows[k])
        for i in range(k + 1, count):
            rows[i] = jnp.where(inside, 0.0, rows[i])
        pivots, row_heads = None, []
        for j in range(SUB):
            pivots = pivot if j == 0 else jnp.where(sub_ids == j, pivot, pivots)
            scale = 1.0 / pivot
            heads = {c: along_sub(diag[c], j) for c in range(j + 1, SUB)}
            row_head = along_sub(rows[k], j)
            row_heads.append(row_head)
            if j < SUB - 1:
                pivot = along_sub(diag[j + 1], j + 1) - (heads[j + 1] * heads[j + 1]) * scale
            elif k + 1 < count:
                head = along_sub(cols[k + 1][j], 0)
                pivot = along_sub(ahead[0], 0) - (head * head) * scale
            if j < SUB - 1:
                below = jnp.where(sub_ids > j, diag[j], 0.0)
                diag[j + 1] = diag[j + 1] - (below * heads[j + 1]) * scale
                factor = below * scale
                for c in range(j + 2, SUB):
                    diag[c] = diag[c] - factor * heads[c]
                rows[k] = rows[k] - factor * row_head
            for i in near:
                factor = cols[i][j] * scale
                if i == k + 1:
                    for c in range(SUB):
                        ahead[c] = ahead[c] - factor * along_sub(cols[i][j], c)
                for c in range(j + 1, SUB):
                    cols[i][c] = cols[i][c] - factor * heads[c]
                rows[i] = rows[i] - factor * row_head
        if k + 1 + NEAR < count:
            turned = jnp.transpose(rows[k] * (1.0 / pivots))
            for i in range(k + 1 + NEAR, count):
                tile = turned[SUB * i : SUB * i + SUB, :]
                for j in range(SUB):
                    factor = jnp.broadcast_to(tile[:, j : j + 1], (SUB, size))
                    rows[i] = rows[i] - factor * row_heads[j]
        kept = jnp.where(lane_ids < SUB * k + SUB, rows[k], 0.0)
        done.append(kept * lax.rsqrt(pivots))
        diag = ahead
        for task in tasks[: -(-len(tasks) // (count - k))]:
            task()
        tasks = tasks[-(-len(tasks) // (count - k)) :]
    return jnp.concatenate(done, axis=0)


def place():
    return [lax.axis_index(axis) for axis in ("gx", "ay", "ac")]


def third_sketch_kernel(
    gx, ay, field_in, plane_in, second_in, mixing_in, kept, given, *scratch
):
    field, plane_sketch, second_sketch, mixing, blocks, arrived = scratch
    copies = [
        pltpu.make_async_copy(source, target, arrived.at[n])
        for n, (source, target) in enumerate(
            (
                (plane_in, plane_sketch),
                (second_in, second_sketch),
                (mixing_in.at[1], mixing),
                (field_in, field),
            )
        )
    ]
    for copy in copies:
        copy.start()
    for copy in copies[:3]:
        copy.wait()
    planes, rows, cells = field.shape
    scaled = [second_sketch[...] * plane_sketch[p, 1:2, :] for p in range(planes)]
    weights = mm(jnp.concatenate(scaled, axis=0), mixing[...])
    copies[3].wait()
    wide = mm_tn(field[...].reshape(planes * rows, cells), weights)
    own = blocks.shape[2]
    for n in range(2 * gx * ay):
        blocks[n // (gx * ay), n % (gx * ay)] = wide[n * own : n * own + own, :]
    core = place()[2]
    blank = jnp.zeros((gx * ay, kept.shape[1] - own, kept.shape[2]), jnp.float32)
    for half, out in ((core, kept), (1 - core, given)):
        out[:, 0:own, :] = blocks[half]
        out[:, own:, :] = blank


def second_sketch_kernel(own, field, plane_sketch, third_sketch, mixing, out):
    planes, rows, cells = field.shape
    across = None
    for p in range(planes):
        term = mm(field[p], third_sketch[...] * plane_sketch[p, 0:1, :])
        across = term if across is None else across + term
    second = mm(across, mixing[0])
    strip = out.shape[1] - own
    for n in range(out.shape[0]):
        out[n, 0:own, :] = jnp.zeros((own, out.shape[2]), jnp.float32)
        out[n, own:, :] = second[n * strip : n * strip + strip, :]


def total_kernel(gx, ay, own, received, out):
    strip = received.shape[1] - own
    third = received[0, 0:own, :]
    for n in range(1, gx * ay):
        third = third + received[n, 0:own, :]
    seconds = []
    for y in range(ay):
        second = received[y, own:, :]
        for g in range(1, gx):
            second = second + received[g * ay + y, own:, :]
        seconds.append(second)
    for n in range(gx * ay):
        out[n, 0:own, :] = third
        for y in range(ay):
            out[n, own + y * strip : own + (y + 1) * strip, :] = seconds[y]


def second_kernel(gx, ay, ac, same, other, *refs):
    fields, (factor, partial, second, third) = refs[: ay * ac], refs[ay * ac :]
    at = place()
    planes, rows, cells = fields[0].shape
    own = cells // (gx * ay * ac)
    strip = rows // (gx * ay)
    rank = same.shape[2]
    for swapped, ranges in enumerate((same, other)):
        core = at[2] ^ swapped
        for n in range(gx * ay):
            third[core * (gx * ay) + n] = ranges[n, 0:own, :]
            for y in range(ay):
                second[y, core, n] = ranges[n, own + y * strip : own + (y + 1) * strip, :]

    def quarter(y, c):
        return jnp.concatenate([second[y, c, n] for n in range(gx * ay)], axis=0)

    all_second = jnp.concatenate([quarter(y, c) for y in range(ay) for c in range(ac)], axis=0)
    gram = mm_tn(all_second, all_second)
    all_third = jnp.concatenate([third[n] for n in range(gx * ay * ac)], axis=0)
    group = [(at[1] ^ (mask // ac), at[2] ^ (mask % ac)) for mask in range(ay * ac)]
    along = [[None] * planes for _ in group]
    raw = [None]

    def field_product(mask, p):
        along[mask][p] = mm(fields[mask][p], all_third)

    def range_product():
        right = [jnp.concatenate(terms, axis=1) for terms in along]
        left = [quarter(y, c) for y, c in group]
        raw[0] = mm_tn(jnp.concatenate(left, axis=0), jnp.concatenate(right, axis=0))

    tasks = [
        functools.partial(field_product, mask, p) for mask in range(len(group)) for p in range(planes)
    ]
    inverse = inverse_lower(gram, tasks + [range_product])
    mine = [second[at[1], at[2], at[0] * ay + y] for y in range(ay)]
    factor[...] = mm_nt(jnp.concatenate(mine, axis=0), inverse)
    share = rank // (ay * ac)
    own_rows = inverse[0:share, :]
    for a in range(1, ay * ac):
        piece = inverse[a * share : a * share + share, :]
        own_rows = jnp.where(at[1] * ac + at[2] == a, piece, own_rows)
    value = mm(own_rows, raw[0])
    for p in range(planes):
        for g in range(gx):
            partial[g, p] = value[:, p * rank : p * rank + rank]


def third_kernel(gx, ay, ac, own, targets, signs, same, other, factor, turned, weights, third):
    at = place()
    for swapped, ranges in enumerate((same, other)):
        for n in range(gx * ay):
            third[(at[2] ^ swapped) * (gx * ay) + n] = ranges[n, 0:own, :]
    all_third = jnp.concatenate([third[n] for n in range(gx * ay * ac)], axis=0)
    inverse = inverse_lower(mm_tn(all_third, all_third))
    turned[...] = jnp.transpose(inverse)
    factor[...] = mm_nt(third[(at[0] * ay + at[1]) * ac + at[2]], inverse)
    out_rows, turns, rank = weights.shape
    for r in range(out_rows):
        row = at[0] * out_rows + r
        for m in range(turns):
            plane = m * BLOCK + lax.rem(row, BLOCK)
            weight = jnp.float32(0)
            for t in range(targets.shape[1]):
                sign = (2 * signs[plane, t] - 1).astype(jnp.float32)
                weight = weight + jnp.where(targets[plane, t] == lax.div(row, BLOCK), sign, 0.0)
            weights[r, m : m + 1, :] = jnp.full((1, rank), weight, jnp.float32)


def core_kernel(weights, turned, planes, out):
    out_rows, turns, rank = weights.shape
    share = planes.shape[1]
    first = place()[0] * out_rows
    rows = []
    for r in range(out_rows):
        slot = r % BLOCK if out_rows % BLOCK == 0 else lax.rem(first + r, BLOCK)
        terms = [weights[r, m : m + 1, :] * planes[m * BLOCK + slot] for m in range(turns)]
        rows.append(sum(terms[1:], terms[0]))
    whole = mm(jnp.concatenate(rows, axis=0), turned[...])
    for r in range(out_rows):
        out[r] = whole[r * share : r * share + share, :]


def call(kernel, out_shapes, in_specs, flops, scratch=(), mib=48):
    return pl.pallas_call(
        kernel,
        out_shape=out_shapes,
        in_specs=in_specs,
        out_specs=jax.tree.map(lambda _: VMEM, out_shapes),
        scratch_shapes=scratch,
        compiler_params=pltpu.CompilerParams(vmem_limit_bytes=int(mib * 2**20)),
        cost_estimate=pl.CostEstimate(flops=flops, bytes_accessed=2**20, transcendentals=0),
    )


def swap(block, axis):
    perm = [(n, n ^ 1) for n in range(lax.axis_size(axis))]
    return lax.ppermute(block, axis, perm)


def body(
    scalar_field, plane_sketch, second_sketch, third_sketch, mixing, plane_targets, plane_signs
):
    gx, ay, ac = lax.axis_size("gx"), lax.axis_size("ay"), lax.axis_size("ac")
    planes, rows, cells = scalar_field.shape
    rank = mixing.shape[2]
    own = cells // (gx * ay * ac)
    strip = rows // (gx * ay)
    share = rank // (ay * ac)
    f32 = functools.partial(jax.ShapeDtypeStruct, dtype=jnp.float32)
    second_blocks = (gx * ay, strip, rank)

    slot = f32((gx * ay, own + strip, rank))
    kept, given = call(
        functools.partial(third_sketch_kernel, gx, ay),
        [slot, slot],
        [HBM] * 4,
        10**9,
        [
            pltpu.VMEM(scalar_field.shape, jnp.float32),
            pltpu.VMEM(plane_sketch.shape, jnp.float32),
            pltpu.VMEM(second_sketch.shape, jnp.float32),
            pltpu.VMEM(mixing.shape[1:], jnp.float32),
            pltpu.VMEM((ac, gx * ay, own, rank), jnp.float32),
            pltpu.SemaphoreType.DMA((4,)),
        ],
        62,
    )(scalar_field, plane_sketch, second_sketch, mixing)
    taken = swap(given, "ac")
    second = call(functools.partial(second_sketch_kernel, own), slot, [VMEM] * 4, 10**9)(
        scalar_field, plane_sketch, third_sketch, mixing
    )
    slots = kept + second + taken
    received = lax.all_to_all(slots, ("gx", "ay"), 0, 0, tiled=True)
    copies = call(
        functools.partial(total_kernel, gx, ay, own),
        f32((gx * ay, own + ay * strip, rank)),
        [VMEM],
        10**6,
    )(received)
    same = lax.all_to_all(copies, ("gx", "ay"), 0, 0, tiled=True)
    other = swap(same, "ac")
    across = swap(scalar_field, "ay")
    fields = (scalar_field, swap(scalar_field, "ac"), across, swap(across, "ac"))
    factor_second, partial = call(
        functools.partial(second_kernel, gx, ay, ac),
        [f32((own, rank)), f32((gx, planes, share, rank))],
        [VMEM] * (2 + ay * ac),
        2 * 10**9,
        [
            pltpu.VMEM((ay, ac) + second_blocks, jnp.float32),
            pltpu.VMEM((gx * ay * ac, own, rank), jnp.float32),
        ],
    )(same, other, *fields)
    every = lax.all_to_all(partial, "gx", 0, 0, tiled=True)
    out_rows = BLOCKS * BLOCK // gx
    factor_third, turned, weights = call(
        functools.partial(third_kernel, gx, ay, ac, own),
        [f32((own, rank)), f32((rank, rank)), f32((out_rows, gx * planes // BLOCK, rank))],
        [SMEM] * 2 + [VMEM] * 2,
        10**9,
        [pltpu.VMEM((gx * ay * ac, own, rank), jnp.float32)],
    )(plane_targets, plane_signs, same, other)
    core_sketch = call(core_kernel, f32((out_rows, share, rank)), [VMEM] * 3, 10**8)(
        weights, turned, every.reshape(gx * planes, share, rank)
    )
    return (factor_second, factor_third, core_sketch)


def solution(mesh):
    gx, af = mesh.devices.shape
    mesh = jax.sharding.Mesh(mesh.devices.reshape(gx, af // 2, 2), ("gx", "ay", "ac"))
    af = ("ay", "ac")
    in_specs = (P("gx", af, None), P("gx", None, None), P(af, None), P(), P(), P(), P())
    out_specs = (P(af + ("gx",), None), P(("gx",) + af, None), P("gx", af, None))
    return jax.shard_map(body, mesh=mesh, in_specs=in_specs, out_specs=out_specs, check_vma=False)
```

```python
import functools

import jax
import jax.numpy as jnp
from jax import lax
from jax.experimental import pallas as pl
from jax.experimental.pallas import tpu as pltpu
from jax.sharding import PartitionSpec as P

BLOCK = 16
BLOCKS = 8
SUB = 8

precise = lax.Precision.HIGHEST
VMEM = pl.BlockSpec(memory_space=pltpu.VMEM)
SMEM = pl.BlockSpec(memory_space=pltpu.SMEM)
HBM = pl.BlockSpec(memory_space=pltpu.HBM)


def dot(left, right, dims):
    return lax.dot_general(
        left, right, (dims, ((), ())), precision=precise, preferred_element_type=jnp.float32
    )


def mm(left, right):
    return dot(left, right, ((1,), (0,)))


def mm_tn(left, right):
    return dot(left, right, ((0,), (0,)))


def mm_nt(left, right):
    return dot(left, right, ((1,), (1,)))


def inverse_lower(gram, tasks=()):
    size = gram.shape[0]
    count = size // SUB
    tasks = list(tasks)
    sub_ids = lax.broadcasted_iota(jnp.int32, (SUB, size), 0)
    lane_ids = lax.broadcasted_iota(jnp.int32, (SUB, size), 1)
    rows = [gram[SUB * i : SUB * i + SUB, :] for i in range(count)]
    done = []

    def along_sub(tile, j):
        return jnp.broadcast_to(tile[j : j + 1, :], (SUB, size))

    def along_lanes(tile, block):
        return [
            jnp.broadcast_to(tile[:, SUB * block + c : SUB * block + c + 1], (SUB, size))
            for c in range(SUB)
        ]

    diag = along_lanes(rows[0], 0)
    pivot = along_sub(diag[0], 0)
    for k in range(count):
        inside = (lane_ids >= SUB * k) & (lane_ids < SUB * k + SUB)
        cols = {i: along_lanes(rows[i], k) for i in range(k + 1, count)}
        ahead = along_lanes(rows[k + 1], k + 1) if k + 1 < count else None
        identity = jnp.where(lane_ids == sub_ids + SUB * k, 1.0, 0.0)
        rows[k] = jnp.where(inside, identity, rows[k])
        for i in range(k + 1, count):
            rows[i] = jnp.where(inside, 0.0, rows[i])
        pivots = None
        for j in range(SUB):
            pivots = pivot if j == 0 else jnp.where(sub_ids == j, pivot, pivots)
            scale = 1.0 / pivot
            heads = {c: along_sub(diag[c], j) for c in range(j + 1, SUB)}
            row_head = along_sub(rows[k], j)
            if j < SUB - 1:
                pivot = along_sub(diag[j + 1], j + 1) - (heads[j + 1] * heads[j + 1]) * scale
            elif k + 1 < count:
                head = along_sub(cols[k + 1][j], 0)
                pivot = along_sub(ahead[0], 0) - (head * head) * scale
            if j < SUB - 1:
                below = jnp.where(sub_ids > j, diag[j], 0.0)
                diag[j + 1] = diag[j + 1] - (below * heads[j + 1]) * scale
                factor = below * scale
                for c in range(j + 2, SUB):
                    diag[c] = diag[c] - factor * heads[c]
                rows[k] = rows[k] - factor * row_head
            for i in range(k + 1, count):
                factor = cols[i][j] * scale
                if i == k + 1:
                    for c in range(SUB):
                        ahead[c] = ahead[c] - factor * along_sub(cols[i][j], c)
                for c in range(j + 1, SUB):
                    cols[i][c] = cols[i][c] - factor * heads[c]
                rows[i] = rows[i] - factor * row_head
        kept = jnp.where(lane_ids < SUB * k + SUB, rows[k], 0.0)
        done.append(kept * lax.rsqrt(pivots))
        diag = ahead
        for task in tasks[: -(-len(tasks) // (count - k))]:
            task()
        tasks = tasks[-(-len(tasks) // (count - k)) :]
    return jnp.concatenate(done, axis=0)


def place():
    return [lax.axis_index(axis) for axis in ("gx", "ay", "ac")]


def third_sketch_kernel(
    gx, ay, field_in, plane_in, second_in, mixing_in, kept, given, *scratch
):
    field, plane_sketch, second_sketch, mixing, blocks, arrived = scratch
    copies = [
        pltpu.make_async_copy(source, target, arrived.at[n])
        for n, (source, target) in enumerate(
            (
                (plane_in, plane_sketch),
                (second_in, second_sketch),
                (mixing_in.at[1], mixing),
                (field_in, field),
            )
        )
    ]
    for copy in copies:
        copy.start()
    for copy in copies[:3]:
        copy.wait()
    planes, rows, cells = field.shape
    scaled = [second_sketch[...] * plane_sketch[p, 1:2, :] for p in range(planes)]
    weights = mm(jnp.concatenate(scaled, axis=0), mixing[...])
    copies[3].wait()
    wide = mm_tn(field[...].reshape(planes * rows, cells), weights)
    own = blocks.shape[2]
    for n in range(2 * gx * ay):
        blocks[n // (gx * ay), n % (gx * ay)] = wide[n * own : n * own + own, :]
    core = place()[2]
    blank = jnp.zeros((gx * ay, kept.shape[1] - own, kept.shape[2]), jnp.float32)
    for half, out in ((core, kept), (1 - core, given)):
        out[:, 0:own, :] = blocks[half]
        out[:, own:, :] = blank


def second_sketch_kernel(own, field, plane_sketch, third_sketch, mixing, out):
    planes, rows, cells = field.shape
    across = None
    for p in range(planes):
        term = mm(field[p], third_sketch[...] * plane_sketch[p, 0:1, :])
        across = term if across is None else across + term
    second = mm(across, mixing[0])
    strip = out.shape[1] - own
    for n in range(out.shape[0]):
        out[n, 0:own, :] = jnp.zeros((own, out.shape[2]), jnp.float32)
        out[n, own:, :] = second[n * strip : n * strip + strip, :]


def total_kernel(gx, ay, own, received, out):
    strip = received.shape[1] - own
    third = received[0, 0:own, :]
    for n in range(1, gx * ay):
        third = third + received[n, 0:own, :]
    seconds = []
    for y in range(ay):
        second = received[y, own:, :]
        for g in range(1, gx):
            second = second + received[g * ay + y, own:, :]
        seconds.append(second)
    for n in range(gx * ay):
        out[n, 0:own, :] = third
        for y in range(ay):
            out[n, own + y * strip : own + (y + 1) * strip, :] = seconds[y]


def core_ranges(gx, ay, own, ranges):
    strip = (ranges.shape[1] - own) // ay
    return [
        jnp.concatenate(
            [ranges[n, own + y * strip : own + (y + 1) * strip, :] for n in range(gx * ay)], axis=0
        )
        for y in range(ay)
    ]


def own_first(quarters):
    at = place()
    return jnp.concatenate(
        [
            jnp.where(at[1] == 0, quarters[0], quarters[1]),
            jnp.where(at[1] == 0, quarters[1], quarters[0]),
        ],
        axis=0,
    )


def same_core_kernel(gx, ay, own, ranges, near_field, far_field, product, gram):
    quarters = core_ranges(gx, ay, own, ranges)
    both = jnp.concatenate(quarters, axis=0)
    gram[...] = mm_tn(both, both)
    turned = jnp.transpose(own_first(quarters))
    cells = near_field.shape[2]
    for p in range(near_field.shape[0]):
        field = jnp.concatenate([near_field[p], far_field[p]], axis=0)
        product[:, p * cells : p * cells + cells] = mm(turned, field)


def second_kernel(
    gx, ay, ac, same, other, near_field, far_field, product, same_gram, factor, partial, third
):
    at = place()
    planes, rows, cells = near_field.shape
    own = cells // (gx * ay * ac)
    rank = same.shape[2]
    quarters = core_ranges(gx, ay, own, other)
    both = jnp.concatenate(quarters, axis=0)
    gram = same_gram[...] + mm_tn(both, both)
    for swapped, ranges in enumerate((same, other)):
        for n in range(gx * ay):
            third[(at[2] ^ swapped) * (gx * ay) + n] = ranges[n, 0:own, :]
    all_third = jnp.concatenate([third[n] for n in range(gx * ay * ac)], axis=0)
    turned = jnp.transpose(own_first(quarters))
    halves = [[None, None] for _ in range(planes)]
    raw = [None] * planes
    width = cells // 2

    def field_product(p, h):
        span = slice(h * width, h * width + width)
        field = jnp.concatenate([near_field[p, :, span], far_field[p, :, span]], axis=0)
        held = product[:, p * cells + h * width : p * cells + h * width + width]
        halves[p][h] = held + mm(turned, field)

    def range_product(p):
        raw[p] = mm(jnp.concatenate(halves[p], axis=1), all_third)

    tasks = [functools.partial(field_product, p, h) for p in range(planes) for h in range(2)]
    tasks += [functools.partial(range_product, p) for p in range(planes)]
    inverse = inverse_lower(gram, tasks)
    mine = core_ranges(gx, ay, own, same)
    mine = jnp.where(at[1] == 0, mine[0], mine[1]).reshape(gx, own, rank)
    own_range = mine[0]
    for g in range(1, gx):
        own_range = jnp.where(at[0] == g, mine[g], own_range)
    factor[...] = mm_nt(own_range, inverse)
    share = rank // (ay * ac)
    own_rows = inverse[0:share, :]
    for a in range(1, ay * ac):
        piece = inverse[a * share : a * share + share, :]
        own_rows = jnp.where(at[1] * ac + at[2] == a, piece, own_rows)
    value = mm(own_rows, jnp.concatenate(raw, axis=1))
    for p in range(planes):
        for g in range(gx):
            partial[g, p] = value[:, p * rank : p * rank + rank]


def third_kernel(gx, ay, ac, own, targets, signs, same, other, factor, turned, weights, third):
    at = place()
    for swapped, ranges in enumerate((same, other)):
        for n in range(gx * ay):
            third[(at[2] ^ swapped) * (gx * ay) + n] = ranges[n, 0:own, :]
    all_third = jnp.concatenate([third[n] for n in range(gx * ay * ac)], axis=0)
    inverse = inverse_lower(mm_tn(all_third, all_third))
    turned[...] = jnp.transpose(inverse)
    factor[...] = mm_nt(third[(at[0] * ay + at[1]) * ac + at[2]], inverse)
    out_rows, turns, rank = weights.shape
    for r in range(out_rows):
        row = at[0] * out_rows + r
        for m in range(turns):
            plane = m * BLOCK + lax.rem(row, BLOCK)
            weight = jnp.float32(0)
            for t in range(targets.shape[1]):
                sign = (2 * signs[plane, t] - 1).astype(jnp.float32)
                weight = weight + jnp.where(targets[plane, t] == lax.div(row, BLOCK), sign, 0.0)
            weights[r, m : m + 1, :] = jnp.full((1, rank), weight, jnp.float32)


def core_kernel(weights, turned, planes, out):
    out_rows, turns, rank = weights.shape
    share = planes.shape[1]
    first = place()[0] * out_rows
    rows = []
    for r in range(out_rows):
        slot = r % BLOCK if out_rows % BLOCK == 0 else lax.rem(first + r, BLOCK)
        terms = [weights[r, m : m + 1, :] * planes[m * BLOCK + slot] for m in range(turns)]
        rows.append(sum(terms[1:], terms[0]))
    whole = mm(jnp.concatenate(rows, axis=0), turned[...])
    for r in range(out_rows):
        out[r] = whole[r * share : r * share + share, :]


def call(kernel, out_shapes, in_specs, flops, scratch=(), mib=48):
    return pl.pallas_call(
        kernel,
        out_shape=out_shapes,
        in_specs=in_specs,
        out_specs=jax.tree.map(lambda _: VMEM, out_shapes),
        scratch_shapes=scratch,
        compiler_params=pltpu.CompilerParams(vmem_limit_bytes=int(mib * 2**20)),
        cost_estimate=pl.CostEstimate(flops=flops, bytes_accessed=2**20, transcendentals=0),
    )


def swap(block, axis):
    perm = [(n, n ^ 1) for n in range(lax.axis_size(axis))]
    return lax.ppermute(block, axis, perm)


def body(
    scalar_field, plane_sketch, second_sketch, third_sketch, mixing, plane_targets, plane_signs
):
    gx, ay, ac = lax.axis_size("gx"), lax.axis_size("ay"), lax.axis_size("ac")
    planes, rows, cells = scalar_field.shape
    rank = mixing.shape[2]
    own = cells // (gx * ay * ac)
    strip = rows // (gx * ay)
    share = rank // (ay * ac)
    f32 = functools.partial(jax.ShapeDtypeStruct, dtype=jnp.float32)

    slot = f32((gx * ay, own + strip, rank))
    kept, given = call(
        functools.partial(third_sketch_kernel, gx, ay),
        [slot, slot],
        [HBM] * 4,
        10**9,
        [
            pltpu.VMEM(scalar_field.shape, jnp.float32),
            pltpu.VMEM(plane_sketch.shape, jnp.float32),
            pltpu.VMEM(second_sketch.shape, jnp.float32),
            pltpu.VMEM(mixing.shape[1:], jnp.float32),
            pltpu.VMEM((ac, gx * ay, own, rank), jnp.float32),
            pltpu.SemaphoreType.DMA((4,)),
        ],
        62,
    )(scalar_field, plane_sketch, second_sketch, mixing)
    taken = swap(given, "ac")
    second = call(functools.partial(second_sketch_kernel, own), slot, [VMEM] * 4, 10**9)(
        scalar_field, plane_sketch, third_sketch, mixing
    )
    slots = kept + second + taken
    received = lax.all_to_all(slots, ("gx", "ay"), 0, 0, tiled=True)
    copies = call(
        functools.partial(total_kernel, gx, ay, own),
        f32((gx * ay, own + ay * strip, rank)),
        [VMEM],
        10**6,
    )(received)
    same = lax.all_to_all(copies, ("gx", "ay"), 0, 0, tiled=True)
    other = swap(same, "ac")
    across = swap(scalar_field, "ay")
    product, same_gram = call(
        functools.partial(same_core_kernel, gx, ay, own),
        [f32((rank, planes * cells)), f32((rank, rank))],
        [VMEM] * 3,
        10**9,
    )(same, scalar_field, across)
    factor_second, partial = call(
        functools.partial(second_kernel, gx, ay, ac),
        [f32((own, rank)), f32((gx, planes, share, rank))],
        [VMEM] * 6,
        2 * 10**9,
        [pltpu.VMEM((gx * ay * ac, own, rank), jnp.float32)],
    )(same, other, swap(scalar_field, "ac"), swap(across, "ac"), product, same_gram)
    every = lax.all_to_all(partial, "gx", 0, 0, tiled=True)
    out_rows = BLOCKS * BLOCK // gx
    factor_third, turned, weights = call(
        functools.partial(third_kernel, gx, ay, ac, own),
        [f32((own, rank)), f32((rank, rank)), f32((out_rows, gx * planes // BLOCK, rank))],
        [SMEM] * 2 + [VMEM] * 2,
        10**9,
        [pltpu.VMEM((gx * ay * ac, own, rank), jnp.float32)],
    )(plane_targets, plane_signs, same, other)
    core_sketch = call(core_kernel, f32((out_rows, share, rank)), [VMEM] * 3, 10**8)(
        weights, turned, every.reshape(gx * planes, share, rank)
    )
    return (factor_second, factor_third, core_sketch)


def solution(mesh):
    gx, af = mesh.devices.shape
    mesh = jax.sharding.Mesh(mesh.devices.reshape(gx, af // 2, 2), ("gx", "ay", "ac"))
    af = ("ay", "ac")
    in_specs = (P("gx", af, None), P("gx", None, None), P(af, None), P(), P(), P(), P())
    out_specs = (P(af + ("gx",), None), P(("gx",) + af, None), P("gx", af, None))
    return jax.shard_map(body, mesh=mesh, in_specs=in_specs, out_specs=out_specs, check_vma=False)
```

```python
import functools

import jax
import jax.numpy as jnp
from jax import lax
from jax.experimental import pallas as pl
from jax.experimental.pallas import tpu as pltpu
from jax.sharding import PartitionSpec as P

BLOCK = 16
BLOCKS = 8
SUB = 8

precise = lax.Precision.HIGHEST
VMEM = pl.BlockSpec(memory_space=pltpu.VMEM)
SMEM = pl.BlockSpec(memory_space=pltpu.SMEM)
HBM = pl.BlockSpec(memory_space=pltpu.HBM)


def dot(left, right, dims):
    return lax.dot_general(
        left, right, (dims, ((), ())), precision=precise, preferred_element_type=jnp.float32
    )


def mm(left, right):
    return dot(left, right, ((1,), (0,)))


def mm_tn(left, right):
    return dot(left, right, ((0,), (0,)))


def mm_nt(left, right):
    return dot(left, right, ((1,), (1,)))


def inverse_lower(gram, tasks=()):
    size = gram.shape[0]
    count = size // SUB
    tasks = list(tasks)
    sub_ids = lax.broadcasted_iota(jnp.int32, (SUB, size), 0)
    lane_ids = lax.broadcasted_iota(jnp.int32, (SUB, size), 1)
    rows = [gram[SUB * i : SUB * i + SUB, :] for i in range(count)]
    done = []

    def along_sub(tile, j):
        return jnp.broadcast_to(tile[j : j + 1, :], (SUB, size))

    def along_lanes(tile, block):
        return [
            jnp.broadcast_to(tile[:, SUB * block + c : SUB * block + c + 1], (SUB, size))
            for c in range(SUB)
        ]

    diag = along_lanes(rows[0], 0)
    pivot = along_sub(diag[0], 0)
    for k in range(count):
        inside = (lane_ids >= SUB * k) & (lane_ids < SUB * k + SUB)
        cols = {i: along_lanes(rows[i], k) for i in range(k + 1, count)}
        ahead = along_lanes(rows[k + 1], k + 1) if k + 1 < count else None
        identity = jnp.where(lane_ids == sub_ids + SUB * k, 1.0, 0.0)
        rows[k] = jnp.where(inside, identity, rows[k])
        for i in range(k + 1, count):
            rows[i] = jnp.where(inside, 0.0, rows[i])
        pivots = None
        for j in range(SUB):
            pivots = pivot if j == 0 else jnp.where(sub_ids == j, pivot, pivots)
            scale = 1.0 / pivot
            heads = {c: along_sub(diag[c], j) for c in range(j + 1, SUB)}
            row_head = along_sub(rows[k], j)
            if j < SUB - 1:
                pivot = along_sub(diag[j + 1], j + 1) - (heads[j + 1] * heads[j + 1]) * scale
            elif k + 1 < count:
                head = along_sub(cols[k + 1][j], 0)
                pivot = along_sub(ahead[0], 0) - (head * head) * scale
            if j < SUB - 1:
                below = jnp.where(sub_ids > j, diag[j], 0.0)
                diag[j + 1] = diag[j + 1] - (below * heads[j + 1]) * scale
                factor = below * scale
                for c in range(j + 2, SUB):
                    diag[c] = diag[c] - factor * heads[c]
                rows[k] = rows[k] - factor * row_head
            for i in range(k + 1, count):
                factor = cols[i][j] * scale
                if i == k + 1:
                    for c in range(SUB):
                        ahead[c] = ahead[c] - factor * along_sub(cols[i][j], c)
                for c in range(j + 1, SUB):
                    cols[i][c] = cols[i][c] - factor * heads[c]
                rows[i] = rows[i] - factor * row_head
        kept = jnp.where(lane_ids < SUB * k + SUB, rows[k], 0.0)
        done.append(kept * lax.rsqrt(pivots))
        diag = ahead
        for task in tasks[: -(-len(tasks) // (count - k))]:
            task()
        tasks = tasks[-(-len(tasks) // (count - k)) :]
    return jnp.concatenate(done, axis=0)


def place():
    return [lax.axis_index(axis) for axis in ("gx", "ay", "ac")]


def third_sketch_kernel(
    gx, ay, field_in, plane_in, second_in, mixing_in, kept, given, *scratch
):
    field, plane_sketch, second_sketch, mixing, blocks, arrived = scratch
    copies = [
        pltpu.make_async_copy(source, target, arrived.at[n])
        for n, (source, target) in enumerate(
            (
                (second_in, second_sketch),
                (plane_in, plane_sketch),
                (mixing_in.at[1], mixing),
                (field_in, field),
            )
        )
    ]
    for copy in copies:
        copy.start()
    for copy in copies[:3]:
        copy.wait()
    planes, rows, cells = field.shape
    scaled = [second_sketch[...] * plane_sketch[p, 1:2, :] for p in range(planes)]
    weights = mm(jnp.concatenate(scaled, axis=0), mixing[...])
    copies[3].wait()
    wide = mm_tn(field[...].reshape(planes * rows, cells), weights)
    own = blocks.shape[2]
    for n in range(2 * gx * ay):
        blocks[n // (gx * ay), n % (gx * ay)] = wide[n * own : n * own + own, :]
    core = place()[2]
    blank = jnp.zeros((gx * ay, kept.shape[1] - own, kept.shape[2]), jnp.float32)
    for half, out in ((core, kept), (1 - core, given)):
        out[:, 0:own, :] = blocks[half]
        out[:, own:, :] = blank


def second_sketch_kernel(
    own, ay, field, plane_sketch, third_sketch, mixing, out, kept_planes, given_planes
):
    planes, rows, cells = field.shape
    across = None
    for p in range(planes):
        term = mm(field[p], third_sketch[...] * plane_sketch[p, 0:1, :])
        across = term if across is None else across + term
    second = mm(across, mixing[0])
    strip = out.shape[1] - own
    for n in range(out.shape[0]):
        out[n, 0:own, :] = jnp.zeros((own, out.shape[2]), jnp.float32)
        out[n, own:, :] = second[n * strip : n * strip + strip, :]
    at = place()
    share = planes // ay
    kept_planes[...] = field[pl.ds(at[1] * share, share)]
    given_planes[...] = field[pl.ds((1 - at[1]) * share, share)]


def total_kernel(gx, ay, own, received, out):
    strip = received.shape[1] - own
    third = received[0, 0:own, :]
    for n in range(1, gx * ay):
        third = third + received[n, 0:own, :]
    seconds = []
    for y in range(ay):
        second = received[y, own:, :]
        for g in range(1, gx):
            second = second + received[g * ay + y, own:, :]
        seconds.append(second)
    for n in range(gx * ay):
        out[n, 0:own, :] = third
        for y in range(ay):
            out[n, own + y * strip : own + (y + 1) * strip, :] = seconds[y]


def core_ranges(gx, ay, own, ranges):
    strip = (ranges.shape[1] - own) // ay
    return [
        jnp.concatenate(
            [ranges[n, own + y * strip : own + (y + 1) * strip, :] for n in range(gx * ay)], axis=0
        )
        for y in range(ay)
    ]


def own_first(quarters):
    at = place()
    return jnp.concatenate(
        [
            jnp.where(at[1] == 0, quarters[0], quarters[1]),
            jnp.where(at[1] == 0, quarters[1], quarters[0]),
        ],
        axis=0,
    )


def same_core_kernel(gx, ay, own, ranges, near_field, far_field, product, gram):
    quarters = core_ranges(gx, ay, own, ranges)
    both = jnp.concatenate(quarters, axis=0)
    gram[...] = mm_tn(both, both)
    turned = jnp.transpose(own_first(quarters))
    cells = near_field.shape[2]
    for p in range(near_field.shape[0]):
        field = jnp.concatenate([near_field[p], far_field[p]], axis=0)
        product[:, p * cells : p * cells + cells] = mm(turned, field)


def second_kernel(
    gx, ay, ac, same, other, near_field, far_field, product, same_gram, factor, partial, third
):
    at = place()
    planes, rows, cells = near_field.shape
    own = cells // (gx * ay * ac)
    rank = same.shape[2]
    quarters = core_ranges(gx, ay, own, other)
    both = jnp.concatenate(quarters, axis=0)
    gram = same_gram[...] + mm_tn(both, both)
    for swapped, ranges in enumerate((same, other)):
        for n in range(gx * ay):
            third[(at[2] ^ swapped) * (gx * ay) + n] = ranges[n, 0:own, :]
    all_third = jnp.concatenate([third[n] for n in range(gx * ay * ac)], axis=0)
    turned = jnp.transpose(own_first(quarters))
    halves = [[None, None] for _ in range(planes)]
    raw = [None] * planes
    width = cells // 2

    def field_product(p, h):
        span = slice(h * width, h * width + width)
        field = jnp.concatenate([near_field[p, :, span], far_field[p, :, span]], axis=0)
        held = product[:, p * cells + h * width : p * cells + h * width + width]
        halves[p][h] = held + mm(turned, field)

    def range_product(p):
        raw[p] = mm(jnp.concatenate(halves[p], axis=1), all_third)

    tasks = [functools.partial(field_product, p, h) for p in range(planes) for h in range(2)]
    tasks += [functools.partial(range_product, p) for p in range(planes)]
    inverse = inverse_lower(gram, tasks)
    mine = core_ranges(gx, ay, own, same)
    mine = jnp.where(at[1] == 0, mine[0], mine[1]).reshape(gx, own, rank)
    own_range = mine[0]
    for g in range(1, gx):
        own_range = jnp.where(at[0] == g, mine[g], own_range)
    factor[...] = mm_nt(own_range, inverse)
    share = rank // (ay * ac)
    core_rows = [
        jnp.where(
            at[2] == 0,
            inverse[2 * y * share : (2 * y + 1) * share, :],
            inverse[(2 * y + 1) * share : (2 * y + 2) * share, :],
        )
        for y in range(ay)
    ]
    value = mm(jnp.concatenate(core_rows, axis=0), jnp.concatenate(raw, axis=1))
    for y in range(ay):
        for p in range(planes):
            piece = value[y * share : y * share + share, p * rank : p * rank + rank]
            for g in range(gx):
                partial[g * ay + y, p] = piece


def third_kernel(gx, ay, ac, own, targets, signs, same, other, factor, turned, weights, third):
    at = place()
    for swapped, ranges in enumerate((same, other)):
        for n in range(gx * ay):
            third[(at[2] ^ swapped) * (gx * ay) + n] = ranges[n, 0:own, :]
    all_third = jnp.concatenate([third[n] for n in range(gx * ay * ac)], axis=0)
    inverse = inverse_lower(mm_tn(all_third, all_third))
    turned[...] = jnp.transpose(inverse)
    factor[...] = mm_nt(third[(at[0] * ay + at[1]) * ac + at[2]], inverse)
    out_rows, turns, rank = weights.shape
    for r in range(out_rows):
        row = at[0] * out_rows + r
        for m in range(turns):
            plane = m * BLOCK + lax.rem(row, BLOCK)
            weight = jnp.float32(0)
            for t in range(targets.shape[1]):
                sign = (2 * signs[plane, t] - 1).astype(jnp.float32)
                weight = weight + jnp.where(targets[plane, t] == lax.div(row, BLOCK), sign, 0.0)
            weights[r, m : m + 1, :] = jnp.full((1, rank), weight, jnp.float32)


def core_kernel(weights, turned, planes, out):
    out_rows, turns, rank = weights.shape
    share = planes.shape[1]
    first = place()[0] * out_rows
    rows = []
    for r in range(out_rows):
        slot = r % BLOCK if out_rows % BLOCK == 0 else lax.rem(first + r, BLOCK)
        terms = [weights[r, m : m + 1, :] * planes[m * BLOCK + slot] for m in range(turns)]
        rows.append(sum(terms[1:], terms[0]))
    whole = mm(jnp.concatenate(rows, axis=0), turned[...])
    for r in range(out_rows):
        out[r] = whole[r * share : r * share + share, :]


def call(kernel, out_shapes, in_specs, flops, scratch=(), mib=48):
    return pl.pallas_call(
        kernel,
        out_shape=out_shapes,
        in_specs=in_specs,
        out_specs=jax.tree.map(lambda _: VMEM, out_shapes),
        scratch_shapes=scratch,
        compiler_params=pltpu.CompilerParams(vmem_limit_bytes=int(mib * 2**20)),
        cost_estimate=pl.CostEstimate(flops=flops, bytes_accessed=2**20, transcendentals=0),
    )


def in_hbm(source):
    return pltpu.with_memory_space_constraint(source, pltpu.HBM)


def swap(block, axis):
    perm = [(n, n ^ 1) for n in range(lax.axis_size(axis))]
    return lax.ppermute(block, axis, perm)


def body(
    scalar_field, plane_sketch, second_sketch, third_sketch, mixing, plane_targets, plane_signs
):
    gx, ay, ac = lax.axis_size("gx"), lax.axis_size("ay"), lax.axis_size("ac")
    planes, rows, cells = scalar_field.shape
    rank = mixing.shape[2]
    own = cells // (gx * ay * ac)
    strip = rows // (gx * ay)
    share = rank // (ay * ac)
    f32 = functools.partial(jax.ShapeDtypeStruct, dtype=jnp.float32)

    slot = f32((gx * ay, own + strip, rank))
    kept, given = call(
        functools.partial(third_sketch_kernel, gx, ay),
        [slot, slot],
        [HBM] * 4,
        10**9,
        [
            pltpu.VMEM(scalar_field.shape, jnp.float32),
            pltpu.VMEM(plane_sketch.shape, jnp.float32),
            pltpu.VMEM(second_sketch.shape, jnp.float32),
            pltpu.VMEM(mixing.shape[1:], jnp.float32),
            pltpu.VMEM((ac, gx * ay, own, rank), jnp.float32),
            pltpu.SemaphoreType.DMA((4,)),
        ],
    )(*(in_hbm(source) for source in (scalar_field, plane_sketch, second_sketch, mixing)))
    taken = swap(given, "ac")
    plane_block = f32((planes // ay, rows, cells))
    second, kept_planes, given_planes = call(
        functools.partial(second_sketch_kernel, own, ay),
        [slot, plane_block, plane_block],
        [VMEM] * 4,
        10**9,
    )(scalar_field, plane_sketch, third_sketch, mixing)
    slots = kept + second + taken
    received = lax.all_to_all(slots, ("gx", "ay"), 0, 0, tiled=True)
    copies = call(
        functools.partial(total_kernel, gx, ay, own),
        f32((gx * ay, own + ay * strip, rank)),
        [VMEM],
        10**6,
    )(received)
    same = lax.all_to_all(copies, ("gx", "ay"), 0, 0, tiled=True)
    other = swap(same, "ac")
    across = swap(given_planes, "ay")
    product, same_gram = call(
        functools.partial(same_core_kernel, gx, ay, own),
        [f32((rank, planes // ay * cells)), f32((rank, rank))],
        [VMEM] * 3,
        10**9,
    )(same, kept_planes, across)
    factor_second, partial = call(
        functools.partial(second_kernel, gx, ay, ac),
        [f32((own, rank)), f32((gx * ay, planes // ay, share, rank))],
        [VMEM] * 6,
        2 * 10**9,
        [pltpu.VMEM((gx * ay * ac, own, rank), jnp.float32)],
    )(same, other, swap(kept_planes, "ac"), swap(across, "ac"), product, same_gram)
    every = lax.all_to_all(partial, ("gx", "ay"), 0, 0, tiled=True)
    out_rows = BLOCKS * BLOCK // gx
    factor_third, turned, weights = call(
        functools.partial(third_kernel, gx, ay, ac, own),
        [f32((own, rank)), f32((rank, rank)), f32((out_rows, gx * planes // BLOCK, rank))],
        [SMEM] * 2 + [VMEM] * 2,
        10**9,
        [pltpu.VMEM((gx * ay * ac, own, rank), jnp.float32)],
    )(plane_targets, plane_signs, same, other)
    core_sketch = call(core_kernel, f32((out_rows, share, rank)), [VMEM] * 3, 10**8)(
        weights, turned, every.reshape(gx * planes, share, rank)
    )
    return (factor_second, factor_third, core_sketch)


def solution(mesh):
    gx, af = mesh.devices.shape
    mesh = jax.sharding.Mesh(mesh.devices.reshape(gx, af // 2, 2), ("gx", "ay", "ac"))
    af = ("ay", "ac")
    in_specs = (P("gx", af, None), P("gx", None, None), P(af, None), P(), P(), P(), P())
    out_specs = (P(af + ("gx",), None), P(("gx",) + af, None), P("gx", af, None))
    return jax.shard_map(body, mesh=mesh, in_specs=in_specs, out_specs=out_specs, check_vma=False)
```

```python
import functools

import jax
import jax.numpy as jnp
from jax import lax
from jax.experimental import pallas as pl
from jax.experimental.pallas import tpu as pltpu
from jax.sharding import PartitionSpec as P

BLOCK = 16
BLOCKS = 8
SUB = 8

precise = lax.Precision.HIGHEST
VMEM = pl.BlockSpec(memory_space=pltpu.VMEM)
SMEM = pl.BlockSpec(memory_space=pltpu.SMEM)
HBM = pl.BlockSpec(memory_space=pltpu.HBM)


def dot(left, right, dims):
    return lax.dot_general(
        left, right, (dims, ((), ())), precision=precise, preferred_element_type=jnp.float32
    )


def mm(left, right):
    return dot(left, right, ((1,), (0,)))


def mm_tn(left, right):
    return dot(left, right, ((0,), (0,)))


def mm_nt(left, right):
    return dot(left, right, ((1,), (1,)))


def inverse_lower(gram, tasks=()):
    size = gram.shape[0]
    count = size // SUB
    tasks = list(tasks)
    sub_ids = lax.broadcasted_iota(jnp.int32, (SUB, size), 0)
    lane_ids = lax.broadcasted_iota(jnp.int32, (SUB, size), 1)
    rows = [gram[SUB * i : SUB * i + SUB, :] for i in range(count)]
    done = []

    def along_sub(tile, j):
        return jnp.broadcast_to(tile[j : j + 1, :], (SUB, size))

    def along_lanes(tile, block):
        return [
            jnp.broadcast_to(tile[:, SUB * block + c : SUB * block + c + 1], (SUB, size))
            for c in range(SUB)
        ]

    diag = along_lanes(rows[0], 0)
    pivot = along_sub(diag[0], 0)
    for k in range(count):
        inside = (lane_ids >= SUB * k) & (lane_ids < SUB * k + SUB)
        cols = {i: along_lanes(rows[i], k) for i in range(k + 1, count)}
        ahead = along_lanes(rows[k + 1], k + 1) if k + 1 < count else None
        identity = jnp.where(lane_ids == sub_ids + SUB * k, 1.0, 0.0)
        rows[k] = jnp.where(inside, identity, rows[k])
        for i in range(k + 1, count):
            rows[i] = jnp.where(inside, 0.0, rows[i])
        pivots = None
        for j in range(SUB):
            pivots = pivot if j == 0 else jnp.where(sub_ids == j, pivot, pivots)
            scale = 1.0 / pivot
            heads = {c: along_sub(diag[c], j) for c in range(j + 1, SUB)}
            row_head = along_sub(rows[k], j)
            if j < SUB - 1:
                pivot = along_sub(diag[j + 1], j + 1) - (heads[j + 1] * heads[j + 1]) * scale
            elif k + 1 < count:
                head = along_sub(cols[k + 1][j], 0)
                pivot = along_sub(ahead[0], 0) - (head * head) * scale
            if j < SUB - 1:
                below = jnp.where(sub_ids > j, diag[j], 0.0)
                diag[j + 1] = diag[j + 1] - (below * heads[j + 1]) * scale
                factor = below * scale
                for c in range(j + 2, SUB):
                    diag[c] = diag[c] - factor * heads[c]
                rows[k] = rows[k] - factor * row_head
            for i in range(k + 1, count):
                factor = cols[i][j] * scale
                if i == k + 1:
                    for c in range(SUB):
                        ahead[c] = ahead[c] - factor * along_sub(cols[i][j], c)
                for c in range(j + 1, SUB):
                    cols[i][c] = cols[i][c] - factor * heads[c]
                rows[i] = rows[i] - factor * row_head
        kept = jnp.where(lane_ids < SUB * k + SUB, rows[k], 0.0)
        done.append(kept * lax.rsqrt(pivots))
        diag = ahead
        for task in tasks[: -(-len(tasks) // (count - k))]:
            task()
        tasks = tasks[-(-len(tasks) // (count - k)) :]
    return jnp.concatenate(done, axis=0)


def place():
    return [lax.axis_index(axis) for axis in ("gx", "ay", "ac")]


def third_sketch_kernel(
    gx, ay, field_in, plane_in, second_in, mixing_in, kept, given, *scratch
):
    field, plane_sketch, second_sketch, mixing, blocks, arrived = scratch
    copies = [
        pltpu.make_async_copy(source, target, arrived.at[n])
        for n, (source, target) in enumerate(
            (
                (second_in, second_sketch),
                (plane_in, plane_sketch),
                (mixing_in.at[1], mixing),
                (field_in, field),
            )
        )
    ]
    for copy in copies:
        copy.start()
    for copy in copies[:3]:
        copy.wait()
    planes, rows, cells = field.shape
    scaled = [second_sketch[...] * plane_sketch[p, 1:2, :] for p in range(planes)]
    weights = mm(jnp.concatenate(scaled, axis=0), mixing[...])
    copies[3].wait()
    wide = mm_tn(field[...].reshape(planes * rows, cells), weights)
    own = blocks.shape[2]
    for n in range(2 * gx * ay):
        blocks[n // (gx * ay), n % (gx * ay)] = wide[n * own : n * own + own, :]
    core = place()[2]
    blank = jnp.zeros((gx * ay, kept.shape[1] - own, kept.shape[2]), jnp.float32)
    for half, out in ((core, kept), (1 - core, given)):
        out[:, 0:own, :] = blocks[half]
        out[:, own:, :] = blank


def second_sketch_kernel(
    own, ay, field, plane_sketch, third_sketch, mixing, out, kept_planes, given_planes
):
    planes, rows, cells = field.shape
    across = None
    for p in range(planes):
        term = mm(field[p], third_sketch[...] * plane_sketch[p, 0:1, :])
        across = term if across is None else across + term
    second = mm(across, mixing[0])
    strip = out.shape[1] - own
    for n in range(out.shape[0]):
        out[n, 0:own, :] = jnp.zeros((own, out.shape[2]), jnp.float32)
        out[n, own:, :] = second[n * strip : n * strip + strip, :]
    at = place()
    share = planes // ay
    kept_planes[...] = field[pl.ds(at[1] * share, share)]
    given_planes[...] = field[pl.ds((1 - at[1]) * share, share)]


def total_kernel(gx, ay, own, received, out):
    strip = received.shape[1] - own
    third = received[0, 0:own, :]
    for n in range(1, gx * ay):
        third = third + received[n, 0:own, :]
    seconds = []
    for y in range(ay):
        second = received[y, own:, :]
        for g in range(1, gx):
            second = second + received[g * ay + y, own:, :]
        seconds.append(second)
    for n in range(gx * ay):
        out[n, 0:own, :] = third
        for y in range(ay):
            out[n, own + y * strip : own + (y + 1) * strip, :] = seconds[y]


def core_ranges(gx, ay, own, ranges):
    strip = (ranges.shape[1] - own) // ay
    return [
        jnp.concatenate(
            [ranges[n, own + y * strip : own + (y + 1) * strip, :] for n in range(gx * ay)], axis=0
        )
        for y in range(ay)
    ]


def own_first(quarters):
    at = place()
    return jnp.concatenate(
        [
            jnp.where(at[1] == 0, quarters[0], quarters[1]),
            jnp.where(at[1] == 0, quarters[1], quarters[0]),
        ],
        axis=0,
    )


def same_core_kernel(gx, ay, own, ranges, near_field, far_field, product, gram):
    quarters = core_ranges(gx, ay, own, ranges)
    both = jnp.concatenate(quarters, axis=0)
    gram[...] = mm_tn(both, both)
    turned = jnp.transpose(own_first(quarters))
    cells = near_field.shape[2]
    for p in range(near_field.shape[0]):
        field = jnp.concatenate([near_field[p], far_field[p]], axis=0)
        product[:, p * cells : p * cells + cells] = mm(turned, field)


def second_kernel(
    gx, ay, ac, same, other, near_field, far_field, product, same_gram, factor, partial, third
):
    at = place()
    planes, rows, cells = near_field.shape
    own = cells // (gx * ay * ac)
    rank = same.shape[2]
    quarters = core_ranges(gx, ay, own, other)
    both = jnp.concatenate(quarters, axis=0)
    gram = same_gram[...] + mm_tn(both, both)
    for swapped, ranges in enumerate((same, other)):
        for n in range(gx * ay):
            third[(at[2] ^ swapped) * (gx * ay) + n] = ranges[n, 0:own, :]
    all_third = jnp.concatenate([third[n] for n in range(gx * ay * ac)], axis=0)
    turned = jnp.transpose(own_first(quarters))
    halves = [[None, None] for _ in range(planes)]
    raw = [None] * planes
    width = cells // 2

    def field_product(p, h):
        span = slice(h * width, h * width + width)
        field = jnp.concatenate([near_field[p, :, span], far_field[p, :, span]], axis=0)
        held = product[:, p * cells + h * width : p * cells + h * width + width]
        halves[p][h] = held + mm(turned, field)

    def range_product(p):
        raw[p] = mm(jnp.concatenate(halves[p], axis=1), all_third)

    tasks = [functools.partial(field_product, p, h) for p in range(planes) for h in range(2)]
    tasks += [functools.partial(range_product, p) for p in range(planes)]
    inverse = inverse_lower(gram, tasks)
    mine = core_ranges(gx, ay, own, same)
    mine = jnp.where(at[1] == 0, mine[0], mine[1]).reshape(gx, own, rank)
    own_range = mine[0]
    for g in range(1, gx):
        own_range = jnp.where(at[0] == g, mine[g], own_range)
    factor[...] = mm_nt(own_range, inverse)
    share = rank // (ay * ac)
    core_rows = [
        jnp.where(
            at[2] == 0,
            inverse[2 * y * share : (2 * y + 1) * share, :],
            inverse[(2 * y + 1) * share : (2 * y + 2) * share, :],
        )
        for y in range(ay)
    ]
    value = mm(jnp.concatenate(core_rows, axis=0), jnp.concatenate(raw, axis=1))
    for y in range(ay):
        for p in range(planes):
            piece = value[y * share : y * share + share, p * rank : p * rank + rank]
            for g in range(gx):
                partial[g * ay + y, p] = piece


def third_kernel(gx, ay, ac, own, targets, signs, same, other, factor, turned, weights, third):
    at = place()
    for swapped, ranges in enumerate((same, other)):
        for n in range(gx * ay):
            third[(at[2] ^ swapped) * (gx * ay) + n] = ranges[n, 0:own, :]
    all_third = jnp.concatenate([third[n] for n in range(gx * ay * ac)], axis=0)
    inverse = inverse_lower(mm_tn(all_third, all_third))
    turned[...] = jnp.transpose(inverse)
    factor[...] = mm_nt(third[(at[0] * ay + at[1]) * ac + at[2]], inverse)
    out_rows, turns, rank = weights.shape
    for r in range(out_rows):
        row = at[0] * out_rows + r
        for m in range(turns):
            plane = m * BLOCK + lax.rem(row, BLOCK)
            weight = jnp.float32(0)
            for t in range(targets.shape[1]):
                sign = (2 * signs[plane, t] - 1).astype(jnp.float32)
                weight = weight + jnp.where(targets[plane, t] == lax.div(row, BLOCK), sign, 0.0)
            weights[r, m : m + 1, :] = jnp.full((1, rank), weight, jnp.float32)


def core_kernel(weights, turned, planes, out):
    out_rows, turns, rank = weights.shape
    share = planes.shape[1]
    first = place()[0] * out_rows
    rows = []
    for r in range(out_rows):
        slot = r % BLOCK if out_rows % BLOCK == 0 else lax.rem(first + r, BLOCK)
        terms = [weights[r, m : m + 1, :] * planes[m * BLOCK + slot] for m in range(turns)]
        rows.append(sum(terms[1:], terms[0]))
    whole = mm(jnp.concatenate(rows, axis=0), turned[...])
    for r in range(out_rows):
        out[r] = whole[r * share : r * share + share, :]


def call(kernel, out_shapes, in_specs, flops, scratch=(), mib=48):
    return pl.pallas_call(
        kernel,
        out_shape=out_shapes,
        in_specs=in_specs,
        out_specs=jax.tree.map(lambda _: VMEM, out_shapes),
        scratch_shapes=scratch,
        compiler_params=pltpu.CompilerParams(vmem_limit_bytes=int(mib * 2**20)),
        cost_estimate=pl.CostEstimate(flops=flops, bytes_accessed=2**20, transcendentals=0),
    )


def in_hbm(source):
    return pltpu.with_memory_space_constraint(source, pltpu.HBM)


def swap(block, axis):
    perm = [(n, n ^ 1) for n in range(lax.axis_size(axis))]
    return lax.ppermute(block, axis, perm)


def body(
    scalar_field, plane_sketch, second_sketch, third_sketch, mixing, plane_targets, plane_signs
):
    gx, ay, ac = lax.axis_size("gx"), lax.axis_size("ay"), lax.axis_size("ac")
    planes, rows, cells = scalar_field.shape
    rank = mixing.shape[2]
    own = cells // (gx * ay * ac)
    strip = rows // (gx * ay)
    share = rank // (ay * ac)
    f32 = functools.partial(jax.ShapeDtypeStruct, dtype=jnp.float32)

    slot = f32((gx * ay, own + strip, rank))
    kept, given = call(
        functools.partial(third_sketch_kernel, gx, ay),
        [slot, slot],
        [HBM] * 4,
        10**9,
        [
            pltpu.VMEM(scalar_field.shape, jnp.float32),
            pltpu.VMEM(plane_sketch.shape, jnp.float32),
            pltpu.VMEM(second_sketch.shape, jnp.float32),
            pltpu.VMEM(mixing.shape[1:], jnp.float32),
            pltpu.VMEM((ac, gx * ay, own, rank), jnp.float32),
            pltpu.SemaphoreType.DMA((4,)),
        ],
    )(*(in_hbm(source) for source in (scalar_field, plane_sketch, second_sketch, mixing)))
    taken = swap(given, "ac")
    plane_block = f32((planes // ay, rows, cells))
    second, kept_planes, given_planes = call(
        functools.partial(second_sketch_kernel, own, ay),
        [slot, plane_block, plane_block],
        [VMEM] * 4,
        10**9,
    )(scalar_field, plane_sketch, third_sketch, mixing)
    slots = kept + second + taken
    received, across = lax.optimization_barrier(
        (lax.all_to_all(slots, ("gx", "ay"), 0, 0, tiled=True), swap(given_planes, "ay"))
    )
    copies = call(
        functools.partial(total_kernel, gx, ay, own),
        f32((gx * ay, own + ay * strip, rank)),
        [VMEM],
        10**6,
    )(received)
    same = lax.all_to_all(copies, ("gx", "ay"), 0, 0, tiled=True)
    other = swap(same, "ac")
    product, same_gram = call(
        functools.partial(same_core_kernel, gx, ay, own),
        [f32((rank, planes // ay * cells)), f32((rank, rank))],
        [VMEM] * 3,
        10**9,
    )(same, kept_planes, across)
    factor_second, partial = call(
        functools.partial(second_kernel, gx, ay, ac),
        [f32((own, rank)), f32((gx * ay, planes // ay, share, rank))],
        [VMEM] * 6,
        2 * 10**9,
        [pltpu.VMEM((gx * ay * ac, own, rank), jnp.float32)],
    )(same, other, swap(kept_planes, "ac"), swap(across, "ac"), product, same_gram)
    every = lax.all_to_all(partial, ("gx", "ay"), 0, 0, tiled=True)
    out_rows = BLOCKS * BLOCK // gx
    factor_third, turned, weights = call(
        functools.partial(third_kernel, gx, ay, ac, own),
        [f32((own, rank)), f32((rank, rank)), f32((out_rows, gx * planes // BLOCK, rank))],
        [SMEM] * 2 + [VMEM] * 2,
        10**9,
        [pltpu.VMEM((gx * ay * ac, own, rank), jnp.float32)],
    )(plane_targets, plane_signs, same, other)
    core_sketch = call(core_kernel, f32((out_rows, share, rank)), [VMEM] * 3, 10**8)(
        weights, turned, every.reshape(gx * planes, share, rank)
    )
    return (factor_second, factor_third, core_sketch)


def solution(mesh):
    gx, af = mesh.devices.shape
    mesh = jax.sharding.Mesh(mesh.devices.reshape(gx, af // 2, 2), ("gx", "ay", "ac"))
    af = ("ay", "ac")
    in_specs = (P("gx", af, None), P("gx", None, None), P(af, None), P(), P(), P(), P())
    out_specs = (P(af + ("gx",), None), P(("gx",) + af, None), P("gx", af, None))
    return jax.shard_map(body, mesh=mesh, in_specs=in_specs, out_specs=out_specs, check_vma=False)
```

```python
import functools

import jax
import jax.numpy as jnp
from jax import lax
from jax.experimental import pallas as pl
from jax.experimental.pallas import tpu as pltpu
from jax.sharding import PartitionSpec as P

BLOCK = 16
BLOCKS = 8
SUB = 8

precise = lax.Precision.HIGHEST
VMEM = pl.BlockSpec(memory_space=pltpu.VMEM)
SMEM = pl.BlockSpec(memory_space=pltpu.SMEM)
HBM = pl.BlockSpec(memory_space=pltpu.HBM)


def dot(left, right, dims):
    return lax.dot_general(
        left, right, (dims, ((), ())), precision=precise, preferred_element_type=jnp.float32
    )


def mm(left, right):
    return dot(left, right, ((1,), (0,)))


def mm_tn(left, right):
    return dot(left, right, ((0,), (0,)))


def mm_nt(left, right):
    return dot(left, right, ((1,), (1,)))


def inverse_lower(gram, tasks=()):
    size = gram.shape[0]
    count = size // SUB
    tasks = list(tasks)
    sub_ids = lax.broadcasted_iota(jnp.int32, (SUB, size), 0)
    lane_ids = lax.broadcasted_iota(jnp.int32, (SUB, size), 1)
    rows = [gram[SUB * i : SUB * i + SUB, :] for i in range(count)]
    done = []

    def along_sub(tile, j):
        return jnp.broadcast_to(tile[j : j + 1, :], (SUB, size))

    def along_lanes(tile, block):
        return [
            jnp.broadcast_to(tile[:, SUB * block + c : SUB * block + c + 1], (SUB, size))
            for c in range(SUB)
        ]

    diag = along_lanes(rows[0], 0)
    pivot = along_sub(diag[0], 0)
    for k in range(count):
        inside = (lane_ids >= SUB * k) & (lane_ids < SUB * k + SUB)
        cols = {i: along_lanes(rows[i], k) for i in range(k + 1, count)}
        ahead = along_lanes(rows[k + 1], k + 1) if k + 1 < count else None
        identity = jnp.where(lane_ids == sub_ids + SUB * k, 1.0, 0.0)
        rows[k] = jnp.where(inside, identity, rows[k])
        for i in range(k + 1, count):
            rows[i] = jnp.where(inside, 0.0, rows[i])
        pivots = None
        for j in range(SUB):
            pivots = pivot if j == 0 else jnp.where(sub_ids == j, pivot, pivots)
            scale = 1.0 / pivot
            heads = {c: along_sub(diag[c], j) for c in range(j + 1, SUB)}
            row_head = along_sub(rows[k], j)
            if j < SUB - 1:
                pivot = along_sub(diag[j + 1], j + 1) - (heads[j + 1] * heads[j + 1]) * scale
            elif k + 1 < count:
                head = along_sub(cols[k + 1][j], 0)
                pivot = along_sub(ahead[0], 0) - (head * head) * scale
            if j < SUB - 1:
                below = jnp.where(sub_ids > j, diag[j], 0.0)
                diag[j + 1] = diag[j + 1] - (below * heads[j + 1]) * scale
                factor = below * scale
                for c in range(j + 2, SUB):
                    diag[c] = diag[c] - factor * heads[c]
                rows[k] = rows[k] - factor * row_head
            for i in range(k + 1, count):
                factor = cols[i][j] * scale
                if i == k + 1:
                    for c in range(SUB):
                        ahead[c] = ahead[c] - factor * along_sub(cols[i][j], c)
                for c in range(j + 1, SUB):
                    cols[i][c] = cols[i][c] - factor * heads[c]
                rows[i] = rows[i] - factor * row_head
        kept = jnp.where(lane_ids < SUB * k + SUB, rows[k], 0.0)
        done.append(kept * lax.rsqrt(pivots))
        diag = ahead
        for task in tasks[: -(-len(tasks) // (count - k))]:
            task()
        tasks = tasks[-(-len(tasks) // (count - k)) :]
    return jnp.concatenate(done, axis=0)


def place():
    return [lax.axis_index(axis) for axis in ("gx", "ay", "ac")]


def third_sketch_kernel(
    gx, ay, field_in, plane_in, second_in, mixing_in, kept, given, *scratch
):
    field, plane_sketch, second_sketch, mixing, blocks, arrived = scratch
    copies = [
        pltpu.make_async_copy(source, target, arrived.at[n])
        for n, (source, target) in enumerate(
            (
                (plane_in, plane_sketch),
                (second_in, second_sketch),
                (mixing_in.at[1], mixing),
                (field_in, field),
            )
        )
    ]
    for copy in copies:
        copy.start()
    for copy in copies[:3]:
        copy.wait()
    planes, rows, cells = field.shape
    scaled = [second_sketch[...] * plane_sketch[p, 1:2, :] for p in range(planes)]
    weights = mm(jnp.concatenate(scaled, axis=0), mixing[...])
    copies[3].wait()
    wide = mm_tn(field[...].reshape(planes * rows, cells), weights)
    own = blocks.shape[2]
    for n in range(2 * gx * ay):
        blocks[n // (gx * ay), n % (gx * ay)] = wide[n * own : n * own + own, :]
    core = place()[2]
    blank = jnp.zeros((gx * ay, kept.shape[1] - own, kept.shape[2]), jnp.float32)
    for half, out in ((core, kept), (1 - core, given)):
        out[:, 0:own, :] = blocks[half]
        out[:, own:, :] = blank


def second_sketch_kernel(own, field, plane_sketch, third_sketch, mixing, out):
    planes, rows, cells = field.shape
    across = None
    for p in range(planes):
        term = mm(field[p], third_sketch[...] * plane_sketch[p, 0:1, :])
        across = term if across is None else across + term
    second = mm(across, mixing[0])
    strip = out.shape[1] - own
    for n in range(out.shape[0]):
        out[n, 0:own, :] = jnp.zeros((own, out.shape[2]), jnp.float32)
        out[n, own:, :] = second[n * strip : n * strip + strip, :]


def total_kernel(gx, ay, own, received, out):
    strip = received.shape[1] - own
    third = received[0, 0:own, :]
    for n in range(1, gx * ay):
        third = third + received[n, 0:own, :]
    seconds = []
    for y in range(ay):
        second = received[y, own:, :]
        for g in range(1, gx):
            second = second + received[g * ay + y, own:, :]
        seconds.append(second)
    for n in range(gx * ay):
        out[n, 0:own, :] = third
        for y in range(ay):
            out[n, own + y * strip : own + (y + 1) * strip, :] = seconds[y]


def core_ranges(gx, ay, own, ranges):
    strip = (ranges.shape[1] - own) // ay
    return [
        jnp.concatenate(
            [ranges[n, own + y * strip : own + (y + 1) * strip, :] for n in range(gx * ay)], axis=0
        )
        for y in range(ay)
    ]


def own_first(quarters):
    at = place()
    return jnp.concatenate(
        [
            jnp.where(at[1] == 0, quarters[0], quarters[1]),
            jnp.where(at[1] == 0, quarters[1], quarters[0]),
        ],
        axis=0,
    )


def same_core_kernel(gx, ay, own, ranges, near_field, far_field, product, gram):
    quarters = core_ranges(gx, ay, own, ranges)
    both = jnp.concatenate(quarters, axis=0)
    gram[...] = mm_tn(both, both)
    turned = jnp.transpose(own_first(quarters))
    cells = near_field.shape[2]
    for p in range(near_field.shape[0]):
        field = jnp.concatenate([near_field[p], far_field[p]], axis=0)
        product[:, p * cells : p * cells + cells] = mm(turned, field)


def second_kernel(
    gx, ay, ac, same, other, near_field, far_field, product, same_gram, inverse_out, partial, third
):
    at = place()
    planes, rows, cells = near_field.shape
    own = cells // (gx * ay * ac)
    rank = same.shape[2]
    quarters = core_ranges(gx, ay, own, other)
    both = jnp.concatenate(quarters, axis=0)
    gram = same_gram[...] + mm_tn(both, both)
    for swapped, ranges in enumerate((same, other)):
        for n in range(gx * ay):
            third[(at[2] ^ swapped) * (gx * ay) + n] = ranges[n, 0:own, :]
    all_third = jnp.concatenate([third[n] for n in range(gx * ay * ac)], axis=0)
    turned = jnp.transpose(own_first(quarters))
    halves = [[None, None] for _ in range(planes)]
    raw = [None] * planes
    width = cells // 2

    def field_product(p, h):
        span = slice(h * width, h * width + width)
        field = jnp.concatenate([near_field[p, :, span], far_field[p, :, span]], axis=0)
        held = product[:, p * cells + h * width : p * cells + h * width + width]
        halves[p][h] = held + mm(turned, field)

    def range_product(p):
        raw[p] = mm(jnp.concatenate(halves[p], axis=1), all_third)

    tasks = [functools.partial(field_product, p, h) for p in range(planes) for h in range(2)]
    tasks += [functools.partial(range_product, p) for p in range(planes)]
    inverse = inverse_lower(gram, tasks)
    inverse_out[...] = inverse
    share = rank // (ay * ac)
    own_rows = inverse[0:share, :]
    for a in range(1, ay * ac):
        piece = inverse[a * share : a * share + share, :]
        own_rows = jnp.where(at[1] * ac + at[2] == a, piece, own_rows)
    value = mm(own_rows, jnp.concatenate(raw, axis=1))
    for p in range(planes):
        for g in range(gx):
            partial[g, p] = value[:, p * rank : p * rank + rank]


def third_kernel(
    gx, ay, ac, own, targets, signs, same, other, second_inverse, *refs
):
    factor_second, factor_third, turned, weights, third = refs
    at = place()
    rank = same.shape[2]
    mine = core_ranges(gx, ay, own, same)
    mine = jnp.where(at[1] == 0, mine[0], mine[1]).reshape(gx, own, rank)
    own_range = mine[0]
    for g in range(1, gx):
        own_range = jnp.where(at[0] == g, mine[g], own_range)
    factor_second[...] = mm_nt(own_range, second_inverse[...])
    for swapped, ranges in enumerate((same, other)):
        for n in range(gx * ay):
            third[(at[2] ^ swapped) * (gx * ay) + n] = ranges[n, 0:own, :]
    all_third = jnp.concatenate([third[n] for n in range(gx * ay * ac)], axis=0)
    inverse = inverse_lower(mm_tn(all_third, all_third))
    turned[...] = jnp.transpose(inverse)
    factor_third[...] = mm_nt(third[(at[0] * ay + at[1]) * ac + at[2]], inverse)
    out_rows, turns, rank = weights.shape
    for r in range(out_rows):
        row = at[0] * out_rows + r
        for m in range(turns):
            plane = m * BLOCK + lax.rem(row, BLOCK)
            weight = jnp.float32(0)
            for t in range(targets.shape[1]):
                sign = (2 * signs[plane, t] - 1).astype(jnp.float32)
                weight = weight + jnp.where(targets[plane, t] == lax.div(row, BLOCK), sign, 0.0)
            weights[r, m : m + 1, :] = jnp.full((1, rank), weight, jnp.float32)


def core_kernel(weights, turned, planes, out):
    out_rows, turns, rank = weights.shape
    share = planes.shape[1]
    first = place()[0] * out_rows
    rows = []
    for r in range(out_rows):
        slot = r % BLOCK if out_rows % BLOCK == 0 else lax.rem(first + r, BLOCK)
        terms = [weights[r, m : m + 1, :] * planes[m * BLOCK + slot] for m in range(turns)]
        rows.append(sum(terms[1:], terms[0]))
    whole = mm(jnp.concatenate(rows, axis=0), turned[...])
    for r in range(out_rows):
        out[r] = whole[r * share : r * share + share, :]


def call(kernel, out_shapes, in_specs, flops, scratch=(), mib=48):
    return pl.pallas_call(
        kernel,
        out_shape=out_shapes,
        in_specs=in_specs,
        out_specs=jax.tree.map(lambda _: VMEM, out_shapes),
        scratch_shapes=scratch,
        compiler_params=pltpu.CompilerParams(vmem_limit_bytes=int(mib * 2**20)),
        cost_estimate=pl.CostEstimate(flops=flops, bytes_accessed=2**20, transcendentals=0),
    )


def in_hbm(source):
    return pltpu.with_memory_space_constraint(source, pltpu.HBM)


def swap(block, axis):
    perm = [(n, n ^ 1) for n in range(lax.axis_size(axis))]
    return lax.ppermute(block, axis, perm)


def body(
    scalar_field, plane_sketch, second_sketch, third_sketch, mixing, plane_targets, plane_signs
):
    gx, ay, ac = lax.axis_size("gx"), lax.axis_size("ay"), lax.axis_size("ac")
    planes, rows, cells = scalar_field.shape
    rank = mixing.shape[2]
    own = cells // (gx * ay * ac)
    strip = rows // (gx * ay)
    share = rank // (ay * ac)
    f32 = functools.partial(jax.ShapeDtypeStruct, dtype=jnp.float32)

    slot = f32((gx * ay, own + strip, rank))
    kept, given = call(
        functools.partial(third_sketch_kernel, gx, ay),
        [slot, slot],
        [HBM] * 4,
        10**9,
        [
            pltpu.VMEM(scalar_field.shape, jnp.float32),
            pltpu.VMEM(plane_sketch.shape, jnp.float32),
            pltpu.VMEM(second_sketch.shape, jnp.float32),
            pltpu.VMEM(mixing.shape[1:], jnp.float32),
            pltpu.VMEM((ac, gx * ay, own, rank), jnp.float32),
            pltpu.SemaphoreType.DMA((4,)),
        ],
    )(*(in_hbm(source) for source in (scalar_field, plane_sketch, second_sketch, mixing)))
    taken = swap(given, "ac")
    second = call(functools.partial(second_sketch_kernel, own), slot, [VMEM] * 4, 10**9)(
        scalar_field, plane_sketch, third_sketch, mixing
    )
    slots = kept + second + taken
    received = lax.all_to_all(slots, ("gx", "ay"), 0, 0, tiled=True)
    copies = call(
        functools.partial(total_kernel, gx, ay, own),
        f32((gx * ay, own + ay * strip, rank)),
        [VMEM],
        10**6,
    )(received)
    same = lax.all_to_all(copies, ("gx", "ay"), 0, 0, tiled=True)
    other = swap(same, "ac")
    across = swap(scalar_field, "ay")
    product, same_gram = call(
        functools.partial(same_core_kernel, gx, ay, own),
        [f32((rank, planes * cells)), f32((rank, rank))],
        [VMEM] * 3,
        10**9,
    )(same, scalar_field, across)
    second_inverse, partial = call(
        functools.partial(second_kernel, gx, ay, ac),
        [f32((rank, rank)), f32((gx, planes, share, rank))],
        [VMEM] * 6,
        2 * 10**9,
        [pltpu.VMEM((gx * ay * ac, own, rank), jnp.float32)],
    )(same, other, swap(scalar_field, "ac"), swap(across, "ac"), product, same_gram)
    every = lax.all_to_all(partial, "gx", 0, 0, tiled=True)
    out_rows = BLOCKS * BLOCK // gx
    factor_second, factor_third, turned, weights = call(
        functools.partial(third_kernel, gx, ay, ac, own),
        [
            f32((own, rank)),
            f32((own, rank)),
            f32((rank, rank)),
            f32((out_rows, gx * planes // BLOCK, rank)),
        ],
        [SMEM] * 2 + [VMEM] * 3,
        10**9,
        [pltpu.VMEM((gx * ay * ac, own, rank), jnp.float32)],
    )(plane_targets, plane_signs, same, other, second_inverse)
    core_sketch = call(core_kernel, f32((out_rows, share, rank)), [VMEM] * 3, 10**8)(
        weights, turned, every.reshape(gx * planes, share, rank)
    )
    return (factor_second, factor_third, core_sketch)


def solution(mesh):
    gx, af = mesh.devices.shape
    mesh = jax.sharding.Mesh(mesh.devices.reshape(gx, af // 2, 2), ("gx", "ay", "ac"))
    af = ("ay", "ac")
    in_specs = (P("gx", af, None), P("gx", None, None), P(af, None), P(), P(), P(), P())
    out_specs = (P(af + ("gx",), None), P(("gx",) + af, None), P("gx", af, None))
    return jax.shard_map(body, mesh=mesh, in_specs=in_specs, out_specs=out_specs, check_vma=False)
```

```python
import functools

import jax
import jax.numpy as jnp
from jax import lax
from jax.experimental import pallas as pl
from jax.experimental.pallas import tpu as pltpu
from jax.sharding import PartitionSpec as P

BLOCK = 16
BLOCKS = 8
SUB = 8

precise = lax.Precision.HIGHEST
VMEM = pl.BlockSpec(memory_space=pltpu.VMEM)
SMEM = pl.BlockSpec(memory_space=pltpu.SMEM)
HBM = pl.BlockSpec(memory_space=pltpu.HBM)


def dot(left, right, dims):
    return lax.dot_general(
        left, right, (dims, ((), ())), precision=precise, preferred_element_type=jnp.float32
    )


def mm(left, right):
    return dot(left, right, ((1,), (0,)))


def mm_tn(left, right):
    return dot(left, right, ((0,), (0,)))


def mm_nt(left, right):
    return dot(left, right, ((1,), (1,)))


def inverse_lower(gram, tasks=()):
    size = gram.shape[0]
    count = size // SUB
    tasks = list(tasks)
    sub_ids = lax.broadcasted_iota(jnp.int32, (SUB, size), 0)
    lane_ids = lax.broadcasted_iota(jnp.int32, (SUB, size), 1)
    rows = [gram[SUB * i : SUB * i + SUB, :] for i in range(count)]
    done = []

    def along_sub(tile, j):
        return jnp.broadcast_to(tile[j : j + 1, :], (SUB, size))

    def along_lanes(tile, block):
        return [
            jnp.broadcast_to(tile[:, SUB * block + c : SUB * block + c + 1], (SUB, size))
            for c in range(SUB)
        ]

    diag = along_lanes(rows[0], 0)
    pivot = along_sub(diag[0], 0)
    for k in range(count):
        inside = (lane_ids >= SUB * k) & (lane_ids < SUB * k + SUB)
        cols = {i: along_lanes(rows[i], k) for i in range(k + 1, count)}
        ahead = along_lanes(rows[k + 1], k + 1) if k + 1 < count else None
        identity = jnp.where(lane_ids == sub_ids + SUB * k, 1.0, 0.0)
        rows[k] = jnp.where(inside, identity, rows[k])
        for i in range(k + 1, count):
            rows[i] = jnp.where(inside, 0.0, rows[i])
        pivots = None
        for j in range(SUB):
            pivots = pivot if j == 0 else jnp.where(sub_ids == j, pivot, pivots)
            scale = 1.0 / pivot
            heads = {c: along_sub(diag[c], j) for c in range(j + 1, SUB)}
            row_head = along_sub(rows[k], j)
            if j < SUB - 1:
                pivot = along_sub(diag[j + 1], j + 1) - (heads[j + 1] * heads[j + 1]) * scale
            elif k + 1 < count:
                head = along_sub(cols[k + 1][j], 0)
                pivot = along_sub(ahead[0], 0) - (head * head) * scale
            if j < SUB - 1:
                below = jnp.where(sub_ids > j, diag[j], 0.0)
                diag[j + 1] = diag[j + 1] - (below * heads[j + 1]) * scale
                factor = below * scale
                for c in range(j + 2, SUB):
                    diag[c] = diag[c] - factor * heads[c]
                rows[k] = rows[k] - factor * row_head
            for i in range(k + 1, count):
                factor = cols[i][j] * scale
                if i == k + 1:
                    for c in range(SUB):
                        ahead[c] = ahead[c] - factor * along_sub(cols[i][j], c)
                for c in range(j + 1, SUB):
                    cols[i][c] = cols[i][c] - factor * heads[c]
                rows[i] = rows[i] - factor * row_head
        kept = jnp.where(lane_ids < SUB * k + SUB, rows[k], 0.0)
        done.append(kept * lax.rsqrt(pivots))
        diag = ahead
        for task in tasks[: -(-len(tasks) // (count - k))]:
            task()
        tasks = tasks[-(-len(tasks) // (count - k)) :]
    return jnp.concatenate(done, axis=0)


def place():
    return [lax.axis_index(axis) for axis in ("gx", "ay", "ac")]


def third_sketch_kernel(
    gx, ay, field_in, plane_in, second_in, mixing_in, kept, given, *scratch
):
    field, plane_sketch, second_sketch, mixing, blocks, arrived = scratch
    copies = [
        pltpu.make_async_copy(source, target, arrived.at[n])
        for n, (source, target) in enumerate(
            (
                (plane_in, plane_sketch),
                (second_in, second_sketch),
                (mixing_in.at[1], mixing),
                (field_in, field),
            )
        )
    ]
    for copy in copies:
        copy.start()
    for copy in copies[:3]:
        copy.wait()
    planes, rows, cells = field.shape
    scaled = [second_sketch[...] * plane_sketch[p, 1:2, :] for p in range(planes)]
    weights = mm(jnp.concatenate(scaled, axis=0), mixing[...])
    copies[3].wait()
    wide = mm_tn(field[...].reshape(planes * rows, cells), weights)
    own = blocks.shape[2]
    for n in range(2 * gx * ay):
        blocks[n // (gx * ay), n % (gx * ay)] = wide[n * own : n * own + own, :]
    core = place()[2]
    blank = jnp.zeros((gx * ay, kept.shape[1] - own, kept.shape[2]), jnp.float32)
    for half, out in ((core, kept), (1 - core, given)):
        out[:, 0:own, :] = blocks[half]
        out[:, own:, :] = blank


def second_sketch_kernel(own, field, plane_sketch, third_sketch, mixing, out):
    planes, rows, cells = field.shape
    across = None
    for p in range(planes):
        term = mm(field[p], third_sketch[...] * plane_sketch[p, 0:1, :])
        across = term if across is None else across + term
    second = mm(across, mixing[0])
    strip = out.shape[1] - own
    for n in range(out.shape[0]):
        out[n, 0:own, :] = jnp.zeros((own, out.shape[2]), jnp.float32)
        out[n, own:, :] = second[n * strip : n * strip + strip, :]


def slots_kernel(kept, second, taken, out):
    out[...] = kept[...] + taken[...] + second[...]


def total_kernel(gx, ay, own, received, out):
    strip = received.shape[1] - own
    third = received[0, 0:own, :]
    for n in range(1, gx * ay):
        third = third + received[n, 0:own, :]
    seconds = []
    for y in range(ay):
        second = received[y, own:, :]
        for g in range(1, gx):
            second = second + received[g * ay + y, own:, :]
        seconds.append(second)
    for n in range(gx * ay):
        out[n, 0:own, :] = third
        for y in range(ay):
            out[n, own + y * strip : own + (y + 1) * strip, :] = seconds[y]


def core_ranges(gx, ay, own, ranges):
    strip = (ranges.shape[1] - own) // ay
    return [
        jnp.concatenate(
            [ranges[n, own + y * strip : own + (y + 1) * strip, :] for n in range(gx * ay)], axis=0
        )
        for y in range(ay)
    ]


def own_first(quarters):
    at = place()
    return jnp.concatenate(
        [
            jnp.where(at[1] == 0, quarters[0], quarters[1]),
            jnp.where(at[1] == 0, quarters[1], quarters[0]),
        ],
        axis=0,
    )


def same_core_kernel(gx, ay, own, ranges, near_field, far_field, product, gram):
    quarters = core_ranges(gx, ay, own, ranges)
    both = jnp.concatenate(quarters, axis=0)
    gram[...] = mm_tn(both, both)
    turned = jnp.transpose(own_first(quarters))
    cells = near_field.shape[2]
    for p in range(near_field.shape[0]):
        field = jnp.concatenate([near_field[p], far_field[p]], axis=0)
        product[:, p * cells : p * cells + cells] = mm(turned, field)


def second_kernel(
    gx, ay, ac, same, other, near_field, far_field, product, same_gram, inverse_out, partial, third
):
    at = place()
    planes, rows, cells = near_field.shape
    own = cells // (gx * ay * ac)
    rank = same.shape[2]
    quarters = core_ranges(gx, ay, own, other)
    both = jnp.concatenate(quarters, axis=0)
    gram = same_gram[...] + mm_tn(both, both)
    for swapped, ranges in enumerate((same, other)):
        for n in range(gx * ay):
            third[(at[2] ^ swapped) * (gx * ay) + n] = ranges[n, 0:own, :]
    all_third = jnp.concatenate([third[n] for n in range(gx * ay * ac)], axis=0)
    turned = jnp.transpose(own_first(quarters))
    halves = [[None, None] for _ in range(planes)]
    raw = [None] * planes
    width = cells // 2

    def field_product(p, h):
        span = slice(h * width, h * width + width)
        field = jnp.concatenate([near_field[p, :, span], far_field[p, :, span]], axis=0)
        held = product[:, p * cells + h * width : p * cells + h * width + width]
        halves[p][h] = held + mm(turned, field)

    def range_product(p):
        raw[p] = mm(jnp.concatenate(halves[p], axis=1), all_third)

    tasks = [functools.partial(field_product, p, h) for p in range(planes) for h in range(2)]
    tasks += [functools.partial(range_product, p) for p in range(planes)]
    inverse = inverse_lower(gram, tasks)
    inverse_out[...] = inverse
    share = rank // (ay * ac)
    own_rows = inverse[0:share, :]
    for a in range(1, ay * ac):
        piece = inverse[a * share : a * share + share, :]
        own_rows = jnp.where(at[1] * ac + at[2] == a, piece, own_rows)
    value = mm(own_rows, jnp.concatenate(raw, axis=1))
    for p in range(planes):
        for g in range(gx):
            partial[g, p] = value[:, p * rank : p * rank + rank]


def third_kernel(
    gx, ay, ac, own, targets, signs, same, other, second_inverse, *refs
):
    factor_second, factor_third, turned, weights, third = refs
    at = place()
    rank = same.shape[2]
    mine = core_ranges(gx, ay, own, same)
    mine = jnp.where(at[1] == 0, mine[0], mine[1]).reshape(gx, own, rank)
    own_range = mine[0]
    for g in range(1, gx):
        own_range = jnp.where(at[0] == g, mine[g], own_range)
    factor_second[...] = mm_nt(own_range, second_inverse[...])
    for swapped, ranges in enumerate((same, other)):
        for n in range(gx * ay):
            third[(at[2] ^ swapped) * (gx * ay) + n] = ranges[n, 0:own, :]
    all_third = jnp.concatenate([third[n] for n in range(gx * ay * ac)], axis=0)
    inverse = inverse_lower(mm_tn(all_third, all_third))
    turned[...] = jnp.transpose(inverse)
    factor_third[...] = mm_nt(third[(at[0] * ay + at[1]) * ac + at[2]], inverse)
    out_rows, turns, rank = weights.shape
    for r in range(out_rows):
        row = at[0] * out_rows + r
        for m in range(turns):
            plane = m * BLOCK + lax.rem(row, BLOCK)
            weight = jnp.float32(0)
            for t in range(targets.shape[1]):
                sign = (2 * signs[plane, t] - 1).astype(jnp.float32)
                weight = weight + jnp.where(targets[plane, t] == lax.div(row, BLOCK), sign, 0.0)
            weights[r, m : m + 1, :] = jnp.full((1, rank), weight, jnp.float32)


def core_kernel(weights, turned, planes, out):
    out_rows, turns, rank = weights.shape
    share = planes.shape[1]
    first = place()[0] * out_rows
    rows = []
    for r in range(out_rows):
        slot = r % BLOCK if out_rows % BLOCK == 0 else lax.rem(first + r, BLOCK)
        terms = [weights[r, m : m + 1, :] * planes[m * BLOCK + slot] for m in range(turns)]
        rows.append(sum(terms[1:], terms[0]))
    whole = mm(jnp.concatenate(rows, axis=0), turned[...])
    for r in range(out_rows):
        out[r] = whole[r * share : r * share + share, :]


def call(kernel, out_shapes, in_specs, flops, scratch=(), mib=48):
    return pl.pallas_call(
        kernel,
        out_shape=out_shapes,
        in_specs=in_specs,
        out_specs=jax.tree.map(lambda _: VMEM, out_shapes),
        scratch_shapes=scratch,
        compiler_params=pltpu.CompilerParams(vmem_limit_bytes=int(mib * 2**20)),
        cost_estimate=pl.CostEstimate(flops=flops, bytes_accessed=2**20, transcendentals=0),
    )


def in_hbm(source):
    return pltpu.with_memory_space_constraint(source, pltpu.HBM)


def swap(block, axis):
    perm = [(n, n ^ 1) for n in range(lax.axis_size(axis))]
    return lax.ppermute(block, axis, perm)


def body(
    scalar_field, plane_sketch, second_sketch, third_sketch, mixing, plane_targets, plane_signs
):
    gx, ay, ac = lax.axis_size("gx"), lax.axis_size("ay"), lax.axis_size("ac")
    planes, rows, cells = scalar_field.shape
    rank = mixing.shape[2]
    own = cells // (gx * ay * ac)
    strip = rows // (gx * ay)
    share = rank // (ay * ac)
    f32 = functools.partial(jax.ShapeDtypeStruct, dtype=jnp.float32)
    vmem32 = functools.partial(pltpu.VMEM, dtype=jnp.float32)

    slot = f32((gx * ay, own + strip, rank))
    kept, given = call(
        functools.partial(third_sketch_kernel, gx, ay),
        [slot, slot],
        [HBM] * 4,
        10**9,
        [
            pltpu.VMEM(scalar_field.shape, jnp.float32),
            pltpu.VMEM(plane_sketch.shape, jnp.float32),
            pltpu.VMEM(second_sketch.shape, jnp.float32),
            pltpu.VMEM(mixing.shape[1:], jnp.float32),
            pltpu.VMEM((ac, gx * ay, own, rank), jnp.float32),
            pltpu.SemaphoreType.DMA((4,)),
        ],
    )(*(in_hbm(source) for source in (scalar_field, plane_sketch, second_sketch, mixing)))
    taken = swap(given, "ac")
    second = call(functools.partial(second_sketch_kernel, own), slot, [VMEM] * 4, 10**9)(
        scalar_field, plane_sketch, third_sketch, mixing
    )
    slots = call(slots_kernel, vmem32(slot.shape), [VMEM] * 3, 10**6)(kept, second, taken)
    received = lax.all_to_all(slots, ("gx", "ay"), 0, 0, tiled=True)
    copies = call(
        functools.partial(total_kernel, gx, ay, own),
        vmem32((gx * ay, own + ay * strip, rank)),
        [VMEM],
        10**6,
    )(received)
    same = lax.all_to_all(copies, ("gx", "ay"), 0, 0, tiled=True)
    other = swap(same, "ac")
    across = swap(scalar_field, "ay")
    product, same_gram = call(
        functools.partial(same_core_kernel, gx, ay, own),
        [f32((rank, planes * cells)), f32((rank, rank))],
        [VMEM] * 3,
        10**9,
    )(same, scalar_field, across)
    second_inverse, partial = call(
        functools.partial(second_kernel, gx, ay, ac),
        [f32((rank, rank)), vmem32((gx, planes, share, rank))],
        [VMEM] * 6,
        2 * 10**9,
        [pltpu.VMEM((gx * ay * ac, own, rank), jnp.float32)],
    )(same, other, swap(scalar_field, "ac"), swap(across, "ac"), product, same_gram)
    every = lax.all_to_all(partial, "gx", 0, 0, tiled=True)
    out_rows = BLOCKS * BLOCK // gx
    factor_second, factor_third, turned, weights = call(
        functools.partial(third_kernel, gx, ay, ac, own),
        [
            f32((own, rank)),
            f32((own, rank)),
            f32((rank, rank)),
            f32((out_rows, gx * planes // BLOCK, rank)),
        ],
        [SMEM] * 2 + [VMEM] * 3,
        10**9,
        [pltpu.VMEM((gx * ay * ac, own, rank), jnp.float32)],
    )(plane_targets, plane_signs, same, other, second_inverse)
    core_sketch = call(core_kernel, f32((out_rows, share, rank)), [VMEM] * 3, 10**8)(
        weights, turned, every.reshape(gx * planes, share, rank)
    )
    return (factor_second, factor_third, core_sketch)


def solution(mesh):
    gx, af = mesh.devices.shape
    mesh = jax.sharding.Mesh(mesh.devices.reshape(gx, af // 2, 2), ("gx", "ay", "ac"))
    af = ("ay", "ac")
    in_specs = (P("gx", af, None), P("gx", None, None), P(af, None), P(), P(), P(), P())
    out_specs = (P(af + ("gx",), None), P(("gx",) + af, None), P("gx", af, None))
    return jax.shard_map(body, mesh=mesh, in_specs=in_specs, out_specs=out_specs, check_vma=False)
```

```python
import functools

import jax
import jax.numpy as jnp
from jax import lax
from jax.experimental import pallas as pl
from jax.experimental.pallas import tpu as pltpu
from jax.sharding import PartitionSpec as P

BLOCK = 16
BLOCKS = 8
SUB = 8
NEAR = 3

precise = lax.Precision.HIGHEST
VMEM = pl.BlockSpec(memory_space=pltpu.VMEM)
SMEM = pl.BlockSpec(memory_space=pltpu.SMEM)
HBM = pl.BlockSpec(memory_space=pltpu.HBM)


def dot(left, right, dims):
    return lax.dot_general(
        left, right, (dims, ((), ())), precision=precise, preferred_element_type=jnp.float32
    )


def mm(left, right):
    return dot(left, right, ((1,), (0,)))


def mm_tn(left, right):
    return dot(left, right, ((0,), (0,)))


def mm_nt(left, right):
    return dot(left, right, ((1,), (1,)))


def inverse_lower(gram, tasks=()):
    size = gram.shape[0]
    count = size // SUB
    tasks = list(tasks)
    sub_ids = lax.broadcasted_iota(jnp.int32, (SUB, size), 0)
    lane_ids = lax.broadcasted_iota(jnp.int32, (SUB, size), 1)
    rows = [gram[SUB * i : SUB * i + SUB, :] for i in range(count)]
    done = []

    def along_sub(tile, j):
        return jnp.broadcast_to(tile[j : j + 1, :], (SUB, size))

    def along_lanes(tile, block):
        return [
            jnp.broadcast_to(tile[:, SUB * block + c : SUB * block + c + 1], (SUB, size))
            for c in range(SUB)
        ]

    diag = along_lanes(rows[0], 0)
    pivot = along_sub(diag[0], 0)
    for k in range(count):
        inside = (lane_ids >= SUB * k) & (lane_ids < SUB * k + SUB)
        near = range(k + 1, min(k + 1 + NEAR, count))
        far = range(k + 1 + NEAR, count)
        cols = {i: along_lanes(rows[i], k) for i in near}
        ahead = along_lanes(rows[k + 1], k + 1) if k + 1 < count else None
        identity = jnp.where(lane_ids == sub_ids + SUB * k, 1.0, 0.0)
        solved = jnp.where(inside, identity, rows[k])
        columns = [jnp.where(inside, rows[i], 0.0) for i in far]
        for i in range(k + 1, count):
            rows[i] = jnp.where(inside, 0.0, rows[i])
        pivots = None
        for j in range(SUB):
            pivots = pivot if j == 0 else jnp.where(sub_ids == j, pivot, pivots)
            scale = 1.0 / pivot
            heads = {c: along_sub(diag[c], j) for c in range(j + 1, SUB)}
            row_head = along_sub(solved, j)
            rows[k] = row_head if j == 0 else jnp.where(sub_ids == j, row_head, rows[k])
            if j < SUB - 1:
                pivot = along_sub(diag[j + 1], j + 1) - (heads[j + 1] * heads[j + 1]) * scale
            elif k + 1 < count:
                head = along_sub(cols[k + 1][j], 0)
                pivot = along_sub(ahead[0], 0) - (head * head) * scale
            others = jnp.where(sub_ids == j, 0.0, diag[j])
            factor = others * scale
            for c in range(j + 1, SUB):
                diag[c] = diag[c] - factor * heads[c]
            solved = solved - factor * row_head
            for i in near:
                factor = cols[i][j] * scale
                if i == k + 1:
                    for c in range(SUB):
                        ahead[c] = ahead[c] - factor * along_sub(cols[i][j], c)
                for c in range(j + 1, SUB):
                    cols[i][c] = cols[i][c] - factor * heads[c]
                rows[i] = rows[i] - factor * row_head
        if len(far):
            parts = [jnp.zeros((SUB * k, size), jnp.float32)] if k else []
            parts.append(solved * (1.0 / pivots))
            parts.append(jnp.zeros((size - SUB * k - SUB, size), jnp.float32))
            update = mm(jnp.concatenate(columns, axis=0), jnp.concatenate(parts, axis=0))
            for n, i in enumerate(far):
                rows[i] = rows[i] - update[SUB * n : SUB * n + SUB, :]
        kept = jnp.where(lane_ids < SUB * k + SUB, rows[k], 0.0)
        done.append(kept * lax.rsqrt(pivots))
        diag = ahead
        for task in tasks[: -(-len(tasks) // (count - k))]:
            task()
        tasks = tasks[-(-len(tasks) // (count - k)) :]
    return jnp.concatenate(done, axis=0)


def place():
    return [lax.axis_index(axis) for axis in ("gx", "ay", "ac")]


def third_sketch_kernel(
    gx, ay, field_in, plane_in, second_in, mixing_in, kept, given, *scratch
):
    field, plane_sketch, second_sketch, mixing, blocks, arrived = scratch
    copies = [
        pltpu.make_async_copy(source, target, arrived.at[n])
        for n, (source, target) in enumerate(
            (
                (plane_in, plane_sketch),
                (second_in, second_sketch),
                (mixing_in.at[1], mixing),
                (field_in, field),
            )
        )
    ]
    for copy in copies:
        copy.start()
    for copy in copies[:3]:
        copy.wait()
    planes, rows, cells = field.shape
    scaled = [second_sketch[...] * plane_sketch[p, 1:2, :] for p in range(planes)]
    weights = mm(jnp.concatenate(scaled, axis=0), mixing[...])
    copies[3].wait()
    wide = jnp.transpose(mm_tn(weights, field[...].reshape(planes * rows, cells)))
    own = blocks.shape[2]
    for n in range(2 * gx * ay):
        blocks[n // (gx * ay), n % (gx * ay)] = wide[n * own : n * own + own, :]
    core = place()[2]
    blank = jnp.zeros((gx * ay, kept.shape[1] - own, kept.shape[2]), jnp.float32)
    for half, out in ((core, kept), (1 - core, given)):
        out[:, 0:own, :] = blocks[half]
        out[:, own:, :] = blank


def second_sketch_kernel(own, field, plane_sketch, third_sketch, mixing, out):
    planes, rows, cells = field.shape
    across = None
    for p in range(planes):
        term = mm(field[p], third_sketch[...] * plane_sketch[p, 0:1, :])
        across = term if across is None else across + term
    second = mm(across, mixing[0])
    strip = out.shape[1] - own
    for n in range(out.shape[0]):
        out[n, 0:own, :] = jnp.zeros((own, out.shape[2]), jnp.float32)
        out[n, own:, :] = second[n * strip : n * strip + strip, :]


def total_kernel(gx, ay, own, received, out):
    strip = received.shape[1] - own
    third = received[0, 0:own, :]
    for n in range(1, gx * ay):
        third = third + received[n, 0:own, :]
    seconds = []
    for y in range(ay):
        second = received[y, own:, :]
        for g in range(1, gx):
            second = second + received[g * ay + y, own:, :]
        seconds.append(second)
    for n in range(gx * ay):
        out[n, 0:own, :] = third
        for y in range(ay):
            out[n, own + y * strip : own + (y + 1) * strip, :] = seconds[y]


def core_ranges(gx, ay, own, ranges):
    strip = (ranges.shape[1] - own) // ay
    return [
        jnp.concatenate(
            [ranges[n, own + y * strip : own + (y + 1) * strip, :] for n in range(gx * ay)], axis=0
        )
        for y in range(ay)
    ]


def own_first(quarters):
    at = place()
    return jnp.concatenate(
        [
            jnp.where(at[1] == 0, quarters[0], quarters[1]),
            jnp.where(at[1] == 0, quarters[1], quarters[0]),
        ],
        axis=0,
    )


def same_core_kernel(gx, ay, own, ranges, near_field, far_field, product, gram):
    quarters = core_ranges(gx, ay, own, ranges)
    both = jnp.concatenate(quarters, axis=0)
    gram[...] = mm_tn(both, both)
    turned = jnp.transpose(own_first(quarters))
    cells = near_field.shape[2]
    for p in range(near_field.shape[0]):
        field = jnp.concatenate([near_field[p], far_field[p]], axis=0)
        product[:, p * cells : p * cells + cells] = mm(turned, field)


def second_kernel(
    gx, ay, ac, same, other, near_field, far_field, product, same_gram, inverse_out, partial, third
):
    at = place()
    planes, rows, cells = near_field.shape
    own = cells // (gx * ay * ac)
    rank = same.shape[2]
    quarters = core_ranges(gx, ay, own, other)
    both = jnp.concatenate(quarters, axis=0)
    gram = same_gram[...] + mm_tn(both, both)
    for swapped, ranges in enumerate((same, other)):
        for n in range(gx * ay):
            third[(at[2] ^ swapped) * (gx * ay) + n] = ranges[n, 0:own, :]
    all_third = jnp.concatenate([third[n] for n in range(gx * ay * ac)], axis=0)
    turned = jnp.transpose(own_first(quarters))
    halves = [[None, None] for _ in range(planes)]
    raw = [None] * planes
    width = cells // 2

    def field_product(p, h):
        span = slice(h * width, h * width + width)
        field = jnp.concatenate([near_field[p, :, span], far_field[p, :, span]], axis=0)
        held = product[:, p * cells + h * width : p * cells + h * width + width]
        halves[p][h] = held + mm(turned, field)

    def range_product(p):
        raw[p] = mm(jnp.concatenate(halves[p], axis=1), all_third)

    tasks = [functools.partial(field_product, p, h) for p in range(planes) for h in range(2)]
    tasks += [functools.partial(range_product, p) for p in range(planes)]
    inverse = inverse_lower(gram, tasks)
    inverse_out[...] = inverse
    share = rank // (ay * ac)
    own_rows = inverse[0:share, :]
    for a in range(1, ay * ac):
        piece = inverse[a * share : a * share + share, :]
        own_rows = jnp.where(at[1] * ac + at[2] == a, piece, own_rows)
    value = mm(own_rows, jnp.concatenate(raw, axis=1))
    for p in range(planes):
        for g in range(gx):
            partial[g, p] = value[:, p * rank : p * rank + rank]


def third_kernel(
    gx, ay, ac, own, targets, signs, same, other, second_inverse, *refs
):
    factor_second, factor_third, turned, weights, third = refs
    at = place()
    rank = same.shape[2]
    mine = core_ranges(gx, ay, own, same)
    mine = jnp.where(at[1] == 0, mine[0], mine[1]).reshape(gx, own, rank)
    own_range = mine[0]
    for g in range(1, gx):
        own_range = jnp.where(at[0] == g, mine[g], own_range)
    factor_second[...] = mm_nt(own_range, second_inverse[...])
    for swapped, ranges in enumerate((same, other)):
        for n in range(gx * ay):
            third[(at[2] ^ swapped) * (gx * ay) + n] = ranges[n, 0:own, :]
    all_third = jnp.concatenate([third[n] for n in range(gx * ay * ac)], axis=0)
    inverse = inverse_lower(mm_tn(all_third, all_third))
    turned[...] = jnp.transpose(inverse)
    factor_third[...] = mm_nt(third[(at[0] * ay + at[1]) * ac + at[2]], inverse)
    out_rows, turns, rank = weights.shape
    for r in range(out_rows):
        row = at[0] * out_rows + r
        for m in range(turns):
            plane = m * BLOCK + lax.rem(row, BLOCK)
            weight = jnp.float32(0)
            for t in range(targets.shape[1]):
                sign = (2 * signs[plane, t] - 1).astype(jnp.float32)
                weight = weight + jnp.where(targets[plane, t] == lax.div(row, BLOCK), sign, 0.0)
            weights[r, m : m + 1, :] = jnp.full((1, rank), weight, jnp.float32)


def core_kernel(weights, turned, planes, out):
    out_rows, turns, rank = weights.shape
    share = planes.shape[1]
    first = place()[0] * out_rows
    rows = []
    for r in range(out_rows):
        slot = r % BLOCK if out_rows % BLOCK == 0 else lax.rem(first + r, BLOCK)
        terms = [weights[r, m : m + 1, :] * planes[m * BLOCK + slot] for m in range(turns)]
        rows.append(sum(terms[1:], terms[0]))
    whole = mm(jnp.concatenate(rows, axis=0), turned[...])
    for r in range(out_rows):
        out[r] = whole[r * share : r * share + share, :]


def call(kernel, out_shapes, in_specs, flops, scratch=(), mib=48):
    return pl.pallas_call(
        kernel,
        out_shape=out_shapes,
        in_specs=in_specs,
        out_specs=jax.tree.map(lambda _: VMEM, out_shapes),
        scratch_shapes=scratch,
        compiler_params=pltpu.CompilerParams(vmem_limit_bytes=int(mib * 2**20)),
        cost_estimate=pl.CostEstimate(flops=flops, bytes_accessed=2**20, transcendentals=0),
    )


def in_hbm(source):
    return pltpu.with_memory_space_constraint(source, pltpu.HBM)


def swap(block, axis):
    perm = [(n, n ^ 1) for n in range(lax.axis_size(axis))]
    return lax.ppermute(block, axis, perm)


def body(
    scalar_field, plane_sketch, second_sketch, third_sketch, mixing, plane_targets, plane_signs
):
    gx, ay, ac = lax.axis_size("gx"), lax.axis_size("ay"), lax.axis_size("ac")
    planes, rows, cells = scalar_field.shape
    rank = mixing.shape[2]
    own = cells // (gx * ay * ac)
    strip = rows // (gx * ay)
    share = rank // (ay * ac)
    f32 = functools.partial(jax.ShapeDtypeStruct, dtype=jnp.float32)

    slot = f32((gx * ay, own + strip, rank))
    kept, given = call(
        functools.partial(third_sketch_kernel, gx, ay),
        [slot, slot],
        [HBM] * 4,
        10**9,
        [
            pltpu.VMEM(scalar_field.shape, jnp.float32),
            pltpu.VMEM(plane_sketch.shape, jnp.float32),
            pltpu.VMEM(second_sketch.shape, jnp.float32),
            pltpu.VMEM(mixing.shape[1:], jnp.float32),
            pltpu.VMEM((ac, gx * ay, own, rank), jnp.float32),
            pltpu.SemaphoreType.DMA((4,)),
        ],
    )(*(in_hbm(source) for source in (scalar_field, plane_sketch, second_sketch, mixing)))
    taken = swap(given, "ac")
    second = call(functools.partial(second_sketch_kernel, own), slot, [VMEM] * 4, 10**9)(
        scalar_field, plane_sketch, third_sketch, mixing
    )
    slots = kept + second + taken
    received = lax.all_to_all(slots, ("gx", "ay"), 0, 0, tiled=True)
    copies = call(
        functools.partial(total_kernel, gx, ay, own),
        f32((gx * ay, own + ay * strip, rank)),
        [VMEM],
        10**6,
    )(received)
    same = lax.all_to_all(copies, ("gx", "ay"), 0, 0, tiled=True)
    other = swap(same, "ac")
    across = swap(scalar_field, "ay")
    product, same_gram = call(
        functools.partial(same_core_kernel, gx, ay, own),
        [f32((rank, planes * cells)), f32((rank, rank))],
        [VMEM] * 3,
        10**9,
    )(same, scalar_field, across)
    second_inverse, partial = call(
        functools.partial(second_kernel, gx, ay, ac),
        [f32((rank, rank)), f32((gx, planes, share, rank))],
        [VMEM] * 6,
        2 * 10**9,
        [pltpu.VMEM((gx * ay * ac, own, rank), jnp.float32)],
    )(same, other, swap(scalar_field, "ac"), swap(across, "ac"), product, same_gram)
    every = lax.all_to_all(partial, "gx", 0, 0, tiled=True)
    out_rows = BLOCKS * BLOCK // gx
    factor_second, factor_third, turned, weights = call(
        functools.partial(third_kernel, gx, ay, ac, own),
        [
            f32((own, rank)),
            f32((own, rank)),
            f32((rank, rank)),
            f32((out_rows, gx * planes // BLOCK, rank)),
        ],
        [SMEM] * 2 + [VMEM] * 3,
        10**9,
        [pltpu.VMEM((gx * ay * ac, own, rank), jnp.float32)],
    )(plane_targets, plane_signs, same, other, second_inverse)
    core_sketch = call(core_kernel, f32((out_rows, share, rank)), [VMEM] * 3, 10**8)(
        weights, turned, every.reshape(gx * planes, share, rank)
    )
    return (factor_second, factor_third, core_sketch)


def solution(mesh):
    gx, af = mesh.devices.shape
    mesh = jax.sharding.Mesh(mesh.devices.reshape(gx, af // 2, 2), ("gx", "ay", "ac"))
    af = ("ay", "ac")
    in_specs = (P("gx", af, None), P("gx", None, None), P(af, None), P(), P(), P(), P())
    out_specs = (P(af + ("gx",), None), P(("gx",) + af, None), P("gx", af, None))
    return jax.shard_map(body, mesh=mesh, in_specs=in_specs, out_specs=out_specs, check_vma=False)
```

```python
import functools

import jax
import jax.numpy as jnp
from jax import lax
from jax.experimental import pallas as pl
from jax.experimental.pallas import tpu as pltpu
from jax.sharding import PartitionSpec as P

BLOCK = 16
BLOCKS = 8
SUB = 8

precise = lax.Precision.HIGHEST
VMEM = pl.BlockSpec(memory_space=pltpu.VMEM)
SMEM = pl.BlockSpec(memory_space=pltpu.SMEM)
HBM = pl.BlockSpec(memory_space=pltpu.HBM)


def dot(left, right, dims):
    return lax.dot_general(
        left, right, (dims, ((), ())), precision=precise, preferred_element_type=jnp.float32
    )


def mm(left, right):
    return dot(left, right, ((1,), (0,)))


def mm_tn(left, right):
    return dot(left, right, ((0,), (0,)))


def mm_nt(left, right):
    return dot(left, right, ((1,), (1,)))


def inverse_lower(gram, tasks=()):
    size = gram.shape[0]
    count = size // SUB
    tasks = list(tasks)
    sub_ids = lax.broadcasted_iota(jnp.int32, (SUB, size), 0)
    lane_ids = lax.broadcasted_iota(jnp.int32, (SUB, size), 1)
    rows = [gram[SUB * i : SUB * i + SUB, :] for i in range(count)]
    done = []

    def along_sub(tile, j):
        return jnp.broadcast_to(tile[j : j + 1, :], (SUB, size))

    def along_lanes(tile, block):
        return [
            jnp.broadcast_to(tile[:, SUB * block + c : SUB * block + c + 1], (SUB, size))
            for c in range(SUB)
        ]

    ahead = along_lanes(rows[0], 0)
    for k in range(count):
        inside = (lane_ids >= SUB * k) & (lane_ids < SUB * k + SUB)
        entry = {(i, c): along_sub(ahead[c], i) for c in range(SUB) for i in range(c + 1)}
        cols = {i: along_lanes(rows[i], k) for i in range(k + 1, count)}
        ahead = along_lanes(rows[k + 1], k + 1) if k + 1 < count else None
        identity = jnp.where(lane_ids == sub_ids + SUB * k, 1.0, 0.0)
        own = jnp.where(inside, identity, rows[k])
        own = [along_sub(own, j) for j in range(SUB)]
        for i in range(k + 1, count):
            rows[i] = jnp.where(inside, 0.0, rows[i])
        for j in range(SUB):
            scale = 1.0 / entry[j, j]
            for i in range(j + 1, SUB):
                if i == j + 1:
                    square = entry[j, i] * entry[j, i]
                    entry[i, i] = entry[i, i] - square * scale
                factor = entry[j, i] * scale
                for c in range(i + (i == j + 1), SUB):
                    entry[i, c] = entry[i, c] - factor * entry[j, c]
                own[i] = own[i] - factor * own[j]
            for i in range(k + 1, count):
                factor = cols[i][j] * scale
                if i == k + 1:
                    for c in range(SUB):
                        ahead[c] = ahead[c] - factor * along_sub(cols[i][j], c)
                for c in range(j + 1, SUB):
                    cols[i][c] = cols[i][c] - factor * entry[j, c]
                rows[i] = rows[i] - factor * own[j]
        pivots, solved = entry[0, 0], own[0]
        for j in range(1, SUB):
            pivots = jnp.where(sub_ids == j, entry[j, j], pivots)
            solved = jnp.where(sub_ids == j, own[j], solved)
        kept = jnp.where(lane_ids < SUB * k + SUB, solved, 0.0)
        done.append(kept * lax.rsqrt(pivots))
        for task in tasks[: -(-len(tasks) // (count - k))]:
            task()
        tasks = tasks[-(-len(tasks) // (count - k)) :]
    return jnp.concatenate(done, axis=0)


def place():
    return [lax.axis_index(axis) for axis in ("gx", "ay", "ac")]


def third_sketch_kernel(
    gx, ay, field_in, plane_in, second_in, mixing_in, kept, given, *scratch
):
    field, plane_sketch, second_sketch, mixing, blocks, arrived = scratch
    copies = [
        pltpu.make_async_copy(source, target, arrived.at[n])
        for n, (source, target) in enumerate(
            (
                (plane_in, plane_sketch),
                (second_in, second_sketch),
                (mixing_in.at[1], mixing),
                (field_in, field),
            )
        )
    ]
    for copy in copies:
        copy.start()
    for copy in copies[:3]:
        copy.wait()
    planes, rows, cells = field.shape
    scaled = [second_sketch[...] * plane_sketch[p, 1:2, :] for p in range(planes)]
    weights = mm(jnp.concatenate(scaled, axis=0), mixing[...])
    copies[3].wait()
    wide = jnp.transpose(mm_tn(weights, field[...].reshape(planes * rows, cells)))
    own = blocks.shape[2]
    for n in range(2 * gx * ay):
        blocks[n // (gx * ay), n % (gx * ay)] = wide[n * own : n * own + own, :]
    core = place()[2]
    blank = jnp.zeros((gx * ay, kept.shape[1] - own, kept.shape[2]), jnp.float32)
    for half, out in ((core, kept), (1 - core, given)):
        out[:, 0:own, :] = blocks[half]
        out[:, own:, :] = blank


def second_sketch_kernel(own, field, plane_sketch, third_sketch, mixing, out):
    planes, rows, cells = field.shape
    across = None
    for p in range(planes):
        term = mm(field[p], third_sketch[...] * plane_sketch[p, 0:1, :])
        across = term if across is None else across + term
    second = mm(across, mixing[0])
    strip = out.shape[1] - own
    for n in range(out.shape[0]):
        out[n, 0:own, :] = jnp.zeros((own, out.shape[2]), jnp.float32)
        out[n, own:, :] = second[n * strip : n * strip + strip, :]


def total_kernel(gx, ay, own, received, out):
    strip = received.shape[1] - own
    third = received[0, 0:own, :]
    for n in range(1, gx * ay):
        third = third + received[n, 0:own, :]
    seconds = []
    for y in range(ay):
        second = received[y, own:, :]
        for g in range(1, gx):
            second = second + received[g * ay + y, own:, :]
        seconds.append(second)
    for n in range(gx * ay):
        out[n, 0:own, :] = third
        for y in range(ay):
            out[n, own + y * strip : own + (y + 1) * strip, :] = seconds[y]


def core_ranges(gx, ay, own, ranges):
    strip = (ranges.shape[1] - own) // ay
    return [
        jnp.concatenate(
            [ranges[n, own + y * strip : own + (y + 1) * strip, :] for n in range(gx * ay)], axis=0
        )
        for y in range(ay)
    ]


def own_first(quarters):
    at = place()
    return jnp.concatenate(
        [
            jnp.where(at[1] == 0, quarters[0], quarters[1]),
            jnp.where(at[1] == 0, quarters[1], quarters[0]),
        ],
        axis=0,
    )


def same_core_kernel(gx, ay, own, ranges, near_field, far_field, product, gram):
    quarters = core_ranges(gx, ay, own, ranges)
    both = jnp.concatenate(quarters, axis=0)
    gram[...] = mm_tn(both, both)
    turned = jnp.transpose(own_first(quarters))
    cells = near_field.shape[2]
    for p in range(near_field.shape[0]):
        field = jnp.concatenate([near_field[p], far_field[p]], axis=0)
        product[:, p * cells : p * cells + cells] = mm(turned, field)


def second_kernel(
    gx, ay, ac, same, other, near_field, far_field, product, same_gram, inverse_out, partial, third
):
    at = place()
    planes, rows, cells = near_field.shape
    own = cells // (gx * ay * ac)
    rank = same.shape[2]
    quarters = core_ranges(gx, ay, own, other)
    both = jnp.concatenate(quarters, axis=0)
    gram = same_gram[...] + mm_tn(both, both)
    for swapped, ranges in enumerate((same, other)):
        for n in range(gx * ay):
            third[(at[2] ^ swapped) * (gx * ay) + n] = ranges[n, 0:own, :]
    all_third = jnp.concatenate([third[n] for n in range(gx * ay * ac)], axis=0)
    turned = jnp.transpose(own_first(quarters))
    halves = [[None, None] for _ in range(planes)]
    raw = [None] * planes
    width = cells // 2

    def field_product(p, h):
        span = slice(h * width, h * width + width)
        field = jnp.concatenate([near_field[p, :, span], far_field[p, :, span]], axis=0)
        held = product[:, p * cells + h * width : p * cells + h * width + width]
        halves[p][h] = held + mm(turned, field)

    def range_product(p):
        raw[p] = mm(jnp.concatenate(halves[p], axis=1), all_third)

    tasks = [functools.partial(field_product, p, h) for p in range(planes) for h in range(2)]
    tasks += [functools.partial(range_product, p) for p in range(planes)]
    inverse = inverse_lower(gram, tasks)
    inverse_out[...] = inverse
    share = rank // (ay * ac)
    own_rows = inverse[0:share, :]
    for a in range(1, ay * ac):
        piece = inverse[a * share : a * share + share, :]
        own_rows = jnp.where(at[1] * ac + at[2] == a, piece, own_rows)
    value = mm(own_rows, jnp.concatenate(raw, axis=1))
    for p in range(planes):
        for g in range(gx):
            partial[g, p] = value[:, p * rank : p * rank + rank]


def third_kernel(
    gx, ay, ac, own, targets, signs, same, other, second_inverse, *refs
):
    factor_second, factor_third, turned, weights, third = refs
    at = place()
    rank = same.shape[2]
    mine = core_ranges(gx, ay, own, same)
    mine = jnp.where(at[1] == 0, mine[0], mine[1]).reshape(gx, own, rank)
    own_range = mine[0]
    for g in range(1, gx):
        own_range = jnp.where(at[0] == g, mine[g], own_range)
    factor_second[...] = mm_nt(own_range, second_inverse[...])
    for swapped, ranges in enumerate((same, other)):
        for n in range(gx * ay):
            third[(at[2] ^ swapped) * (gx * ay) + n] = ranges[n, 0:own, :]
    all_third = jnp.concatenate([third[n] for n in range(gx * ay * ac)], axis=0)
    inverse = inverse_lower(mm_tn(all_third, all_third))
    turned[...] = jnp.transpose(inverse)
    factor_third[...] = mm_nt(third[(at[0] * ay + at[1]) * ac + at[2]], inverse)
    out_rows, turns, rank = weights.shape
    for r in range(out_rows):
        row = at[0] * out_rows + r
        for m in range(turns):
            plane = m * BLOCK + lax.rem(row, BLOCK)
            weight = jnp.float32(0)
            for t in range(targets.shape[1]):
                sign = (2 * signs[plane, t] - 1).astype(jnp.float32)
                weight = weight + jnp.where(targets[plane, t] == lax.div(row, BLOCK), sign, 0.0)
            weights[r, m : m + 1, :] = jnp.full((1, rank), weight, jnp.float32)


def core_kernel(weights, turned, planes, out):
    out_rows, turns, rank = weights.shape
    share = planes.shape[1]
    first = place()[0] * out_rows
    rows = []
    for r in range(out_rows):
        slot = r % BLOCK if out_rows % BLOCK == 0 else lax.rem(first + r, BLOCK)
        terms = [weights[r, m : m + 1, :] * planes[m * BLOCK + slot] for m in range(turns)]
        rows.append(sum(terms[1:], terms[0]))
    whole = mm(jnp.concatenate(rows, axis=0), turned[...])
    for r in range(out_rows):
        out[r] = whole[r * share : r * share + share, :]


def call(kernel, out_shapes, in_specs, flops, scratch=(), mib=48):
    return pl.pallas_call(
        kernel,
        out_shape=out_shapes,
        in_specs=in_specs,
        out_specs=jax.tree.map(lambda _: VMEM, out_shapes),
        scratch_shapes=scratch,
        compiler_params=pltpu.CompilerParams(vmem_limit_bytes=int(mib * 2**20)),
        cost_estimate=pl.CostEstimate(flops=flops, bytes_accessed=2**20, transcendentals=0),
    )


def in_hbm(source):
    return pltpu.with_memory_space_constraint(source, pltpu.HBM)


def swap(block, axis):
    perm = [(n, n ^ 1) for n in range(lax.axis_size(axis))]
    return lax.ppermute(block, axis, perm)


def body(
    scalar_field, plane_sketch, second_sketch, third_sketch, mixing, plane_targets, plane_signs
):
    gx, ay, ac = lax.axis_size("gx"), lax.axis_size("ay"), lax.axis_size("ac")
    planes, rows, cells = scalar_field.shape
    rank = mixing.shape[2]
    own = cells // (gx * ay * ac)
    strip = rows // (gx * ay)
    share = rank // (ay * ac)
    f32 = functools.partial(jax.ShapeDtypeStruct, dtype=jnp.float32)

    slot = f32((gx * ay, own + strip, rank))
    kept, given = call(
        functools.partial(third_sketch_kernel, gx, ay),
        [slot, slot],
        [HBM] * 4,
        10**9,
        [
            pltpu.VMEM(scalar_field.shape, jnp.float32),
            pltpu.VMEM(plane_sketch.shape, jnp.float32),
            pltpu.VMEM(second_sketch.shape, jnp.float32),
            pltpu.VMEM(mixing.shape[1:], jnp.float32),
            pltpu.VMEM((ac, gx * ay, own, rank), jnp.float32),
            pltpu.SemaphoreType.DMA((4,)),
        ],
    )(*(in_hbm(source) for source in (scalar_field, plane_sketch, second_sketch, mixing)))
    taken = swap(given, "ac")
    second = call(functools.partial(second_sketch_kernel, own), slot, [VMEM] * 4, 10**9)(
        scalar_field, plane_sketch, third_sketch, mixing
    )
    slots = kept + second + taken
    received = lax.all_to_all(slots, ("gx", "ay"), 0, 0, tiled=True)
    copies = call(
        functools.partial(total_kernel, gx, ay, own),
        f32((gx * ay, own + ay * strip, rank)),
        [VMEM],
        10**6,
    )(received)
    same = lax.all_to_all(copies, ("gx", "ay"), 0, 0, tiled=True)
    other = swap(same, "ac")
    across = swap(scalar_field, "ay")
    product, same_gram = call(
        functools.partial(same_core_kernel, gx, ay, own),
        [f32((rank, planes * cells)), f32((rank, rank))],
        [VMEM] * 3,
        10**9,
    )(same, scalar_field, across)
    second_inverse, partial = call(
        functools.partial(second_kernel, gx, ay, ac),
        [f32((rank, rank)), f32((gx, planes, share, rank))],
        [VMEM] * 6,
        2 * 10**9,
        [pltpu.VMEM((gx * ay * ac, own, rank), jnp.float32)],
    )(same, other, swap(scalar_field, "ac"), swap(across, "ac"), product, same_gram)
    every = lax.all_to_all(partial, "gx", 0, 0, tiled=True)
    out_rows = BLOCKS * BLOCK // gx
    factor_second, factor_third, turned, weights = call(
        functools.partial(third_kernel, gx, ay, ac, own),
        [
            f32((own, rank)),
            f32((own, rank)),
            f32((rank, rank)),
            f32((out_rows, gx * planes // BLOCK, rank)),
        ],
        [SMEM] * 2 + [VMEM] * 3,
        10**9,
        [pltpu.VMEM((gx * ay * ac, own, rank), jnp.float32)],
    )(plane_targets, plane_signs, same, other, second_inverse)
    core_sketch = call(core_kernel, f32((out_rows, share, rank)), [VMEM] * 3, 10**8)(
        weights, turned, every.reshape(gx * planes, share, rank)
    )
    return (factor_second, factor_third, core_sketch)


def solution(mesh):
    gx, af = mesh.devices.shape
    mesh = jax.sharding.Mesh(mesh.devices.reshape(gx, af // 2, 2), ("gx", "ay", "ac"))
    af = ("ay", "ac")
    in_specs = (P("gx", af, None), P("gx", None, None), P(af, None), P(), P(), P(), P())
    out_specs = (P(af + ("gx",), None), P(("gx",) + af, None), P("gx", af, None))
    return jax.shard_map(body, mesh=mesh, in_specs=in_specs, out_specs=out_specs, check_vma=False)
```

```python
import functools

import jax
import jax.numpy as jnp
from jax import lax
from jax.experimental import pallas as pl
from jax.experimental.pallas import tpu as pltpu
from jax.sharding import PartitionSpec as P

BLOCK = 16
BLOCKS = 8
SUB = 8

precise = lax.Precision.HIGHEST
VMEM = pl.BlockSpec(memory_space=pltpu.VMEM)
SMEM = pl.BlockSpec(memory_space=pltpu.SMEM)
HBM = pl.BlockSpec(memory_space=pltpu.HBM)


def dot(left, right, dims):
    return lax.dot_general(
        left, right, (dims, ((), ())), precision=precise, preferred_element_type=jnp.float32
    )


def mm(left, right):
    return dot(left, right, ((1,), (0,)))


def mm_tn(left, right):
    return dot(left, right, ((0,), (0,)))


def mm_nt(left, right):
    return dot(left, right, ((1,), (1,)))


def inverse_lower(gram, tasks=()):
    size = gram.shape[0]
    count = size // SUB
    tasks = list(tasks)
    sub_ids = lax.broadcasted_iota(jnp.int32, (SUB, size), 0)
    lane_ids = lax.broadcasted_iota(jnp.int32, (SUB, size), 1)
    rows = [gram[SUB * i : SUB * i + SUB, :] for i in range(count)]
    done = []

    def along_sub(tile, j):
        return jnp.broadcast_to(tile[j : j + 1, :], (SUB, size))

    def along_lanes(tile, block):
        return [
            jnp.broadcast_to(tile[:, SUB * block + c : SUB * block + c + 1], (SUB, size))
            for c in range(SUB)
        ]

    diag = along_lanes(rows[0], 0)
    pivot = along_sub(diag[0], 0)
    for k in range(count):
        inside = (lane_ids >= SUB * k) & (lane_ids < SUB * k + SUB)
        cols = {i: along_lanes(rows[i], k) for i in range(k + 2, count)}
        if k + 1 < count:
            cols[k + 1] = along_lanes(rows[1], 0) if k == 0 else below_next
        below_next = along_lanes(rows[k + 2], k + 1) if k + 2 < count else None
        ahead = along_lanes(rows[k + 1], k + 1) if k + 1 < count else None
        identity = jnp.where(lane_ids == sub_ids + SUB * k, 1.0, 0.0)
        rows[k] = jnp.where(inside, identity, rows[k])
        for i in range(k + 1, count):
            rows[i] = jnp.where(inside, 0.0, rows[i])
        pivots = None
        for j in range(SUB):
            pivots = pivot if j == 0 else jnp.where(sub_ids == j, pivot, pivots)
            scale = 1.0 / pivot
            heads = {c: along_sub(diag[c], j) for c in range(j + 1, SUB)}
            row_head = along_sub(rows[k], j)
            if j < SUB - 1:
                pivot = along_sub(diag[j + 1], j + 1) - (heads[j + 1] * heads[j + 1]) * scale
            elif k + 1 < count:
                head = along_sub(cols[k + 1][j], 0)
                pivot = along_sub(ahead[0], 0) - (head * head) * scale
            if j < SUB - 1:
                below = jnp.where(sub_ids > j, diag[j], 0.0)
                diag[j + 1] = diag[j + 1] - (below * heads[j + 1]) * scale
                factor = below * scale
                for c in range(j + 2, SUB):
                    diag[c] = diag[c] - factor * heads[c]
                rows[k] = rows[k] - factor * row_head
            for i in range(k + 1, count):
                factor = cols[i][j] * scale
                if i == k + 1:
                    next_heads = [along_sub(cols[i][j], c) for c in range(SUB)]
                    for c in range(SUB):
                        ahead[c] = ahead[c] - factor * next_heads[c]
                if i == k + 2:
                    for c in range(SUB):
                        below_next[c] = below_next[c] - factor * next_heads[c]
                for c in range(j + 1, SUB):
                    cols[i][c] = cols[i][c] - factor * heads[c]
                rows[i] = rows[i] - factor * row_head
        kept = jnp.where(lane_ids < SUB * k + SUB, rows[k], 0.0)
        done.append(kept * lax.rsqrt(pivots))
        diag = ahead
        for task in tasks[: -(-len(tasks) // (count - k))]:
            task()
        tasks = tasks[-(-len(tasks) // (count - k)) :]
    return jnp.concatenate(done, axis=0)


def place():
    return [lax.axis_index(axis) for axis in ("gx", "ay", "ac")]


def third_sketch_kernel(
    gx, ay, field_in, plane_in, second_in, mixing_in, kept, given, *scratch
):
    field, plane_sketch, second_sketch, mixing, blocks, arrived = scratch
    copies = [
        pltpu.make_async_copy(source, target, arrived.at[n])
        for n, (source, target) in enumerate(
            (
                (plane_in, plane_sketch),
                (second_in, second_sketch),
                (mixing_in.at[1], mixing),
                (field_in, field),
            )
        )
    ]
    for copy in copies:
        copy.start()
    for copy in copies[:3]:
        copy.wait()
    planes, rows, cells = field.shape
    scaled = [second_sketch[...] * plane_sketch[p, 1:2, :] for p in range(planes)]
    weights = mm(jnp.concatenate(scaled, axis=0), mixing[...])
    copies[3].wait()
    wide = jnp.transpose(mm_tn(weights, field[...].reshape(planes * rows, cells)))
    own = blocks.shape[2]
    for n in range(2 * gx * ay):
        blocks[n // (gx * ay), n % (gx * ay)] = wide[n * own : n * own + own, :]
    core = place()[2]
    blank = jnp.zeros((gx * ay, kept.shape[1] - own, kept.shape[2]), jnp.float32)
    for half, out in ((core, kept), (1 - core, given)):
        out[:, 0:own, :] = blocks[half]
        out[:, own:, :] = blank


def second_sketch_kernel(own, field, plane_sketch, third_sketch, mixing, out):
    planes, rows, cells = field.shape
    across = None
    for p in range(planes):
        term = mm(field[p], third_sketch[...] * plane_sketch[p, 0:1, :])
        across = term if across is None else across + term
    second = mm(across, mixing[0])
    strip = out.shape[1] - own
    for n in range(out.shape[0]):
        out[n, 0:own, :] = jnp.zeros((own, out.shape[2]), jnp.float32)
        out[n, own:, :] = second[n * strip : n * strip + strip, :]


def total_kernel(gx, ay, own, received, out):
    strip = received.shape[1] - own
    third = received[0, 0:own, :]
    for n in range(1, gx * ay):
        third = third + received[n, 0:own, :]
    seconds = []
    for y in range(ay):
        second = received[y, own:, :]
        for g in range(1, gx):
            second = second + received[g * ay + y, own:, :]
        seconds.append(second)
    for n in range(gx * ay):
        out[n, 0:own, :] = third
        for y in range(ay):
            out[n, own + y * strip : own + (y + 1) * strip, :] = seconds[y]


def core_ranges(gx, ay, own, ranges):
    strip = (ranges.shape[1] - own) // ay
    return [
        jnp.concatenate(
            [ranges[n, own + y * strip : own + (y + 1) * strip, :] for n in range(gx * ay)], axis=0
        )
        for y in range(ay)
    ]


def own_first(quarters):
    at = place()
    return jnp.concatenate(
        [
            jnp.where(at[1] == 0, quarters[0], quarters[1]),
            jnp.where(at[1] == 0, quarters[1], quarters[0]),
        ],
        axis=0,
    )


def same_core_kernel(gx, ay, own, ranges, near_field, far_field, product, gram):
    quarters = core_ranges(gx, ay, own, ranges)
    both = jnp.concatenate(quarters, axis=0)
    gram[...] = mm_tn(both, both)
    turned = jnp.transpose(own_first(quarters))
    cells = near_field.shape[2]
    for p in range(near_field.shape[0]):
        field = jnp.concatenate([near_field[p], far_field[p]], axis=0)
        product[:, p * cells : p * cells + cells] = mm(turned, field)


def second_kernel(
    gx, ay, ac, same, other, near_field, far_field, product, same_gram, inverse_out, partial, third
):
    at = place()
    planes, rows, cells = near_field.shape
    own = cells // (gx * ay * ac)
    rank = same.shape[2]
    quarters = core_ranges(gx, ay, own, other)
    both = jnp.concatenate(quarters, axis=0)
    gram = same_gram[...] + mm_tn(both, both)
    for swapped, ranges in enumerate((same, other)):
        for n in range(gx * ay):
            third[(at[2] ^ swapped) * (gx * ay) + n] = ranges[n, 0:own, :]
    all_third = jnp.concatenate([third[n] for n in range(gx * ay * ac)], axis=0)
    turned = jnp.transpose(own_first(quarters))
    halves = [[None, None] for _ in range(planes)]
    raw = [None] * planes
    width = cells // 2

    def field_product(p, h):
        span = slice(h * width, h * width + width)
        field = jnp.concatenate([near_field[p, :, span], far_field[p, :, span]], axis=0)
        held = product[:, p * cells + h * width : p * cells + h * width + width]
        halves[p][h] = held + mm(turned, field)

    def range_product(p):
        raw[p] = mm(jnp.concatenate(halves[p], axis=1), all_third)

    tasks = [functools.partial(field_product, p, h) for p in range(planes) for h in range(2)]
    tasks += [functools.partial(range_product, p) for p in range(planes)]
    inverse = inverse_lower(gram, tasks)
    inverse_out[...] = inverse
    share = rank // (ay * ac)
    own_rows = inverse[0:share, :]
    for a in range(1, ay * ac):
        piece = inverse[a * share : a * share + share, :]
        own_rows = jnp.where(at[1] * ac + at[2] == a, piece, own_rows)
    value = mm(own_rows, jnp.concatenate(raw, axis=1))
    for p in range(planes):
        for g in range(gx):
            partial[g, p] = value[:, p * rank : p * rank + rank]


def third_kernel(
    gx, ay, ac, own, targets, signs, same, other, second_inverse, *refs
):
    factor_second, factor_third, turned, weights, third = refs
    at = place()
    rank = same.shape[2]
    mine = core_ranges(gx, ay, own, same)
    mine = jnp.where(at[1] == 0, mine[0], mine[1]).reshape(gx, own, rank)
    own_range = mine[0]
    for g in range(1, gx):
        own_range = jnp.where(at[0] == g, mine[g], own_range)
    factor_second[...] = mm_nt(own_range, second_inverse[...])
    for swapped, ranges in enumerate((same, other)):
        for n in range(gx * ay):
            third[(at[2] ^ swapped) * (gx * ay) + n] = ranges[n, 0:own, :]
    all_third = jnp.concatenate([third[n] for n in range(gx * ay * ac)], axis=0)
    inverse = inverse_lower(mm_tn(all_third, all_third))
    turned[...] = jnp.transpose(inverse)
    factor_third[...] = mm_nt(third[(at[0] * ay + at[1]) * ac + at[2]], inverse)
    out_rows, turns, rank = weights.shape
    for r in range(out_rows):
        row = at[0] * out_rows + r
        for m in range(turns):
            plane = m * BLOCK + lax.rem(row, BLOCK)
            weight = jnp.float32(0)
            for t in range(targets.shape[1]):
                sign = (2 * signs[plane, t] - 1).astype(jnp.float32)
                weight = weight + jnp.where(targets[plane, t] == lax.div(row, BLOCK), sign, 0.0)
            weights[r, m : m + 1, :] = jnp.full((1, rank), weight, jnp.float32)


def core_kernel(weights, turned, planes, out):
    out_rows, turns, rank = weights.shape
    share = planes.shape[1]
    first = place()[0] * out_rows
    rows = []
    for r in range(out_rows):
        slot = r % BLOCK if out_rows % BLOCK == 0 else lax.rem(first + r, BLOCK)
        terms = [weights[r, m : m + 1, :] * planes[m * BLOCK + slot] for m in range(turns)]
        rows.append(sum(terms[1:], terms[0]))
    whole = mm(jnp.concatenate(rows, axis=0), turned[...])
    for r in range(out_rows):
        out[r] = whole[r * share : r * share + share, :]


def call(kernel, out_shapes, in_specs, flops, scratch=(), mib=48):
    return pl.pallas_call(
        kernel,
        out_shape=out_shapes,
        in_specs=in_specs,
        out_specs=jax.tree.map(lambda _: VMEM, out_shapes),
        scratch_shapes=scratch,
        compiler_params=pltpu.CompilerParams(vmem_limit_bytes=int(mib * 2**20)),
        cost_estimate=pl.CostEstimate(flops=flops, bytes_accessed=2**20, transcendentals=0),
    )


def in_hbm(source):
    return pltpu.with_memory_space_constraint(source, pltpu.HBM)


def swap(block, axis):
    perm = [(n, n ^ 1) for n in range(lax.axis_size(axis))]
    return lax.ppermute(block, axis, perm)


def body(
    scalar_field, plane_sketch, second_sketch, third_sketch, mixing, plane_targets, plane_signs
):
    gx, ay, ac = lax.axis_size("gx"), lax.axis_size("ay"), lax.axis_size("ac")
    planes, rows, cells = scalar_field.shape
    rank = mixing.shape[2]
    own = cells // (gx * ay * ac)
    strip = rows // (gx * ay)
    share = rank // (ay * ac)
    f32 = functools.partial(jax.ShapeDtypeStruct, dtype=jnp.float32)

    slot = f32((gx * ay, own + strip, rank))
    kept, given = call(
        functools.partial(third_sketch_kernel, gx, ay),
        [slot, slot],
        [HBM] * 4,
        10**9,
        [
            pltpu.VMEM(scalar_field.shape, jnp.float32),
            pltpu.VMEM(plane_sketch.shape, jnp.float32),
            pltpu.VMEM(second_sketch.shape, jnp.float32),
            pltpu.VMEM(mixing.shape[1:], jnp.float32),
            pltpu.VMEM((ac, gx * ay, own, rank), jnp.float32),
            pltpu.SemaphoreType.DMA((4,)),
        ],
    )(*(in_hbm(source) for source in (scalar_field, plane_sketch, second_sketch, mixing)))
    taken = swap(given, "ac")
    second = call(functools.partial(second_sketch_kernel, own), slot, [VMEM] * 4, 10**9)(
        scalar_field, plane_sketch, third_sketch, mixing
    )
    slots = kept + second + taken
    received = lax.all_to_all(slots, ("gx", "ay"), 0, 0, tiled=True)
    copies = call(
        functools.partial(total_kernel, gx, ay, own),
        f32((gx * ay, own + ay * strip, rank)),
        [VMEM],
        10**6,
    )(received)
    same = lax.all_to_all(copies, ("gx", "ay"), 0, 0, tiled=True)
    other = swap(same, "ac")
    across = swap(scalar_field, "ay")
    product, same_gram = call(
        functools.partial(same_core_kernel, gx, ay, own),
        [f32((rank, planes * cells)), f32((rank, rank))],
        [VMEM] * 3,
        10**9,
    )(same, scalar_field, across)
    second_inverse, partial = call(
        functools.partial(second_kernel, gx, ay, ac),
        [f32((rank, rank)), f32((gx, planes, share, rank))],
        [VMEM] * 6,
        2 * 10**9,
        [pltpu.VMEM((gx * ay * ac, own, rank), jnp.float32)],
    )(same, other, swap(scalar_field, "ac"), swap(across, "ac"), product, same_gram)
    every = lax.all_to_all(partial, "gx", 0, 0, tiled=True)
    out_rows = BLOCKS * BLOCK // gx
    factor_second, factor_third, turned, weights = call(
        functools.partial(third_kernel, gx, ay, ac, own),
        [
            f32((own, rank)),
            f32((own, rank)),
            f32((rank, rank)),
            f32((out_rows, gx * planes // BLOCK, rank)),
        ],
        [SMEM] * 2 + [VMEM] * 3,
        10**9,
        [pltpu.VMEM((gx * ay * ac, own, rank), jnp.float32)],
    )(plane_targets, plane_signs, same, other, second_inverse)
    core_sketch = call(core_kernel, f32((out_rows, share, rank)), [VMEM] * 3, 10**8)(
        weights, turned, every.reshape(gx * planes, share, rank)
    )
    return (factor_second, factor_third, core_sketch)


def solution(mesh):
    gx, af = mesh.devices.shape
    mesh = jax.sharding.Mesh(mesh.devices.reshape(gx, af // 2, 2), ("gx", "ay", "ac"))
    af = ("ay", "ac")
    in_specs = (P("gx", af, None), P("gx", None, None), P(af, None), P(), P(), P(), P())
    out_specs = (P(af + ("gx",), None), P(("gx",) + af, None), P("gx", af, None))
    return jax.shard_map(body, mesh=mesh, in_specs=in_specs, out_specs=out_specs, check_vma=False)
```

```python
import functools

import jax
import jax.numpy as jnp
from jax import lax
from jax.experimental import pallas as pl
from jax.experimental.pallas import tpu as pltpu
from jax.sharding import PartitionSpec as P

BLOCK = 16
BLOCKS = 8
SUB = 8

precise = lax.Precision.HIGHEST
VMEM = pl.BlockSpec(memory_space=pltpu.VMEM)
SMEM = pl.BlockSpec(memory_space=pltpu.SMEM)
HBM = pl.BlockSpec(memory_space=pltpu.HBM)


def dot(left, right, dims):
    return lax.dot_general(
        left, right, (dims, ((), ())), precision=precise, preferred_element_type=jnp.float32
    )


def mm(left, right):
    return dot(left, right, ((1,), (0,)))


def mm_tn(left, right):
    return dot(left, right, ((0,), (0,)))


def mm_nt(left, right):
    return dot(left, right, ((1,), (1,)))


def inverse_lower(gram, tasks=()):
    size = gram.shape[0]
    count = size // SUB
    due = {}
    for n, task in enumerate(reversed(tasks)):
        due.setdefault(max(count - 2 - 2 * n, 0), []).insert(0, task)
    sub_ids = lax.broadcasted_iota(jnp.int32, (SUB, size), 0)
    lane_ids = lax.broadcasted_iota(jnp.int32, (SUB, size), 1)
    rows = [gram[SUB * i : SUB * i + SUB, :] for i in range(count)]
    done = []

    def along_sub(tile, j):
        return jnp.broadcast_to(tile[j : j + 1, :], (SUB, size))

    def along_lanes(tile, block):
        return [
            jnp.broadcast_to(tile[:, SUB * block + c : SUB * block + c + 1], (SUB, size))
            for c in range(SUB)
        ]

    diag = along_lanes(rows[0], 0)
    pivot = along_sub(diag[0], 0)
    for k in range(count):
        inside = (lane_ids >= SUB * k) & (lane_ids < SUB * k + SUB)
        cols = {i: along_lanes(rows[i], k) for i in range(k + 2, count)}
        if k + 1 < count:
            cols[k + 1] = along_lanes(rows[1], 0) if k == 0 else below_next
        below_next = along_lanes(rows[k + 2], k + 1) if k + 2 < count else None
        ahead = along_lanes(rows[k + 1], k + 1) if k + 1 < count else None
        identity = jnp.where(lane_ids == sub_ids + SUB * k, 1.0, 0.0)
        rows[k] = jnp.where(inside, identity, rows[k])
        for i in range(k + 1, count):
            rows[i] = jnp.where(inside, 0.0, rows[i])
        pivots = None
        for j in range(SUB):
            pivots = pivot if j == 0 else jnp.where(sub_ids == j, pivot, pivots)
            scale = 1.0 / pivot
            heads = {c: along_sub(diag[c], j) for c in range(j + 1, SUB)}
            row_head = along_sub(rows[k], j)
            if j < SUB - 1:
                pivot = along_sub(diag[j + 1], j + 1) - (heads[j + 1] * heads[j + 1]) * scale
            elif k + 1 < count:
                head = along_sub(cols[k + 1][j], 0)
                pivot = along_sub(ahead[0], 0) - (head * head) * scale
            if j < SUB - 1:
                below = jnp.where(sub_ids > j, diag[j], 0.0)
                diag[j + 1] = diag[j + 1] - (below * heads[j + 1]) * scale
                factor = below * scale
                for c in range(j + 2, SUB):
                    diag[c] = diag[c] - factor * heads[c]
                rows[k] = rows[k] - factor * row_head
            for i in range(k + 1, count):
                factor = cols[i][j] * scale
                if i == k + 1:
                    next_heads = [along_sub(cols[i][j], c) for c in range(SUB)]
                    for c in range(SUB):
                        ahead[c] = ahead[c] - factor * next_heads[c]
                if i == k + 2:
                    for c in range(SUB):
                        below_next[c] = below_next[c] - factor * next_heads[c]
                for c in range(j + 1, SUB):
                    cols[i][c] = cols[i][c] - factor * heads[c]
                rows[i] = rows[i] - factor * row_head
        kept = jnp.where(lane_ids < SUB * k + SUB, rows[k], 0.0)
        done.append(kept * lax.rsqrt(pivots))
        diag = ahead
        for task in due.get(k, ()):
            task()
    return jnp.concatenate(done, axis=0)


def place():
    return [lax.axis_index(axis) for axis in ("gx", "ay", "ac")]


def third_sketch_kernel(
    gx, ay, field_in, plane_in, second_in, mixing_in, kept, given, *scratch
):
    field, plane_sketch, second_sketch, mixing, blocks, arrived = scratch
    copies = [
        pltpu.make_async_copy(source, target, arrived.at[n])
        for n, (source, target) in enumerate(
            (
                (plane_in, plane_sketch),
                (second_in, second_sketch),
                (mixing_in.at[1], mixing),
                (field_in, field),
            )
        )
    ]
    for copy in copies:
        copy.start()
    for copy in copies[:3]:
        copy.wait()
    planes, rows, cells = field.shape
    scaled = [second_sketch[...] * plane_sketch[p, 1:2, :] for p in range(planes)]
    weights = mm(jnp.concatenate(scaled, axis=0), mixing[...])
    copies[3].wait()
    wide = jnp.transpose(mm_tn(weights, field[...].reshape(planes * rows, cells)))
    own = blocks.shape[2]
    for n in range(2 * gx * ay):
        blocks[n // (gx * ay), n % (gx * ay)] = wide[n * own : n * own + own, :]
    core = place()[2]
    blank = jnp.zeros((gx * ay, kept.shape[1] - own, kept.shape[2]), jnp.float32)
    for half, out in ((core, kept), (1 - core, given)):
        out[:, 0:own, :] = blocks[half]
        out[:, own:, :] = blank


def second_sketch_kernel(own, field, plane_sketch, third_sketch, mixing, out):
    planes, rows, cells = field.shape
    across = None
    for p in range(planes):
        term = mm(field[p], third_sketch[...] * plane_sketch[p, 0:1, :])
        across = term if across is None else across + term
    second = mm(across, mixing[0])
    strip = out.shape[1] - own
    for n in range(out.shape[0]):
        out[n, 0:own, :] = jnp.zeros((own, out.shape[2]), jnp.float32)
        out[n, own:, :] = second[n * strip : n * strip + strip, :]


def total_kernel(gx, ay, own, received, out):
    strip = received.shape[1] - own
    third = received[0, 0:own, :]
    for n in range(1, gx * ay):
        third = third + received[n, 0:own, :]
    seconds = []
    for y in range(ay):
        second = received[y, own:, :]
        for g in range(1, gx):
            second = second + received[g * ay + y, own:, :]
        seconds.append(second)
    for n in range(gx * ay):
        out[n, 0:own, :] = third
        for y in range(ay):
            out[n, own + y * strip : own + (y + 1) * strip, :] = seconds[y]


def core_ranges(gx, ay, own, ranges):
    strip = (ranges.shape[1] - own) // ay
    return [
        jnp.concatenate(
            [ranges[n, own + y * strip : own + (y + 1) * strip, :] for n in range(gx * ay)], axis=0
        )
        for y in range(ay)
    ]


def own_first(quarters):
    at = place()
    return jnp.concatenate(
        [
            jnp.where(at[1] == 0, quarters[0], quarters[1]),
            jnp.where(at[1] == 0, quarters[1], quarters[0]),
        ],
        axis=0,
    )


def same_core_kernel(gx, ay, own, ranges, near_field, far_field, product, gram):
    quarters = core_ranges(gx, ay, own, ranges)
    both = jnp.concatenate(quarters, axis=0)
    gram[...] = mm_tn(both, both)
    turned = jnp.transpose(own_first(quarters))
    cells = near_field.shape[2]
    for p in range(near_field.shape[0]):
        field = jnp.concatenate([near_field[p], far_field[p]], axis=0)
        product[:, p * cells : p * cells + cells] = mm(turned, field)


def second_kernel(
    gx, ay, ac, same, other, near_field, far_field, product, same_gram, inverse_out, partial, third
):
    at = place()
    planes, rows, cells = near_field.shape
    own = cells // (gx * ay * ac)
    rank = same.shape[2]
    quarters = core_ranges(gx, ay, own, other)
    both = jnp.concatenate(quarters, axis=0)
    gram = same_gram[...] + mm_tn(both, both)
    for swapped, ranges in enumerate((same, other)):
        for n in range(gx * ay):
            third[(at[2] ^ swapped) * (gx * ay) + n] = ranges[n, 0:own, :]
    all_third = jnp.concatenate([third[n] for n in range(gx * ay * ac)], axis=0)
    turned = jnp.transpose(own_first(quarters))
    halves = [[None, None] for _ in range(planes)]
    raw = [None] * planes
    width = cells // 2

    def field_product(p, h):
        span = slice(h * width, h * width + width)
        field = jnp.concatenate([near_field[p, :, span], far_field[p, :, span]], axis=0)
        held = product[:, p * cells + h * width : p * cells + h * width + width]
        halves[p][h] = held + mm(turned, field)

    def range_product(p):
        raw[p] = mm(jnp.concatenate(halves[p], axis=1), all_third)

    tasks = [functools.partial(field_product, p, h) for p in range(planes) for h in range(2)]
    tasks += [functools.partial(range_product, p) for p in range(planes)]
    inverse = inverse_lower(gram, tasks)
    inverse_out[...] = inverse
    share = rank // (ay * ac)
    own_rows = inverse[0:share, :]
    for a in range(1, ay * ac):
        piece = inverse[a * share : a * share + share, :]
        own_rows = jnp.where(at[1] * ac + at[2] == a, piece, own_rows)
    value = mm(own_rows, jnp.concatenate(raw, axis=1))
    for p in range(planes):
        for g in range(gx):
            partial[g, p] = value[:, p * rank : p * rank + rank]


def third_kernel(
    gx, ay, ac, own, targets, signs, same, other, second_inverse, *refs
):
    factor_second, factor_third, turned, weights, third = refs
    at = place()
    rank = same.shape[2]
    mine = core_ranges(gx, ay, own, same)
    mine = jnp.where(at[1] == 0, mine[0], mine[1]).reshape(gx, own, rank)
    own_range = mine[0]
    for g in range(1, gx):
        own_range = jnp.where(at[0] == g, mine[g], own_range)
    factor_second[...] = mm_nt(own_range, second_inverse[...])
    for swapped, ranges in enumerate((same, other)):
        for n in range(gx * ay):
            third[(at[2] ^ swapped) * (gx * ay) + n] = ranges[n, 0:own, :]
    all_third = jnp.concatenate([third[n] for n in range(gx * ay * ac)], axis=0)
    inverse = inverse_lower(mm_tn(all_third, all_third))
    turned[...] = jnp.transpose(inverse)
    factor_third[...] = mm_nt(third[(at[0] * ay + at[1]) * ac + at[2]], inverse)
    out_rows, turns, rank = weights.shape
    for r in range(out_rows):
        row = at[0] * out_rows + r
        for m in range(turns):
            plane = m * BLOCK + lax.rem(row, BLOCK)
            weight = jnp.float32(0)
            for t in range(targets.shape[1]):
                sign = (2 * signs[plane, t] - 1).astype(jnp.float32)
                weight = weight + jnp.where(targets[plane, t] == lax.div(row, BLOCK), sign, 0.0)
            weights[r, m : m + 1, :] = jnp.full((1, rank), weight, jnp.float32)


def core_kernel(weights, turned, planes, out):
    out_rows, turns, rank = weights.shape
    share = planes.shape[1]
    first = place()[0] * out_rows
    rows = []
    for r in range(out_rows):
        slot = r % BLOCK if out_rows % BLOCK == 0 else lax.rem(first + r, BLOCK)
        terms = [weights[r, m : m + 1, :] * planes[m * BLOCK + slot] for m in range(turns)]
        rows.append(sum(terms[1:], terms[0]))
    whole = mm(jnp.concatenate(rows, axis=0), turned[...])
    for r in range(out_rows):
        out[r] = whole[r * share : r * share + share, :]


def call(kernel, out_shapes, in_specs, flops, scratch=(), mib=48):
    return pl.pallas_call(
        kernel,
        out_shape=out_shapes,
        in_specs=in_specs,
        out_specs=jax.tree.map(lambda _: VMEM, out_shapes),
        scratch_shapes=scratch,
        compiler_params=pltpu.CompilerParams(vmem_limit_bytes=int(mib * 2**20)),
        cost_estimate=pl.CostEstimate(flops=flops, bytes_accessed=2**20, transcendentals=0),
    )


def in_hbm(source):
    return pltpu.with_memory_space_constraint(source, pltpu.HBM)


def swap(block, axis):
    perm = [(n, n ^ 1) for n in range(lax.axis_size(axis))]
    return lax.ppermute(block, axis, perm)


def body(
    scalar_field, plane_sketch, second_sketch, third_sketch, mixing, plane_targets, plane_signs
):
    gx, ay, ac = lax.axis_size("gx"), lax.axis_size("ay"), lax.axis_size("ac")
    planes, rows, cells = scalar_field.shape
    rank = mixing.shape[2]
    own = cells // (gx * ay * ac)
    strip = rows // (gx * ay)
    share = rank // (ay * ac)
    f32 = functools.partial(jax.ShapeDtypeStruct, dtype=jnp.float32)

    slot = f32((gx * ay, own + strip, rank))
    kept, given = call(
        functools.partial(third_sketch_kernel, gx, ay),
        [slot, slot],
        [HBM] * 4,
        10**9,
        [
            pltpu.VMEM(scalar_field.shape, jnp.float32),
            pltpu.VMEM(plane_sketch.shape, jnp.float32),
            pltpu.VMEM(second_sketch.shape, jnp.float32),
            pltpu.VMEM(mixing.shape[1:], jnp.float32),
            pltpu.VMEM((ac, gx * ay, own, rank), jnp.float32),
            pltpu.SemaphoreType.DMA((4,)),
        ],
    )(*(in_hbm(source) for source in (scalar_field, plane_sketch, second_sketch, mixing)))
    taken = swap(given, "ac")
    second = call(functools.partial(second_sketch_kernel, own), slot, [VMEM] * 4, 10**9)(
        scalar_field, plane_sketch, third_sketch, mixing
    )
    slots = kept + second + taken
    received = lax.all_to_all(slots, ("gx", "ay"), 0, 0, tiled=True)
    copies = call(
        functools.partial(total_kernel, gx, ay, own),
        f32((gx * ay, own + ay * strip, rank)),
        [VMEM],
        10**6,
    )(received)
    same = lax.all_to_all(copies, ("gx", "ay"), 0, 0, tiled=True)
    other = swap(same, "ac")
    across = swap(scalar_field, "ay")
    product, same_gram = call(
        functools.partial(same_core_kernel, gx, ay, own),
        [f32((rank, planes * cells)), f32((rank, rank))],
        [VMEM] * 3,
        10**9,
    )(same, scalar_field, across)
    second_inverse, partial = call(
        functools.partial(second_kernel, gx, ay, ac),
        [f32((rank, rank)), f32((gx, planes, share, rank))],
        [VMEM] * 6,
        2 * 10**9,
        [pltpu.VMEM((gx * ay * ac, own, rank), jnp.float32)],
    )(same, other, swap(scalar_field, "ac"), swap(across, "ac"), product, same_gram)
    every = lax.all_to_all(partial, "gx", 0, 0, tiled=True)
    out_rows = BLOCKS * BLOCK // gx
    factor_second, factor_third, turned, weights = call(
        functools.partial(third_kernel, gx, ay, ac, own),
        [
            f32((own, rank)),
            f32((own, rank)),
            f32((rank, rank)),
            f32((out_rows, gx * planes // BLOCK, rank)),
        ],
        [SMEM] * 2 + [VMEM] * 3,
        10**9,
        [pltpu.VMEM((gx * ay * ac, own, rank), jnp.float32)],
    )(plane_targets, plane_signs, same, other, second_inverse)
    core_sketch = call(core_kernel, f32((out_rows, share, rank)), [VMEM] * 3, 10**8)(
        weights, turned, every.reshape(gx * planes, share, rank)
    )
    return (factor_second, factor_third, core_sketch)


def solution(mesh):
    gx, af = mesh.devices.shape
    mesh = jax.sharding.Mesh(mesh.devices.reshape(gx, af // 2, 2), ("gx", "ay", "ac"))
    af = ("ay", "ac")
    in_specs = (P("gx", af, None), P("gx", None, None), P(af, None), P(), P(), P(), P())
    out_specs = (P(af + ("gx",), None), P(("gx",) + af, None), P("gx", af, None))
    return jax.shard_map(body, mesh=mesh, in_specs=in_specs, out_specs=out_specs, check_vma=False)
```

```python
import functools

import jax
import jax.numpy as jnp
from jax import lax
from jax.experimental import pallas as pl
from jax.experimental.pallas import tpu as pltpu
from jax.sharding import PartitionSpec as P

BLOCK = 16
BLOCKS = 8
SUB = 8

precise = lax.Precision.HIGHEST
VMEM = pl.BlockSpec(memory_space=pltpu.VMEM)
SMEM = pl.BlockSpec(memory_space=pltpu.SMEM)
HBM = pl.BlockSpec(memory_space=pltpu.HBM)


def dot(left, right, dims):
    return lax.dot_general(
        left, right, (dims, ((), ())), precision=precise, preferred_element_type=jnp.float32
    )


def mm(left, right):
    return dot(left, right, ((1,), (0,)))


def mm_tn(left, right):
    return dot(left, right, ((0,), (0,)))


def mm_nt(left, right):
    return dot(left, right, ((1,), (1,)))


def inverse_lower(gram, tasks=()):
    size = gram.shape[0]
    count = size // SUB
    tasks = list(tasks)
    sub_ids = lax.broadcasted_iota(jnp.int32, (SUB, size), 0)
    lane_ids = lax.broadcasted_iota(jnp.int32, (SUB, size), 1)
    rows = [gram[SUB * i : SUB * i + SUB, :] for i in range(count)]
    done = []

    def along_sub(tile, j):
        return jnp.broadcast_to(tile[j : j + 1, :], (SUB, size))

    def along_lanes(tile, block):
        return [
            jnp.broadcast_to(tile[:, SUB * block + c : SUB * block + c + 1], (SUB, size))
            for c in range(SUB)
        ]

    diag = along_lanes(rows[0], 0)
    pivot = along_sub(diag[0], 0)
    for k in range(count):
        inside = (lane_ids >= SUB * k) & (lane_ids < SUB * k + SUB)
        cols = {i: along_lanes(rows[i], k) for i in range(k + 2, count)}
        if k + 1 < count:
            cols[k + 1] = along_lanes(rows[1], 0) if k == 0 else below_next
        below_next = along_lanes(rows[k + 2], k + 1) if k + 2 < count else None
        ahead = along_lanes(rows[k + 1], k + 1) if k + 1 < count else None
        identity = jnp.where(lane_ids == sub_ids + SUB * k, 1.0, 0.0)
        rows[k] = jnp.where(inside, identity, rows[k])
        for i in range(k + 1, count):
            rows[i] = jnp.where(inside, 0.0, rows[i])
        pivots = None
        for j in range(SUB):
            pivots = pivot if j == 0 else jnp.where(sub_ids == j, pivot, pivots)
            scale = 1.0 / pivot
            heads = {c: along_sub(diag[c], j) for c in range(j + 1, SUB)}
            row_head = along_sub(rows[k], j)
            if j < SUB - 1:
                pivot = along_sub(diag[j + 1], j + 1) - (heads[j + 1] * heads[j + 1]) * scale
            elif k + 1 < count:
                head = along_sub(cols[k + 1][j], 0)
                pivot = along_sub(ahead[0], 0) - (head * head) * scale
            if j < SUB - 1:
                below = jnp.where(sub_ids > j, diag[j], 0.0)
                diag[j + 1] = diag[j + 1] - (below * heads[j + 1]) * scale
                factor = below * scale
                for c in range(j + 2, SUB):
                    diag[c] = diag[c] - factor * heads[c]
                rows[k] = rows[k] - factor * row_head
            for i in range(k + 1, count):
                factor = cols[i][j] * scale
                if i == k + 1:
                    next_heads = [along_sub(cols[i][j], c) for c in range(SUB)]
                    for c in range(SUB):
                        ahead[c] = ahead[c] - factor * next_heads[c]
                if i == k + 2:
                    for c in range(SUB):
                        below_next[c] = below_next[c] - factor * next_heads[c]
                for c in range(j + 1, SUB):
                    cols[i][c] = cols[i][c] - factor * heads[c]
                rows[i] = rows[i] - factor * row_head
        kept = jnp.where(lane_ids < SUB * k + SUB, rows[k], 0.0)
        done.append(kept * lax.rsqrt(pivots))
        diag = ahead
        for task in tasks[: -(-len(tasks) // (count - k))]:
            task()
        tasks = tasks[-(-len(tasks) // (count - k)) :]
    return jnp.concatenate(done, axis=0)


def place():
    return [lax.axis_index(axis) for axis in ("gx", "ay", "ac")]


def third_sketch_kernel(
    gx, ay, field_in, plane_in, second_in, mixing_in, kept, given, *scratch
):
    field, plane_sketch, second_sketch, mixing, blocks, arrived = scratch
    copies = [
        pltpu.make_async_copy(source, target, arrived.at[n])
        for n, (source, target) in enumerate(
            (
                (plane_in, plane_sketch),
                (second_in, second_sketch),
                (mixing_in.at[1], mixing),
                (field_in, field),
            )
        )
    ]
    for copy in copies:
        copy.start()
    for copy in copies[:3]:
        copy.wait()
    planes, rows, cells = field.shape
    scaled = [second_sketch[...] * plane_sketch[p, 1:2, :] for p in range(planes)]
    weights = mm(jnp.concatenate(scaled, axis=0), mixing[...])
    copies[3].wait()
    wide = jnp.transpose(mm_tn(weights, field[...].reshape(planes * rows, cells)))
    own = blocks.shape[2]
    for n in range(2 * gx * ay):
        blocks[n // (gx * ay), n % (gx * ay)] = wide[n * own : n * own + own, :]
    core = place()[2]
    blank = jnp.zeros((gx * ay, kept.shape[1] - own, kept.shape[2]), jnp.float32)
    for half, out in ((core, kept), (1 - core, given)):
        out[:, 0:own, :] = blocks[half]
        out[:, own:, :] = blank


def second_sketch_kernel(own, field, plane_sketch, third_sketch, mixing, out):
    planes, rows, cells = field.shape
    across = None
    for p in range(planes):
        term = mm(field[p], third_sketch[...] * plane_sketch[p, 0:1, :])
        across = term if across is None else across + term
    second = mm(across, mixing[0])
    strip = out.shape[1] - own
    for n in range(out.shape[0]):
        out[n, 0:own, :] = jnp.zeros((own, out.shape[2]), jnp.float32)
        out[n, own:, :] = second[n * strip : n * strip + strip, :]


def spread(block, out, sent):
    copies = [pltpu.make_async_copy(block, out.at[n], sent.at[n]) for n in range(out.shape[0])]
    for copy in copies:
        copy.start()
    for copy in copies:
        copy.wait()


def total_kernel(gx, ay, own, received, out, block, sent):
    strip = received.shape[1] - own
    third = received[0, 0:own, :]
    for n in range(1, gx * ay):
        third = third + received[n, 0:own, :]
    seconds = []
    for y in range(ay):
        second = received[y, own:, :]
        for g in range(1, gx):
            second = second + received[g * ay + y, own:, :]
        seconds.append(second)
    block[0:own, :] = third
    for y in range(ay):
        block[own + y * strip : own + (y + 1) * strip, :] = seconds[y]
    spread(block, out, sent)


def core_ranges(gx, ay, own, ranges):
    strip = (ranges.shape[1] - own) // ay
    return [
        jnp.concatenate(
            [ranges[n, own + y * strip : own + (y + 1) * strip, :] for n in range(gx * ay)], axis=0
        )
        for y in range(ay)
    ]


def own_first(quarters):
    at = place()
    return jnp.concatenate(
        [
            jnp.where(at[1] == 0, quarters[0], quarters[1]),
            jnp.where(at[1] == 0, quarters[1], quarters[0]),
        ],
        axis=0,
    )


def same_core_kernel(gx, ay, own, ranges, near_field, far_field, product, gram):
    quarters = core_ranges(gx, ay, own, ranges)
    both = jnp.concatenate(quarters, axis=0)
    gram[...] = mm_tn(both, both)
    turned = jnp.transpose(own_first(quarters))
    cells = near_field.shape[2]
    for p in range(near_field.shape[0]):
        field = jnp.concatenate([near_field[p], far_field[p]], axis=0)
        product[:, p * cells : p * cells + cells] = mm(turned, field)


def second_kernel(
    gx, ay, ac, same, other, near_field, far_field, product, same_gram, inverse_out, partial, *scratch
):
    third, block, sent = scratch
    at = place()
    planes, rows, cells = near_field.shape
    own = cells // (gx * ay * ac)
    rank = same.shape[2]
    quarters = core_ranges(gx, ay, own, other)
    both = jnp.concatenate(quarters, axis=0)
    gram = same_gram[...] + mm_tn(both, both)
    for swapped, ranges in enumerate((same, other)):
        for n in range(gx * ay):
            third[(at[2] ^ swapped) * (gx * ay) + n] = ranges[n, 0:own, :]
    all_third = jnp.concatenate([third[n] for n in range(gx * ay * ac)], axis=0)
    turned = jnp.transpose(own_first(quarters))
    halves = [[None, None] for _ in range(planes)]
    raw = [None] * planes
    width = cells // 2

    def field_product(p, h):
        span = slice(h * width, h * width + width)
        field = jnp.concatenate([near_field[p, :, span], far_field[p, :, span]], axis=0)
        held = product[:, p * cells + h * width : p * cells + h * width + width]
        halves[p][h] = held + mm(turned, field)

    def range_product(p):
        raw[p] = mm(jnp.concatenate(halves[p], axis=1), all_third)

    tasks = [functools.partial(field_product, p, h) for p in range(planes) for h in range(2)]
    tasks += [functools.partial(range_product, p) for p in range(planes)]
    inverse = inverse_lower(gram, tasks)
    inverse_out[...] = inverse
    share = rank // (ay * ac)
    own_rows = inverse[0:share, :]
    for a in range(1, ay * ac):
        piece = inverse[a * share : a * share + share, :]
        own_rows = jnp.where(at[1] * ac + at[2] == a, piece, own_rows)
    value = mm(own_rows, jnp.concatenate(raw, axis=1))
    for p in range(planes):
        block[p] = value[:, p * rank : p * rank + rank]
    spread(block, partial, sent)


def third_kernel(
    gx, ay, ac, own, targets, signs, same, other, second_inverse, *refs
):
    factor_second, factor_third, turned, weights, third = refs
    at = place()
    rank = same.shape[2]
    mine = core_ranges(gx, ay, own, same)
    mine = jnp.where(at[1] == 0, mine[0], mine[1]).reshape(gx, own, rank)
    own_range = mine[0]
    for g in range(1, gx):
        own_range = jnp.where(at[0] == g, mine[g], own_range)
    factor_second[...] = mm_nt(own_range, second_inverse[...])
    for swapped, ranges in enumerate((same, other)):
        for n in range(gx * ay):
            third[(at[2] ^ swapped) * (gx * ay) + n] = ranges[n, 0:own, :]
    all_third = jnp.concatenate([third[n] for n in range(gx * ay * ac)], axis=0)
    inverse = inverse_lower(mm_tn(all_third, all_third))
    turned[...] = jnp.transpose(inverse)
    factor_third[...] = mm_nt(third[(at[0] * ay + at[1]) * ac + at[2]], inverse)
    out_rows, turns, rank = weights.shape
    for r in range(out_rows):
        row = at[0] * out_rows + r
        for m in range(turns):
            plane = m * BLOCK + lax.rem(row, BLOCK)
            weight = jnp.float32(0)
            for t in range(targets.shape[1]):
                sign = (2 * signs[plane, t] - 1).astype(jnp.float32)
                weight = weight + jnp.where(targets[plane, t] == lax.div(row, BLOCK), sign, 0.0)
            weights[r, m : m + 1, :] = jnp.full((1, rank), weight, jnp.float32)


def core_kernel(weights, turned, planes, out):
    out_rows, turns, rank = weights.shape
    share = planes.shape[1]
    first = place()[0] * out_rows
    rows = []
    for r in range(out_rows):
        slot = r % BLOCK if out_rows % BLOCK == 0 else lax.rem(first + r, BLOCK)
        terms = [weights[r, m : m + 1, :] * planes[m * BLOCK + slot] for m in range(turns)]
        rows.append(sum(terms[1:], terms[0]))
    whole = mm(jnp.concatenate(rows, axis=0), turned[...])
    for r in range(out_rows):
        out[r] = whole[r * share : r * share + share, :]


def call(kernel, out_shapes, in_specs, flops, scratch=(), mib=48, out_specs=None):
    return pl.pallas_call(
        kernel,
        out_shape=out_shapes,
        in_specs=in_specs,
        out_specs=out_specs or jax.tree.map(lambda _: VMEM, out_shapes),
        scratch_shapes=scratch,
        compiler_params=pltpu.CompilerParams(vmem_limit_bytes=int(mib * 2**20)),
        cost_estimate=pl.CostEstimate(flops=flops, bytes_accessed=2**20, transcendentals=0),
    )


def in_hbm(source):
    return pltpu.with_memory_space_constraint(source, pltpu.HBM)


def swap(block, axis):
    perm = [(n, n ^ 1) for n in range(lax.axis_size(axis))]
    return lax.ppermute(block, axis, perm)


def body(
    scalar_field, plane_sketch, second_sketch, third_sketch, mixing, plane_targets, plane_signs
):
    gx, ay, ac = lax.axis_size("gx"), lax.axis_size("ay"), lax.axis_size("ac")
    planes, rows, cells = scalar_field.shape
    rank = mixing.shape[2]
    own = cells // (gx * ay * ac)
    strip = rows // (gx * ay)
    share = rank // (ay * ac)
    f32 = functools.partial(jax.ShapeDtypeStruct, dtype=jnp.float32)

    slot = f32((gx * ay, own + strip, rank))
    kept, given = call(
        functools.partial(third_sketch_kernel, gx, ay),
        [slot, slot],
        [HBM] * 4,
        10**9,
        [
            pltpu.VMEM(scalar_field.shape, jnp.float32),
            pltpu.VMEM(plane_sketch.shape, jnp.float32),
            pltpu.VMEM(second_sketch.shape, jnp.float32),
            pltpu.VMEM(mixing.shape[1:], jnp.float32),
            pltpu.VMEM((ac, gx * ay, own, rank), jnp.float32),
            pltpu.SemaphoreType.DMA((4,)),
        ],
    )(*(in_hbm(source) for source in (scalar_field, plane_sketch, second_sketch, mixing)))
    taken = swap(given, "ac")
    second = call(functools.partial(second_sketch_kernel, own), slot, [VMEM] * 4, 10**9)(
        scalar_field, plane_sketch, third_sketch, mixing
    )
    slots = kept + second + taken
    received = lax.all_to_all(slots, ("gx", "ay"), 0, 0, tiled=True)
    copies = call(
        functools.partial(total_kernel, gx, ay, own),
        f32((gx * ay, own + ay * strip, rank)),
        [VMEM],
        10**6,
        [
            pltpu.VMEM((own + ay * strip, rank), jnp.float32),
            pltpu.SemaphoreType.DMA((gx * ay,)),
        ],
        out_specs=HBM,
    )(received)
    same = lax.all_to_all(copies, ("gx", "ay"), 0, 0, tiled=True)
    other = swap(same, "ac")
    across = swap(scalar_field, "ay")
    product, same_gram = call(
        functools.partial(same_core_kernel, gx, ay, own),
        [f32((rank, planes * cells)), f32((rank, rank))],
        [VMEM] * 3,
        10**9,
    )(same, scalar_field, across)
    second_inverse, partial = call(
        functools.partial(second_kernel, gx, ay, ac),
        [f32((rank, rank)), f32((gx, planes, share, rank))],
        [VMEM] * 6,
        2 * 10**9,
        [
            pltpu.VMEM((gx * ay * ac, own, rank), jnp.float32),
            pltpu.VMEM((planes, share, rank), jnp.float32),
            pltpu.SemaphoreType.DMA((gx,)),
        ],
        out_specs=[VMEM, HBM],
    )(same, other, swap(scalar_field, "ac"), swap(across, "ac"), product, same_gram)
    every = lax.all_to_all(partial, "gx", 0, 0, tiled=True)
    out_rows = BLOCKS * BLOCK // gx
    factor_second, factor_third, turned, weights = call(
        functools.partial(third_kernel, gx, ay, ac, own),
        [
            f32((own, rank)),
            f32((own, rank)),
            f32((rank, rank)),
            f32((out_rows, gx * planes // BLOCK, rank)),
        ],
        [SMEM] * 2 + [VMEM] * 3,
        10**9,
        [pltpu.VMEM((gx * ay * ac, own, rank), jnp.float32)],
    )(plane_targets, plane_signs, same, other, second_inverse)
    core_sketch = call(core_kernel, f32((out_rows, share, rank)), [VMEM] * 3, 10**8)(
        weights, turned, every.reshape(gx * planes, share, rank)
    )
    return (factor_second, factor_third, core_sketch)


def solution(mesh):
    gx, af = mesh.devices.shape
    mesh = jax.sharding.Mesh(mesh.devices.reshape(gx, af // 2, 2), ("gx", "ay", "ac"))
    af = ("ay", "ac")
    in_specs = (P("gx", af, None), P("gx", None, None), P(af, None), P(), P(), P(), P())
    out_specs = (P(af + ("gx",), None), P(("gx",) + af, None), P("gx", af, None))
    return jax.shard_map(body, mesh=mesh, in_specs=in_specs, out_specs=out_specs, check_vma=False)
```

```python
import functools

import jax
import jax.numpy as jnp
from jax import lax
from jax.experimental import pallas as pl
from jax.experimental.pallas import tpu as pltpu
from jax.sharding import PartitionSpec as P

BLOCK = 16
BLOCKS = 8
SUB = 8

precise = lax.Precision.HIGHEST
VMEM = pl.BlockSpec(memory_space=pltpu.VMEM)
SMEM = pl.BlockSpec(memory_space=pltpu.SMEM)
HBM = pl.BlockSpec(memory_space=pltpu.HBM)


def dot(left, right, dims):
    return lax.dot_general(
        left, right, (dims, ((), ())), precision=precise, preferred_element_type=jnp.float32
    )


def mm(left, right):
    return dot(left, right, ((1,), (0,)))


def mm_tn(left, right):
    return dot(left, right, ((0,), (0,)))


def mm_nt(left, right):
    return dot(left, right, ((1,), (1,)))


def inverse_lower(gram, tasks=()):
    size = gram.shape[0]
    count = size // SUB
    tasks = list(tasks)
    sub_ids = lax.broadcasted_iota(jnp.int32, (SUB, size), 0)
    lane_ids = lax.broadcasted_iota(jnp.int32, (SUB, size), 1)
    rows = [gram[SUB * i : SUB * i + SUB, :] for i in range(count)]
    done = []

    def along_sub(tile, j):
        return jnp.broadcast_to(tile[j : j + 1, :], (SUB, size))

    def along_lanes(tile, block):
        return [
            jnp.broadcast_to(tile[:, SUB * block + c : SUB * block + c + 1], (SUB, size))
            for c in range(SUB)
        ]

    diag = along_lanes(rows[0], 0)
    pivot = along_sub(diag[0], 0)
    for k in range(count):
        inside = (lane_ids >= SUB * k) & (lane_ids < SUB * k + SUB)
        cols = {i: along_lanes(rows[i], k) for i in range(k + 2, count)}
        if k + 1 < count:
            cols[k + 1] = along_lanes(rows[1], 0) if k == 0 else below_next
        below_next = along_lanes(rows[k + 2], k + 1) if k + 2 < count else None
        ahead = along_lanes(rows[k + 1], k + 1) if k + 1 < count else None
        identity = jnp.where(lane_ids == sub_ids + SUB * k, 1.0, 0.0)
        rows[k] = jnp.where(inside, identity, rows[k])
        for i in range(k + 1, count):
            rows[i] = jnp.where(inside, 0.0, rows[i])
        pivots = None
        for j in range(SUB):
            pivots = pivot if j == 0 else jnp.where(sub_ids == j, pivot, pivots)
            scale = 1.0 / pivot
            heads = {c: along_sub(diag[c], j) for c in range(j + 1, SUB)}
            row_head = along_sub(rows[k], j)
            if j < SUB - 1:
                pivot = along_sub(diag[j + 1], j + 1) - (heads[j + 1] * heads[j + 1]) * scale
            elif k + 1 < count:
                head = along_sub(cols[k + 1][j], 0)
                pivot = along_sub(ahead[0], 0) - (head * head) * scale
            if j < SUB - 1:
                below = jnp.where(sub_ids > j, diag[j], 0.0)
                diag[j + 1] = diag[j + 1] - (below * heads[j + 1]) * scale
                factor = below * scale
                for c in range(j + 2, SUB):
                    diag[c] = diag[c] - factor * heads[c]
                rows[k] = rows[k] - factor * row_head
            for i in range(k + 1, count):
                factor = cols[i][j] * scale
                if i == k + 1:
                    next_heads = [along_sub(cols[i][j], c) for c in range(SUB)]
                    for c in range(SUB):
                        ahead[c] = ahead[c] - factor * next_heads[c]
                if i == k + 2:
                    for c in range(SUB):
                        below_next[c] = below_next[c] - factor * next_heads[c]
                for c in range(j + 1, SUB):
                    cols[i][c] = cols[i][c] - factor * heads[c]
                rows[i] = rows[i] - factor * row_head
        kept = jnp.where(lane_ids < SUB * k + SUB, rows[k], 0.0)
        done.append(kept * lax.rsqrt(pivots))
        diag = ahead
        for task in tasks[: -(-len(tasks) // (count - k))]:
            task()
        tasks = tasks[-(-len(tasks) // (count - k)) :]
    return jnp.concatenate(done, axis=0)


def place():
    return [lax.axis_index(axis) for axis in ("gx", "ay", "ac")]


def third_sketch_kernel(
    gx, ay, field_in, plane_in, second_in, mixing_in, kept, given, *scratch
):
    field, plane_sketch, second_sketch, mixing, blocks, arrived = scratch
    copies = [
        pltpu.make_async_copy(source, target, arrived.at[n])
        for n, (source, target) in enumerate(
            (
                (plane_in, plane_sketch),
                (second_in, second_sketch),
                (mixing_in.at[1], mixing),
                (field_in, field),
            )
        )
    ]
    for copy in copies[::-1]:
        copy.start()
    for copy in copies[:3]:
        copy.wait()
    planes, rows, cells = field.shape
    scaled = [second_sketch[...] * plane_sketch[p, 1:2, :] for p in range(planes)]
    weights = mm(jnp.concatenate(scaled, axis=0), mixing[...])
    copies[3].wait()
    wide = jnp.transpose(mm_tn(weights, field[...].reshape(planes * rows, cells)))
    own = blocks.shape[2]
    for n in range(2 * gx * ay):
        blocks[n // (gx * ay), n % (gx * ay)] = wide[n * own : n * own + own, :]
    core = place()[2]
    blank = jnp.zeros((gx * ay, kept.shape[1] - own, kept.shape[2]), jnp.float32)
    for half, out in ((core, kept), (1 - core, given)):
        out[:, 0:own, :] = blocks[half]
        out[:, own:, :] = blank


def second_sketch_kernel(own, field, plane_sketch, third_sketch, mixing, out):
    planes, rows, cells = field.shape
    scaled = [third_sketch[...] * plane_sketch[p, 0:1, :] for p in range(planes)]
    wide = jnp.concatenate([field[p] for p in range(planes)], axis=1)
    across = mm(wide, jnp.concatenate(scaled, axis=0))
    second = mm(across, mixing[0])
    strip = out.shape[1] - own
    for n in range(out.shape[0]):
        out[n, 0:own, :] = jnp.zeros((own, out.shape[2]), jnp.float32)
        out[n, own:, :] = second[n * strip : n * strip + strip, :]


def spread(block, out, sent):
    copies = [pltpu.make_async_copy(block, out.at[n], sent.at[n]) for n in range(out.shape[0])]
    for copy in copies:
        copy.start()
    for copy in copies:
        copy.wait()


def total_kernel(gx, ay, own, received, out):
    strip = received.shape[1] - own
    third = received[0, 0:own, :]
    for n in range(1, gx * ay):
        third = third + received[n, 0:own, :]
    seconds = []
    for y in range(ay):
        second = received[y, own:, :]
        for g in range(1, gx):
            second = second + received[g * ay + y, own:, :]
        seconds.append(second)
    for n in range(gx * ay):
        out[n, 0:own, :] = third
        for y in range(ay):
            out[n, own + y * strip : own + (y + 1) * strip, :] = seconds[y]


def core_ranges(gx, ay, own, ranges):
    strip = (ranges.shape[1] - own) // ay
    return [
        jnp.concatenate(
            [ranges[n, own + y * strip : own + (y + 1) * strip, :] for n in range(gx * ay)], axis=0
        )
        for y in range(ay)
    ]


def own_first(quarters):
    at = place()
    return jnp.concatenate(
        [
            jnp.where(at[1] == 0, quarters[0], quarters[1]),
            jnp.where(at[1] == 0, quarters[1], quarters[0]),
        ],
        axis=0,
    )


def same_core_kernel(gx, ay, own, ranges, near_field, far_field, product, gram):
    quarters = core_ranges(gx, ay, own, ranges)
    both = jnp.concatenate(quarters, axis=0)
    gram[...] = mm_tn(both, both)
    turned = jnp.transpose(own_first(quarters))
    cells = near_field.shape[2]
    for p in range(near_field.shape[0]):
        field = jnp.concatenate([near_field[p], far_field[p]], axis=0)
        product[:, p * cells : p * cells + cells] = mm(turned, field)


def second_kernel(
    gx, ay, ac, same, other, near_field, far_field, product, same_gram, inverse_out, partial, *scratch
):
    third, block, sent = scratch
    at = place()
    planes, rows, cells = near_field.shape
    own = cells // (gx * ay * ac)
    rank = same.shape[2]
    quarters = core_ranges(gx, ay, own, other)
    both = jnp.concatenate(quarters, axis=0)
    gram = same_gram[...] + mm_tn(both, both)
    for swapped, ranges in enumerate((same, other)):
        for n in range(gx * ay):
            third[(at[2] ^ swapped) * (gx * ay) + n] = ranges[n, 0:own, :]
    all_third = jnp.concatenate([third[n] for n in range(gx * ay * ac)], axis=0)
    turned = jnp.transpose(own_first(quarters))
    halves = [[None, None] for _ in range(planes)]
    raw = [None] * planes
    width = cells // 2

    def field_product(p, h):
        span = slice(h * width, h * width + width)
        field = jnp.concatenate([near_field[p, :, span], far_field[p, :, span]], axis=0)
        held = product[:, p * cells + h * width : p * cells + h * width + width]
        halves[p][h] = held + mm(turned, field)

    def range_product(p):
        raw[p] = mm(jnp.concatenate(halves[p], axis=1), all_third)

    tasks = [functools.partial(field_product, p, h) for p in range(planes) for h in range(2)]
    tasks += [functools.partial(range_product, p) for p in range(planes)]
    inverse = inverse_lower(gram, tasks)
    inverse_out[...] = inverse
    share = rank // (ay * ac)
    own_rows = inverse[0:share, :]
    for a in range(1, ay * ac):
        piece = inverse[a * share : a * share + share, :]
        own_rows = jnp.where(at[1] * ac + at[2] == a, piece, own_rows)
    value = mm(own_rows, jnp.concatenate(raw, axis=1))
    for p in range(planes):
        block[p] = value[:, p * rank : p * rank + rank]
    spread(block, partial, sent)


def third_kernel(
    gx, ay, ac, own, targets, signs, same, other, second_inverse, *refs
):
    factor_second, factor_third, turned, weights, third = refs
    at = place()
    rank = same.shape[2]
    mine = core_ranges(gx, ay, own, same)
    mine = jnp.where(at[1] == 0, mine[0], mine[1]).reshape(gx, own, rank)
    own_range = mine[0]
    for g in range(1, gx):
        own_range = jnp.where(at[0] == g, mine[g], own_range)
    factor_second[...] = mm_nt(own_range, second_inverse[...])
    for swapped, ranges in enumerate((same, other)):
        for n in range(gx * ay):
            third[(at[2] ^ swapped) * (gx * ay) + n] = ranges[n, 0:own, :]
    all_third = jnp.concatenate([third[n] for n in range(gx * ay * ac)], axis=0)
    inverse = inverse_lower(mm_tn(all_third, all_third))
    turned[...] = jnp.transpose(inverse)
    factor_third[...] = mm_nt(third[(at[0] * ay + at[1]) * ac + at[2]], inverse)
    out_rows, turns, rank = weights.shape
    for r in range(out_rows):
        row = at[0] * out_rows + r
        for m in range(turns):
            plane = m * BLOCK + lax.rem(row, BLOCK)
            weight = jnp.float32(0)
            for t in range(targets.shape[1]):
                sign = (2 * signs[plane, t] - 1).astype(jnp.float32)
                weight = weight + jnp.where(targets[plane, t] == lax.div(row, BLOCK), sign, 0.0)
            weights[r, m : m + 1, :] = jnp.full((1, rank), weight, jnp.float32)


def core_kernel(weights, turned, planes, out):
    out_rows, turns, rank = weights.shape
    share = planes.shape[1]
    first = place()[0] * out_rows
    rows = []
    for r in range(out_rows):
        slot = r % BLOCK if out_rows % BLOCK == 0 else lax.rem(first + r, BLOCK)
        terms = [weights[r, m : m + 1, :] * planes[m * BLOCK + slot] for m in range(turns)]
        rows.append(sum(terms[1:], terms[0]))
    whole = mm(jnp.concatenate(rows, axis=0), turned[...])
    for r in range(out_rows):
        out[r] = whole[r * share : r * share + share, :]


def call(kernel, out_shapes, in_specs, flops, scratch=(), mib=48, out_specs=None):
    return pl.pallas_call(
        kernel,
        out_shape=out_shapes,
        in_specs=in_specs,
        out_specs=out_specs or jax.tree.map(lambda _: VMEM, out_shapes),
        scratch_shapes=scratch,
        compiler_params=pltpu.CompilerParams(vmem_limit_bytes=int(mib * 2**20)),
        cost_estimate=pl.CostEstimate(flops=flops, bytes_accessed=2**20, transcendentals=0),
    )


def in_hbm(source):
    return pltpu.with_memory_space_constraint(source, pltpu.HBM)


def swap(block, axis):
    perm = [(n, n ^ 1) for n in range(lax.axis_size(axis))]
    return lax.ppermute(block, axis, perm)


def body(
    scalar_field, plane_sketch, second_sketch, third_sketch, mixing, plane_targets, plane_signs
):
    gx, ay, ac = lax.axis_size("gx"), lax.axis_size("ay"), lax.axis_size("ac")
    planes, rows, cells = scalar_field.shape
    rank = mixing.shape[2]
    own = cells // (gx * ay * ac)
    strip = rows // (gx * ay)
    share = rank // (ay * ac)
    f32 = functools.partial(jax.ShapeDtypeStruct, dtype=jnp.float32)

    slot = f32((gx * ay, own + strip, rank))
    kept, given = call(
        functools.partial(third_sketch_kernel, gx, ay),
        [slot, slot],
        [HBM] * 4,
        10**9,
        [
            pltpu.VMEM(scalar_field.shape, jnp.float32),
            pltpu.VMEM(plane_sketch.shape, jnp.float32),
            pltpu.VMEM(second_sketch.shape, jnp.float32),
            pltpu.VMEM(mixing.shape[1:], jnp.float32),
            pltpu.VMEM((ac, gx * ay, own, rank), jnp.float32),
            pltpu.SemaphoreType.DMA((4,)),
        ],
    )(*(in_hbm(source) for source in (scalar_field, plane_sketch, second_sketch, mixing)))
    taken = swap(given, "ac")
    second = call(functools.partial(second_sketch_kernel, own), slot, [VMEM] * 4, 10**9)(
        scalar_field, plane_sketch, third_sketch, mixing
    )
    slots = kept + second + taken
    received = lax.all_to_all(slots, ("gx", "ay"), 0, 0, tiled=True)
    copies = call(
        functools.partial(total_kernel, gx, ay, own),
        f32((gx * ay, own + ay * strip, rank)),
        [VMEM],
        10**6,
    )(received)
    same = lax.all_to_all(copies, ("gx", "ay"), 0, 0, tiled=True)
    other = swap(same, "ac")
    across = swap(scalar_field, "ay")
    product, same_gram = call(
        functools.partial(same_core_kernel, gx, ay, own),
        [f32((rank, planes * cells)), f32((rank, rank))],
        [VMEM] * 3,
        10**9,
    )(same, scalar_field, across)
    second_inverse, partial = call(
        functools.partial(second_kernel, gx, ay, ac),
        [f32((rank, rank)), f32((gx, planes, share, rank))],
        [VMEM] * 6,
        2 * 10**9,
        [
            pltpu.VMEM((gx * ay * ac, own, rank), jnp.float32),
            pltpu.VMEM((planes, share, rank), jnp.float32),
            pltpu.SemaphoreType.DMA((gx,)),
        ],
        out_specs=[VMEM, HBM],
    )(same, other, swap(scalar_field, "ac"), swap(across, "ac"), product, same_gram)
    every = lax.all_to_all(partial, "gx", 0, 0, tiled=True)
    out_rows = BLOCKS * BLOCK // gx
    factor_second, factor_third, turned, weights = call(
        functools.partial(third_kernel, gx, ay, ac, own),
        [
            f32((own, rank)),
            f32((own, rank)),
            f32((rank, rank)),
            f32((out_rows, gx * planes // BLOCK, rank)),
        ],
        [SMEM] * 2 + [VMEM] * 3,
        10**9,
        [pltpu.VMEM((gx * ay * ac, own, rank), jnp.float32)],
    )(plane_targets, plane_signs, same, other, second_inverse)
    core_sketch = call(core_kernel, f32((out_rows, share, rank)), [VMEM] * 3, 10**8)(
        weights, turned, every.reshape(gx * planes, share, rank)
    )
    return (factor_second, factor_third, core_sketch)


def solution(mesh):
    gx, af = mesh.devices.shape
    mesh = jax.sharding.Mesh(mesh.devices.reshape(gx, af // 2, 2), ("gx", "ay", "ac"))
    af = ("ay", "ac")
    in_specs = (P("gx", af, None), P("gx", None, None), P(af, None), P(), P(), P(), P())
    out_specs = (P(af + ("gx",), None), P(("gx",) + af, None), P("gx", af, None))
    return jax.shard_map(body, mesh=mesh, in_specs=in_specs, out_specs=out_specs, check_vma=False)
```
